512 devices in a mesh: dom: 32 (over x, y), strip: 16 (over z, core).
Axes of the slice: x: 4, y: 8, z: 8, core: 2. Of those that a mesh axis runs over, the one named last changes fastest.
Arguments:
- surface: bfloat16 [768, 512, 256], P('dom', 'strip'), may hold values from 0.5 to 2
- discharge: bfloat16 [768, 512, 256], P('dom', 'strip'), may hold values from -3 to 3
- storage: bfloat16 [768, 512, 256], P('dom', 'strip'), may hold values from 0 to 1.5
- exchange: bfloat16 [512, 256], P('strip'), may hold values from 0.049804688 to 0.29882812
- depth_perturbation: bfloat16 [2, 768, 512, 256], P(None, 'dom', 'strip'), may hold values from -1.1953125 to 1.1953125
- flow_perturbation: bfloat16 [2, 768, 512, 256], P(None, 'dom', 'strip'), may hold values from -1.1953125 to 1.1953125
- sensor_cell: int32 [512], P('strip'), may hold values from 0 to 131071, as said below
- sensor_radius: int32 [512], P('strip'), may hold values from 8 to 32
- observed: float32 [512], P('strip'), may hold values from -1 to 33
- sensor_sigma: float32 [512], P('strip'), may hold values from 0.3 to 1.5
Outputs:
- posterior_depth: float32 [512, 256], P('strip')
- posterior_flow: float32 [512, 256], P('strip')
- posterior_storage: float32 [512, 256], P('strip')
The draws below stay inside these ranges and needn't reach their ends.
Inputs may be any that keep to these rules, and one draw needn't show every extreme that they name: `sensor_cell`: sensor k lies in strip k // 32, that is in rows (k // 32) * 32 to (k // 32 + 1) * 32 - 1.
All inputs are finite; a program needn't handle non-finite values.
Results may differ from the reference program's by a relative error of at most 0.0003.
Values may be sent and summed in bfloat16 or wider, within the bound.
No kernel may reach another device: no remote copies, remote signals or barrier semaphores. Data moves between devices by JAX's collectives and lax.ppermute only.
A program may use at most 64 MiB of HBM per device.

```python
import math
import jax
import jax.numpy as jnp
from jax import lax

P_DEV = 24
ROWS_DEV = 32
COLS = 256
SENS_DEV = 32
STEPS = 2
PARTICLES = 768
NROWS = 512
SENSORS = 512
N_DOM = 32
N_STRIP = 16


def draw_sensor_cell(key, part):
    owner = jnp.arange(SENSORS, dtype=jnp.int32) // SENS_DEV
    offset = jax.random.randint(key, (SENSORS,), 0, ROWS_DEV * COLS, dtype=jnp.int32)
    return owner * (ROWS_DEV * COLS) + offset


def draw_observed(key, part):
    level = 1.2 + 0.6 * jax.random.normal(key, (SENSORS,), jnp.float32)
    return jnp.clip(level, -1.0, 3.4)


def with_ends(values, own_key, least, top_value):
    shape = values.shape
    place = [jax.random.randint(jax.random.fold_in(own_key, axis), (), 0, shape[axis]) for axis in range(len(shape))]
    values = values.at[tuple(place)].set(least)
    longest = shape.index(max(shape))
    place[longest] = (place[longest] + 1) % shape[longest]
    return values.at[tuple(place)].set(top_value)


def levels(rng, extent, split, least, top_value):
    gain, own = 1.0, jax.random.fold_in(rng, 6)
    for position, shards_of in split:
        heights = jnp.exp(jax.random.uniform(jax.random.fold_in(own, position), (shards_of,), jnp.float32, least / len(split), top_value / len(split)))
        gain = gain * jnp.repeat(heights, extent[position] // shards_of).reshape([-1 if axis == position else 1 for axis in range(len(extent))])
    return gain


def noise(stream_key, shape, spread, limit, cuts=(), held_as=jnp.bfloat16):
    entries = jax.random.normal(stream_key, shape, jnp.float32) * spread
    if len(cuts) > 0:
        entries = levels(stream_key, shape, cuts, -0.22, 0.18) * entries
    return jnp.clip(entries, min=-limit, max=limit).astype(held_as)


def setup_inputs(seed: int = 0) -> dict:
    splits = jax.random.split(jax.random.key(seed), 11)
    return {
        "surface": jnp.clip(0.5 + 1.5 * jax.random.uniform(splits[0], (PARTICLES, NROWS, COLS), jnp.float32) ** levels(splits[0], (PARTICLES, NROWS, COLS), ((0, 32), (1, 16)), -0.2, 0.2), 0.5, 2.0).astype(jnp.bfloat16),
        "discharge": noise(splits[1], (PARTICLES, NROWS, COLS), 0.5, 3.0, ((0, 32), (1, 16))),
        "storage": jnp.clip(1.5 * jax.random.uniform(splits[2], (PARTICLES, NROWS, COLS), jnp.float32) ** levels(splits[2], (PARTICLES, NROWS, COLS), ((0, 32), (1, 16)), -0.2, 0.2), 0.0, 1.5).astype(jnp.bfloat16),
        "exchange": jnp.clip(jnp.exp(math.log(0.29882812) - 1.7917595 * jax.random.uniform(splits[3], (NROWS, COLS), jnp.float32) ** levels(splits[3], (NROWS, COLS), ((0, 16),), -0.2, 0.2)), 0.049804688, 0.29882812).astype(jnp.bfloat16),
        "depth_perturbation": noise(splits[4], (STEPS, PARTICLES, NROWS, COLS), 0.2, 1.1953125, ((1, 32), (2, 16))),
        "flow_perturbation": noise(splits[5], (STEPS, PARTICLES, NROWS, COLS), 0.2, 1.1953125, ((1, 32), (2, 16))),
        "sensor_cell": draw_sensor_cell(jax.random.fold_in(splits[10], 71), 0),
        "sensor_radius": with_ends(jax.random.randint(splits[7], (SENSORS,), max(ROWS_DEV // 4, 1), ROWS_DEV + 1), jax.random.fold_in(splits[7], 1), max(ROWS_DEV // 4, 1), ROWS_DEV).astype(jnp.int32),
        "observed": draw_observed(jax.random.fold_in(splits[10], 71), 0),
        "sensor_sigma": jnp.clip(jnp.exp(math.log(1.5) - 1.60943787 * jax.random.uniform(splits[9], (SENSORS,), jnp.float32) ** levels(splits[9], (SENSORS,), ((0, 16),), -0.2, 0.2)), 0.3, 1.5),
    }


advection = 0.4
gravity = 0.5
diffusion = 0.15
friction = 0.3
drainage = 0.1


def column_spread(field):
    left_side = jnp.concatenate([field[..., :1], field[..., :-1]], axis=-1)
    right_side = jnp.concatenate([field[..., 1:], field[..., -1:]], axis=-1)
    return left_side - 2.0 * field + right_side


def advance_depth(current_depth, current_flow, flow_below, current_storage, exchange, jitter):
    inflow = exchange * (current_depth - current_storage)
    depth_next = current_depth - advection * (current_flow - flow_below) + diffusion * column_spread(current_depth) - inflow + jitter
    stored_next = (1.0 - drainage) * current_storage + inflow
    return depth_next, stored_next


def advance_flow(current_flow, current_depth, depth_above, jitter):
    return (current_flow - gravity * (depth_above - current_depth) + jitter) / (1.0 + friction * jnp.abs(current_flow))


def taper_table(sensor_rows, sensor_cols, sensor_reach, cell_rows, cell_cols):
    row_gap = cell_rows[None, :] - sensor_rows[:, None]
    col_gap = cell_cols[None, :] - sensor_cols[:, None]
    distance = row_gap * row_gap + col_gap * col_gap
    reach = jnp.maximum(sensor_reach * sensor_reach, 1.0)
    return jnp.maximum(1.0 - distance / reach[:, None], 0.0)


def predict_ahead(current_depth, current_flow, current_storage, exchange, depth_perturbation, flow_perturbation):
    for time_step in range(STEPS):
        flow_below = jnp.pad(current_flow, ((0, 0), (1, 0), (0, 0)))[:, :-1]
        current_depth, current_storage = advance_depth(current_depth, current_flow, flow_below, current_storage, exchange, depth_perturbation[time_step])
        depth_above = jnp.pad(current_depth, ((0, 0), (0, 1), (0, 0)))[:, 1:]
        current_flow = advance_flow(current_flow, current_depth, depth_above, flow_perturbation[time_step])
    return current_depth, current_flow, current_storage


def reference(surface, discharge, storage, exchange, depth_perturbation, flow_perturbation, sensor_cell, sensor_radius, observed, sensor_sigma):
    cells_dev = ROWS_DEV * COLS
    sensor_rows = (sensor_cell // COLS).astype(jnp.float32)
    sensor_cols = (sensor_cell % COLS).astype(jnp.float32)
    sensor_reach = sensor_radius.astype(jnp.float32)
    padded_rows = jnp.pad(sensor_rows, (SENS_DEV, SENS_DEV))
    padded_cols = jnp.pad(sensor_cols, (SENS_DEV, SENS_DEV))
    padded_reach = jnp.pad(sensor_reach, (SENS_DEV, SENS_DEV))
    cell_ids = jnp.arange(cells_dev, dtype=jnp.int32)
    local_rows = cell_ids // COLS
    local_cols = (cell_ids % COLS).astype(jnp.float32)
    exchange_rate = exchange.astype(jnp.float32)

    def block_terms(carry, block_index):
        first_member = (block_index * P_DEV).astype(jnp.int32)
        current_depth = lax.dynamic_slice_in_dim(surface, first_member, P_DEV, 0).astype(jnp.float32)
        current_flow = lax.dynamic_slice_in_dim(discharge, first_member, P_DEV, 0).astype(jnp.float32)
        current_storage = lax.dynamic_slice_in_dim(storage, first_member, P_DEV, 0).astype(jnp.float32)
        depth_noise_draws = lax.dynamic_slice_in_dim(depth_perturbation, first_member, P_DEV, 1).astype(jnp.float32)
        flow_noise_draws = lax.dynamic_slice_in_dim(flow_perturbation, first_member, P_DEV, 1).astype(jnp.float32)
        current_depth, current_flow, current_storage = predict_ahead(current_depth, current_flow, current_storage, exchange_rate, depth_noise_draws, flow_noise_draws)
        flat_depth = current_depth.reshape(P_DEV, NROWS * COLS)
        flat_flow = current_flow.reshape(P_DEV, NROWS * COLS)
        flat_stored = current_storage.reshape(P_DEV, NROWS * COLS)
        sampled = jnp.take(flat_depth, sensor_cell, axis=1)
        misfit = (sampled - observed[None, :]) / sensor_sigma[None, :]
        loglik = -0.5 * misfit * misfit
        padded_lik = jnp.pad(loglik, ((0, 0), (SENS_DEV, SENS_DEV)))

        def strip_weights(strip_index):
            offset = (strip_index * SENS_DEV).astype(jnp.int32)
            cell_rows = (local_rows + strip_index * ROWS_DEV).astype(jnp.float32)
            taper_rows = taper_table(
                lax.dynamic_slice_in_dim(padded_rows, offset, 3 * SENS_DEV, 0),
                lax.dynamic_slice_in_dim(padded_cols, offset, 3 * SENS_DEV, 0),
                lax.dynamic_slice_in_dim(padded_reach, offset, 3 * SENS_DEV, 0),
                cell_rows, local_cols)
            nearby = lax.dynamic_slice_in_dim(padded_lik, offset, 3 * SENS_DEV, 1)
            return jnp.dot(nearby, taper_rows, precision=lax.Precision.HIGHEST, preferred_element_type=jnp.float32)

        weights = lax.map(strip_weights, jnp.arange(N_STRIP, dtype=jnp.int32))
        weights = jnp.transpose(weights, (1, 0, 2)).reshape(P_DEV, NROWS * COLS)
        highest = jnp.max(weights, axis=0)
        factor = jnp.exp(weights - highest[None, :])
        sums = (jnp.sum(factor, axis=0), jnp.sum(factor * flat_depth, axis=0),
                jnp.sum(factor * flat_flow, axis=0), jnp.sum(factor * flat_stored, axis=0))
        best_before, totals = carry
        largest = jnp.maximum(best_before, highest)
        keep_old = jnp.exp(best_before - largest)
        keep_new = jnp.exp(highest - largest)
        totals = tuple(old_sum * keep_old + new_sum * keep_new for old_sum, new_sum in zip(totals, sums))
        return (largest, totals), None

    start_best = jnp.full((NROWS * COLS,), -jnp.inf, dtype=jnp.float32)
    zeros_sum = jnp.zeros((NROWS * COLS,), dtype=jnp.float32)
    carry = (start_best, (zeros_sum, zeros_sum, zeros_sum, zeros_sum))
    (largest, totals), unused = lax.scan(block_terms, carry, jnp.arange(N_DOM, dtype=jnp.int32))
    posterior_depth = (totals[1] / totals[0]).reshape(NROWS, COLS)
    posterior_flow = (totals[2] / totals[0]).reshape(NROWS, COLS)
    posterior_storage = (totals[3] / totals[0]).reshape(NROWS, COLS)
    return (posterior_depth, posterior_flow, posterior_storage)
```

```python
import jax
import jax.numpy as jnp
from jax import lax
from jax.experimental import pallas as pl
from jax.experimental.pallas import tpu as pltpu
from jax.sharding import PartitionSpec as P

advection = 0.4
gravity = 0.5
diffusion = 0.15
friction = 0.3
drainage = 0.1

MEMBERS = 24
ROWS = 32
COLS = 256
SENS = 32
LANES = 128
HALO = 3 * MEMBERS
MESSAGE = HALO + SENS

f32 = jnp.float32
bf16 = jnp.bfloat16


def column_spread(field):
    width = field.shape[-1]
    lane = lax.broadcasted_iota(jnp.int32, field.shape, field.ndim - 1)
    left_side = jnp.where(lane == 0, field, pltpu.roll(field, 1, field.ndim - 1))
    right_side = jnp.where(lane == width - 1, field, pltpu.roll(field, width - 1, field.ndim - 1))
    return left_side - 2.0 * field + right_side


def pack_kernel(
    cell_ref, radius_ref, surface_ref, discharge_ref, storage_ref, exchange_ref, depth_noise_ref, flow_noise_ref,
    up_ref, down_ref, first_ref, last_ref,
):
    def keep(scratch, slot, rows):
        flat = rows.reshape(MEMBERS * 8, COLS)
        scratch[slot, 0] = flat[:, :LANES]
        scratch[slot, 1] = flat[:, LANES:]

    def take(ref, lead, slot):
        head = ref[lead + (slice(None), slice(0, 16), slice(None))].astype(f32)
        tail = ref[lead + (slice(None), slice(16, 32), slice(None))].astype(f32)
        keep(first_ref, slot, head[:, :8])
        keep(last_ref, slot, tail[:, 8:])

    take(surface_ref, (), 0)
    take(discharge_ref, (), 1)
    take(storage_ref, (), 2)
    take(depth_noise_ref, (0,), 3)
    take(flow_noise_ref, (0,), 4)
    late = depth_noise_ref[1, :, 0:16, :].astype(f32)
    keep(first_ref, 5, late[:, :8])

    def row_of(ref, slot, row):
        halves = [ref[slot, half, pl.ds(row, MEMBERS, stride=8)] for half in range(2)]
        return jnp.concatenate(halves, axis=1)

    rate = exchange_ref[...].astype(f32)
    surface_0, surface_1 = row_of(first_ref, 0, 0), row_of(first_ref, 0, 1)
    flow_0, flow_1 = row_of(first_ref, 1, 0), row_of(first_ref, 1, 1)
    stored_0, stored_1 = row_of(first_ref, 2, 0), row_of(first_ref, 2, 1)
    noise_0, noise_1 = row_of(first_ref, 3, 0), row_of(first_ref, 3, 1)
    flow_noise_0, late_0 = row_of(first_ref, 4, 0), row_of(first_ref, 5, 0)
    rate_0, rate_1 = rate[0:1], rate[1:2]
    inflow_0 = rate_0 * (surface_0 - stored_0)
    partial_0 = surface_0 - advection * flow_0 + diffusion * column_spread(surface_0) - inflow_0 + noise_0
    stored_next = (1.0 - drainage) * stored_0 + inflow_0
    depth_1 = (
        surface_1 - advection * (flow_1 - flow_0) + diffusion * column_spread(surface_1)
        - rate_1 * (surface_1 - stored_1) + noise_1
    )
    inverse_0 = 1.0 / (1.0 + friction * jnp.abs(flow_0))
    flow_part = (flow_0 - gravity * depth_1 + flow_noise_0) * inverse_0
    up_ref[0:MEMBERS] = partial_0
    up_ref[MEMBERS : 2 * MEMBERS] = 1.0 - rate_0 - (advection * gravity) * inverse_0
    up_ref[2 * MEMBERS : HALO] = rate_0 * stored_next + late_0 - advection * flow_part
    surface_31, flow_30, flow_31 = row_of(last_ref, 0, 7), row_of(last_ref, 1, 6), row_of(last_ref, 1, 7)
    stored_31, noise_31, flow_noise_31 = row_of(last_ref, 2, 7), row_of(last_ref, 3, 7), row_of(last_ref, 4, 7)
    rate_31 = rate[ROWS - 1 : ROWS]
    depth_31 = (
        surface_31 - advection * (flow_31 - flow_30) + diffusion * column_spread(surface_31)
        - rate_31 * (surface_31 - stored_31) + noise_31
    )
    inverse_31 = 1.0 / (1.0 + friction * jnp.abs(flow_31))
    down_ref[0:MEMBERS] = flow_31
    down_ref[MEMBERS : 2 * MEMBERS] = (flow_31 + gravity * depth_31 + flow_noise_31) * inverse_31
    down_ref[2 * MEMBERS : HALO] = gravity * inverse_31
    lane = lax.broadcasted_iota(jnp.int32, (1, COLS), 1)
    for k in range(SENS):
        cell = cell_ref[k]
        row = ((cell >> 8) & (ROWS - 1)).astype(f32)
        column = (cell & (COLS - 1)).astype(f32)
        reach = radius_ref[k].astype(f32)
        entry = jnp.where(lane == 0, row, jnp.where(lane == 1, column, jnp.where(lane == 2, reach * reach, 1.0)))
        up_ref[HALO + k : HALO + k + 1] = entry
        down_ref[HALO + k : HALO + k + 1] = entry


def forecast_kernel(
    cell_ref, surface_ref, discharge_ref, storage_ref, exchange_ref, depth_noise_ref, flow_noise_ref,
    up_ref, down_ref, before_ref, after_ref, radius_ref, observed_ref, sigma_ref,
    depth_ref, flow_ref, stored_ref, lik_ref, edge_ref,
):
    third = lambda ref, i: ref[i * MEMBERS : (i + 1) * MEMBERS]
    has_after = after_ref[HALO : HALO + 1, 3:4]
    flow_before = third(before_ref, 0)
    depth_0 = third(up_ref, 0) + advection * flow_before
    next_before = third(before_ref, 1) - third(before_ref, 2) * depth_0
    depth_32 = (third(after_ref, 0) + advection * third(down_ref, 0)) * has_after
    flow_31 = third(down_ref, 1) - third(down_ref, 2) * depth_32
    late_32 = (
        depth_32 * third(after_ref, 1) + diffusion * column_spread(depth_32) + third(after_ref, 2) + advection * flow_31
    ) * has_after
    edge_ref[0] = flow_before
    edge_ref[1] = next_before
    edge_ref[2] = depth_32
    edge_ref[3] = late_32
    rate = exchange_ref[...].astype(f32)
    row = lax.broadcasted_iota(jnp.int32, (ROWS, COLS), 0)

    def member(p, carry):
        depth = surface_ref[p].astype(f32)
        flow = discharge_ref[p].astype(f32)
        stored = storage_ref[p].astype(f32)
        for step in range(2):
            flow_below = jnp.where(row == 0, edge_ref[step, pl.ds(p, 1)], pltpu.roll(flow, 1, 0))
            inflow = rate * (depth - stored)
            depth_next = (
                depth - advection * (flow - flow_below) + diffusion * column_spread(depth) - inflow
                + depth_noise_ref[step, p].astype(f32)
            )
            stored = (1.0 - drainage) * stored + inflow
            depth_above = jnp.where(row == ROWS - 1, edge_ref[2 + step, pl.ds(p, 1)], pltpu.roll(depth_next, ROWS - 1, 0))
            flow = (flow - gravity * (depth_above - depth_next) + flow_noise_ref[step, p].astype(f32)) / (
                1.0 + friction * jnp.abs(flow)
            )
            depth = depth_next
        at = pl.ds(pl.multiple_of(p * ROWS, ROWS), ROWS)
        for ref, value in ((depth_ref, depth), (flow_ref, flow), (stored_ref, stored)):
            ref[0, at] = value[:, :LANES]
            ref[1, at] = value[:, LANES:]
        return carry

    lax.fori_loop(0, MEMBERS, member, 0)
    lane = lax.broadcasted_iota(jnp.int32, (MEMBERS, LANES), 1)
    sampled = jnp.zeros((MEMBERS, LANES), f32)
    for k in range(SENS):
        cell = cell_ref[k]
        found = depth_ref[(cell >> 7) & 1, pl.ds((cell >> 8) & (ROWS - 1), MEMBERS, stride=ROWS)]
        found = pltpu.roll(found, (k - cell) & (LANES - 1), 1)
        sampled = jnp.where(lane == k, found, sampled)
    misfit = (sampled[:, :SENS] - observed_ref[...]) / sigma_ref[...]
    reach = radius_ref[...].astype(f32)
    lik = -0.5 * misfit * misfit / (reach * reach)
    lik_ref[...] = jnp.concatenate([lik, jnp.zeros((MEMBERS, LANES - SENS), f32)], axis=1)


def taper_kernel(down_ref, before_ref, after_ref, taper_ref):
    entries = [ref[HALO:MESSAGE, 0:LANES] for ref in (before_ref, down_ref, after_ref)]
    column_at = lax.broadcasted_iota(jnp.int32, (SENS, COLS), 1).astype(f32)
    near, rows = [], []
    for shift, entry in zip((-ROWS, 0, ROWS), entries):
        gap = column_at - entry[:, 1:2]
        near.append(entry[:, 2:3] - gap * gap)
        rows.append(jnp.broadcast_to(entry[:, 0:1] + float(shift), (SENS, COLS)))
    blank = jnp.zeros((SENS, COLS), bf16)

    def at_row(r, carry):
        here = r.astype(f32)
        for part in range(3):
            gap = here - rows[part]
            value = jnp.maximum(near[part] - gap * gap, 0.0)
            coarse = value.astype(bf16)
            taper_ref[r, part * SENS : (part + 1) * SENS] = coarse
            taper_ref[r, LANES + part * SENS : LANES + (part + 1) * SENS] = (value - coarse.astype(f32)).astype(bf16)
        taper_ref[r, 3 * SENS : LANES] = blank
        taper_ref[r, LANES + 3 * SENS : 2 * LANES] = blank
        return carry

    lax.fori_loop(0, ROWS, at_row, 0)


def weight_kernel(taper_ref, lik_ref, before_ref, after_ref, depth_ref, flow_ref, stored_ref, out_ref, weight_ref):
    lik = before_ref[...] + pltpu.roll(lik_ref[...], SENS, 1) + pltpu.roll(after_ref[...], 2 * SENS, 1)
    high = lik.astype(bf16)
    rest = lik - high.astype(f32)
    middle = rest.astype(bf16)
    low = (rest - middle.astype(f32)).astype(bf16)
    pieces = jnp.concatenate([high.astype(f32), middle.astype(f32), low.astype(f32)], axis=0).astype(bf16)
    pieces = jnp.concatenate([pieces, pieces], axis=1)

    def at_row(r, carry):
        part = jnp.dot(pieces, taper_ref[r], preferred_element_type=f32)
        weight = part[:MEMBERS] + part[MEMBERS : 2 * MEMBERS] + part[2 * MEMBERS :]
        weight_ref[0, pl.ds(pl.multiple_of(r * MEMBERS, MEMBERS), MEMBERS)] = weight[:, :LANES]
        weight_ref[1, pl.ds(pl.multiple_of(r * MEMBERS, MEMBERS), MEMBERS)] = weight[:, LANES:]
        return carry

    lax.fori_loop(0, ROWS, at_row, 0)

    def block(i, carry):
        for half in range(2):
            weights = [weight_ref[half, pl.ds(i * 8 * MEMBERS + p, 8, stride=MEMBERS)] for p in range(MEMBERS)]
            best = weights[0]
            for p in range(1, MEMBERS):
                best = jnp.maximum(best, weights[p])
            sums = [jnp.zeros((8, LANES), f32) for _ in range(4)]
            for p in range(MEMBERS):
                factor = jnp.exp(weights[p] - best)
                at = pl.ds(pl.multiple_of(p * ROWS + i * 8, 8), 8)
                sums[0] = sums[0] + factor
                sums[1] = sums[1] + factor * depth_ref[half, at]
                sums[2] = sums[2] + factor * flow_ref[half, at]
                sums[3] = sums[3] + factor * stored_ref[half, at]
            inverse = 1.0 / sums[0]
            results = (best + jnp.log(sums[0]), sums[1] * inverse, sums[2] * inverse, sums[3] * inverse)
            for slot, result in enumerate(results):
                out_ref[pl.ds(i * 64 + 2 * slot + half, 8, stride=8)] = result
        return carry

    lax.fori_loop(0, ROWS // 8, block, 0)


def combine_kernel(groups, in_ref, out_ref):
    def quantity(slot, half):
        return in_ref[pl.ds(2 * slot + half, groups, stride=8)]

    rows = []
    totals = []
    for half in range(2):
        level = quantity(0, half)
        share = jnp.exp(level - jnp.max(level, axis=0, keepdims=True))
        totals.append((share, 1.0 / jnp.sum(share, axis=0, keepdims=True)))
    for slot in range(1, 4):
        for half in range(2):
            share, inverse = totals[half]
            rows.append(jnp.sum(share * quantity(slot, half), axis=0, keepdims=True) * inverse)
    rows.append(jnp.zeros((2, LANES), f32))
    result = jnp.concatenate(rows, axis=0)
    for copy in range(groups):
        out_ref[copy * 8 : (copy + 1) * 8] = result


def spread_kernel(in_ref, depth_ref, flow_ref, stored_ref):
    for slot, ref in enumerate((depth_ref, flow_ref, stored_ref)):
        for half in range(2):
            ref[:, half * LANES : (half + 1) * LANES] = in_ref[pl.ds(2 * slot + half, ROWS, stride=8)]


VMEM = pl.BlockSpec(memory_space=pltpu.VMEM)
SMEM = pl.BlockSpec(memory_space=pltpu.SMEM)


def call(kernel, name, in_specs, outs, scratch=(), flops=0, nbytes=0):
    return pl.pallas_call(
        kernel,
        name=name,
        in_specs=in_specs,
        out_specs=[VMEM] * len(outs),
        out_shape=[jax.ShapeDtypeStruct(shape, dtype) for shape, dtype in outs],
        scratch_shapes=list(scratch),
        compiler_params=pltpu.CompilerParams(vmem_limit_bytes=40 * 1024 * 1024),
        cost_estimate=pl.CostEstimate(flops=flops, bytes_accessed=nbytes, transcendentals=0),
    )


def local(
    surface, discharge, storage, exchange, depth_perturbation, flow_perturbation,
    sensor_cell, sensor_radius, observed, sensor_sigma,
):
    strips = lax.axis_size("strip")
    groups = lax.axis_size("dom")
    downward = [(i, i + 1) for i in range(strips - 1)]
    upward = [(i + 1, i) for i in range(strips - 1)]
    fields = (surface, discharge, storage, exchange, depth_perturbation, flow_perturbation)
    up, down = call(
        pack_kernel, "pack", [SMEM] * 2 + [VMEM] * 6, [((MESSAGE, COLS), f32)] * 2,
        [pltpu.VMEM((6, 2, MEMBERS * 8, LANES), f32), pltpu.VMEM((5, 2, MEMBERS * 8, LANES), f32)],
    )(sensor_cell, sensor_radius, *fields)
    before = lax.ppermute(down, "strip", downward)
    after = lax.ppermute(up, "strip", upward)
    grid = ((2, MEMBERS * ROWS, LANES), f32)
    as_row = lambda values: values.reshape(1, SENS)
    depth, flow, stored, lik = call(
        forecast_kernel, "forecast", [SMEM] + [VMEM] * 13, [grid, grid, grid, ((MEMBERS, LANES), f32)],
        [pltpu.VMEM((4, MEMBERS, COLS), f32)],
    )(sensor_cell, *fields, up, down, before, after, as_row(sensor_radius), as_row(observed), as_row(sensor_sigma))
    lik_before = lax.ppermute(lik, "strip", downward)
    lik_after = lax.ppermute(lik, "strip", upward)
    (taper,) = call(
        taper_kernel, "taper", [VMEM] * 3, [((ROWS, 2 * LANES, COLS), bf16)], nbytes=4 << 20, flops=8 << 20,
    )(down, before, after)
    (parts,) = call(
        weight_kernel, "weights", [VMEM] * 7, [((groups * 8, LANES), f32)],
        [pltpu.VMEM((2, ROWS * MEMBERS, LANES), f32)],
    )(taper, lik, lik_before, lik_after, depth, flow, stored)
    shared = lax.all_to_all(parts.reshape(groups, 8, LANES), "dom", 0, 0, tiled=True)
    (rows,) = call(
        lambda *refs: combine_kernel(groups, *refs), "combine", [VMEM], [((groups * 8, LANES), f32)],
    )(shared.reshape(groups * 8, LANES))
    whole = lax.all_to_all(rows.reshape(groups, 8, LANES), "dom", 0, 0, tiled=True)
    return tuple(
        call(spread_kernel, "spread", [VMEM], [((ROWS, COLS), f32)] * 3)(whole.reshape(groups * 8, LANES))
    )


def solution(mesh):
    return jax.shard_map(
        local,
        mesh=mesh,
        in_specs=(
            P("dom", "strip", None),
            P("dom", "strip", None),
            P("dom", "strip", None),
            P("strip", None),
            P(None, "dom", "strip", None),
            P(None, "dom", "strip", None),
            P("strip"),
            P("strip"),
            P("strip"),
            P("strip"),
        ),
        out_specs=(P("strip", None), P("strip", None), P("strip", None)),
        check_vma=False,
    )
```

```python
import jax
import jax.numpy as jnp
from jax import lax
from jax.experimental import pallas as pl
from jax.experimental.pallas import tpu as pltpu
from jax.sharding import PartitionSpec as P

advection = 0.4
gravity = 0.5
diffusion = 0.15
friction = 0.3
drainage = 0.1

MEMBERS = 24
ROWS = 32
COLS = 256
SENS = 32
LANES = 128
HALO = 3 * MEMBERS
MESSAGE = HALO + SENS

f32 = jnp.float32
bf16 = jnp.bfloat16


def column_spread(field):
    width = field.shape[-1]
    lane = lax.broadcasted_iota(jnp.int32, field.shape, field.ndim - 1)
    left_side = jnp.where(lane == 0, field, pltpu.roll(field, 1, field.ndim - 1))
    right_side = jnp.where(lane == width - 1, field, pltpu.roll(field, width - 1, field.ndim - 1))
    return left_side - 2.0 * field + right_side


def sides(left_half, right_half):
    lane = lax.broadcasted_iota(jnp.int32, left_half.shape, 1)
    first, last = lane == 0, lane == LANES - 1
    left_back, right_back = pltpu.roll(left_half, 1, 1), pltpu.roll(right_half, 1, 1)
    left_on, right_on = pltpu.roll(left_half, LANES - 1, 1), pltpu.roll(right_half, LANES - 1, 1)
    return (
        jnp.where(first, left_half, left_back) + jnp.where(last, right_on, left_on),
        jnp.where(first, left_back, right_back) + jnp.where(last, right_half, right_on),
    )


def load_kernel(
    cell_hbm, radius_hbm, surface_hbm, discharge_hbm, storage_hbm, exchange_hbm, depth_noise_hbm, flow_noise_hbm,
    up_ref, down_ref, surface_ref, discharge_ref, storage_ref, exchange_ref, depth_noise_ref, flow_noise_ref,
    first_ref, last_ref, cell_ref, radius_ref, sems,
):
    pairs = [
        (surface_hbm, surface_ref), (discharge_hbm, discharge_ref), (storage_hbm, storage_ref),
        (depth_noise_hbm.at[0], depth_noise_ref.at[0]), (flow_noise_hbm.at[0], flow_noise_ref.at[0]),
        (depth_noise_hbm.at[1], depth_noise_ref.at[1]), (exchange_hbm, exchange_ref),
        (cell_hbm, cell_ref), (radius_hbm, radius_ref), (flow_noise_hbm.at[1], flow_noise_ref.at[1]),
    ]
    copies = [pltpu.make_async_copy(source, target, sems.at[i]) for i, (source, target) in enumerate(pairs)]
    for copy in copies:
        copy.start()

    def keep(scratch, slot, rows):
        flat = rows.reshape(MEMBERS * 8, COLS)
        scratch[slot, 0] = flat[:, :LANES]
        scratch[slot, 1] = flat[:, LANES:]

    def take(ref, lead, slot):
        copies[slot].wait()
        keep(first_ref, slot, ref[lead + (slice(None), slice(0, 16), slice(None))].astype(f32)[:, :8])
        keep(last_ref, slot, ref[lead + (slice(None), slice(16, 32), slice(None))].astype(f32)[:, 8:])

    take(surface_ref, (), 0)
    take(discharge_ref, (), 1)
    take(storage_ref, (), 2)
    take(depth_noise_ref, (0,), 3)
    take(flow_noise_ref, (0,), 4)
    copies[5].wait()
    keep(first_ref, 5, depth_noise_ref[1, :, 0:16, :].astype(f32)[:, :8])
    for copy in copies[6:9]:
        copy.wait()

    def row_of(ref, slot, row):
        halves = [ref[slot, half, pl.ds(row, MEMBERS, stride=8)] for half in range(2)]
        return jnp.concatenate(halves, axis=1)

    rate = exchange_ref[...].astype(f32)
    surface_0, surface_1 = row_of(first_ref, 0, 0), row_of(first_ref, 0, 1)
    flow_0, flow_1 = row_of(first_ref, 1, 0), row_of(first_ref, 1, 1)
    stored_0, stored_1 = row_of(first_ref, 2, 0), row_of(first_ref, 2, 1)
    noise_0, noise_1 = row_of(first_ref, 3, 0), row_of(first_ref, 3, 1)
    flow_noise_0, late_0 = row_of(first_ref, 4, 0), row_of(first_ref, 5, 0)
    rate_0, rate_1 = rate[0:1], rate[1:2]
    inflow_0 = rate_0 * (surface_0 - stored_0)
    partial_0 = surface_0 - advection * flow_0 + diffusion * column_spread(surface_0) - inflow_0 + noise_0
    stored_next = (1.0 - drainage) * stored_0 + inflow_0
    depth_1 = (
        surface_1 - advection * (flow_1 - flow_0) + diffusion * column_spread(surface_1)
        - rate_1 * (surface_1 - stored_1) + noise_1
    )
    inverse_0 = 1.0 / (1.0 + friction * jnp.abs(flow_0))
    flow_part = (flow_0 - gravity * depth_1 + flow_noise_0) * inverse_0
    up_ref[0:MEMBERS] = partial_0
    up_ref[MEMBERS : 2 * MEMBERS] = 1.0 - rate_0 - (advection * gravity) * inverse_0
    up_ref[2 * MEMBERS : HALO] = rate_0 * stored_next + late_0 - advection * flow_part
    surface_31, flow_30, flow_31 = row_of(last_ref, 0, 7), row_of(last_ref, 1, 6), row_of(last_ref, 1, 7)
    stored_31, noise_31, flow_noise_31 = row_of(last_ref, 2, 7), row_of(last_ref, 3, 7), row_of(last_ref, 4, 7)
    rate_31 = rate[ROWS - 1 : ROWS]
    depth_31 = (
        surface_31 - advection * (flow_31 - flow_30) + diffusion * column_spread(surface_31)
        - rate_31 * (surface_31 - stored_31) + noise_31
    )
    inverse_31 = 1.0 / (1.0 + friction * jnp.abs(flow_31))
    down_ref[0:MEMBERS] = flow_31
    down_ref[MEMBERS : 2 * MEMBERS] = (flow_31 + gravity * depth_31 + flow_noise_31) * inverse_31
    down_ref[2 * MEMBERS : HALO] = gravity * inverse_31
    lane = lax.broadcasted_iota(jnp.int32, (1, COLS), 1)
    for k in range(SENS):
        cell = cell_ref[k]
        row = ((cell >> 8) & (ROWS - 1)).astype(f32)
        column = (cell & (COLS - 1)).astype(f32)
        reach = radius_ref[k].astype(f32)
        entry = jnp.where(lane == 0, row, jnp.where(lane == 1, column, jnp.where(lane == 2, reach * reach, 1.0)))
        up_ref[HALO + k : HALO + k + 1] = entry
        down_ref[HALO + k : HALO + k + 1] = entry
    copies[9].wait()


def forecast_kernel(
    cell_hbm, radius_hbm, observed_hbm, sigma_hbm,
    surface_ref, discharge_ref, storage_ref, exchange_ref, depth_noise_ref, flow_noise_ref,
    up_ref, down_ref, before_ref, after_ref,
    depth_ref, flow_ref, stored_ref, lik_ref,
    edge_ref, cell_ref, radius_ref, observed_ref, sigma_ref, sems,
):
    pairs = [(cell_hbm, cell_ref), (radius_hbm, radius_ref), (observed_hbm, observed_ref), (sigma_hbm, sigma_ref)]
    copies = [pltpu.make_async_copy(source, target, sems.at[i]) for i, (source, target) in enumerate(pairs)]
    for copy in copies:
        copy.start()
    third = lambda ref, i: ref[i * MEMBERS : (i + 1) * MEMBERS]
    has_after = after_ref[HALO : HALO + 1, 3:4]
    flow_before = third(before_ref, 0)
    depth_0 = third(up_ref, 0) + advection * flow_before
    next_before = third(before_ref, 1) - third(before_ref, 2) * depth_0
    depth_32 = (third(after_ref, 0) + advection * third(down_ref, 0)) * has_after
    flow_31 = third(down_ref, 1) - third(down_ref, 2) * depth_32
    late_32 = (
        depth_32 * third(after_ref, 1) + diffusion * column_spread(depth_32) + third(after_ref, 2) + advection * flow_31
    ) * has_after
    edge_ref[0] = flow_before
    edge_ref[1] = next_before
    edge_ref[2] = depth_32
    edge_ref[3] = late_32
    row = lax.broadcasted_iota(jnp.int32, (ROWS, LANES), 0)

    def halves(values):
        return [values[:, :LANES], values[:, LANES:]]

    rates = halves(exchange_ref[...].astype(f32))

    def member(p, carry):
        depth, flow, stored = [halves(ref[p].astype(f32)) for ref in (surface_ref, discharge_ref, storage_ref)]
        for step in range(2):
            depth_noise, flow_noise = [halves(ref[step, p].astype(f32)) for ref in (depth_noise_ref, flow_noise_ref)]
            row_before, row_after = [halves(edge_ref[slot, pl.ds(p, 1)]) for slot in (step, 2 + step)]
            beside = sides(*depth)
            for h in range(2):
                flow_below = jnp.where(row == 0, row_before[h], pltpu.roll(flow[h], 1, 0))
                inflow = rates[h] * (depth[h] - stored[h])
                depth_next = (
                    (1.0 - 2.0 * diffusion) * depth[h] + diffusion * beside[h]
                    - advection * (flow[h] - flow_below) - inflow + depth_noise[h]
                )
                stored[h] = (1.0 - drainage) * stored[h] + inflow
                depth_above = jnp.where(row == ROWS - 1, row_after[h], pltpu.roll(depth_next, ROWS - 1, 0))
                flow[h] = (flow[h] - gravity * (depth_above - depth_next) + flow_noise[h]) * (
                    1.0 / (1.0 + friction * jnp.abs(flow[h]))
                )
                depth[h] = depth_next
        at = pl.ds(pl.multiple_of(p * ROWS, ROWS), ROWS)
        for ref, value in ((depth_ref, depth), (flow_ref, flow), (stored_ref, stored)):
            for h in range(2):
                ref[h, at] = value[h]
        return carry

    lax.fori_loop(0, MEMBERS, member, 0, unroll=4)
    for copy in copies:
        copy.wait()
    lane = lax.broadcasted_iota(jnp.int32, (MEMBERS, LANES), 1)
    sampled = jnp.zeros((MEMBERS, LANES), f32)
    for k in range(SENS):
        cell = cell_ref[k]
        found = depth_ref[(cell >> 7) & 1, pl.ds((cell >> 8) & (ROWS - 1), MEMBERS, stride=ROWS)]
        found = pltpu.roll(found, (k - cell) & (LANES - 1), 1)
        sampled = jnp.where(lane == k, found, sampled)
    misfit = (sampled[:, :SENS] - observed_ref[...]) / sigma_ref[...]
    reach = radius_ref[...].astype(f32)
    lik = -0.5 * misfit * misfit / (reach * reach)
    lik_ref[...] = jnp.concatenate([lik, jnp.zeros((MEMBERS, LANES - SENS), f32)], axis=1)


def taper_kernel(down_ref, before_ref, after_ref, taper_ref):
    entries = [ref[HALO:MESSAGE, 0:LANES] for ref in (before_ref, down_ref, after_ref)]
    column_at = lax.broadcasted_iota(jnp.int32, (SENS, COLS), 1).astype(f32)
    near, rows = [], []
    for shift, entry in zip((-ROWS, 0, ROWS), entries):
        gap = column_at - entry[:, 1:2]
        near.append(entry[:, 2:3] - gap * gap)
        rows.append(jnp.broadcast_to(entry[:, 0:1] + float(shift), (SENS, COLS)))
    blank = jnp.zeros((SENS, COLS), bf16)

    def at_row(r, carry):
        here = r.astype(f32)
        for part in range(3):
            gap = here - rows[part]
            value = jnp.maximum(near[part] - gap * gap, 0.0)
            coarse = value.astype(bf16)
            taper_ref[r, part * SENS : (part + 1) * SENS] = coarse
            taper_ref[r, LANES + part * SENS : LANES + (part + 1) * SENS] = (value - coarse.astype(f32)).astype(bf16)
        taper_ref[r, 3 * SENS : LANES] = blank
        taper_ref[r, LANES + 3 * SENS : 2 * LANES] = blank
        return carry

    lax.fori_loop(0, ROWS, at_row, 0)


def weight_kernel(taper_ref, lik_ref, before_ref, after_ref, depth_ref, flow_ref, stored_ref, out_ref, weight_ref):
    lik = before_ref[...] + pltpu.roll(lik_ref[...], SENS, 1) + pltpu.roll(after_ref[...], 2 * SENS, 1)
    high = lik.astype(bf16)
    rest = lik - high.astype(f32)
    middle = rest.astype(bf16)
    low = (rest - middle.astype(f32)).astype(bf16)
    pieces = jnp.concatenate([high.astype(f32), middle.astype(f32), low.astype(f32)], axis=0).astype(bf16)
    pieces = jnp.concatenate([pieces, pieces], axis=1)

    for i in range(ROWS // 8):
        for r in range(8 * i, 8 * i + 8):
            part = jnp.dot(pieces, taper_ref[r], preferred_element_type=f32)
            weight = part[:MEMBERS] + part[MEMBERS : 2 * MEMBERS] + part[2 * MEMBERS :]
            for half in range(2):
                weight_ref[half, r * MEMBERS : (r + 1) * MEMBERS] = weight[:, half * LANES : (half + 1) * LANES]
        for half in range(2):
            weights = [weight_ref[half, pl.ds(8 * i * MEMBERS + p, 8, stride=MEMBERS)] for p in range(MEMBERS)]
            best = weights[0]
            for p in range(1, MEMBERS):
                best = jnp.maximum(best, weights[p])
            sums = [jnp.zeros((8, LANES), f32) for _ in range(4)]
            for p in range(MEMBERS):
                factor = jnp.exp(weights[p] - best)
                at = pl.ds(p * ROWS + 8 * i, 8)
                sums[0] = sums[0] + factor
                sums[1] = sums[1] + factor * depth_ref[half, at]
                sums[2] = sums[2] + factor * flow_ref[half, at]
                sums[3] = sums[3] + factor * stored_ref[half, at]
            inverse = 1.0 / sums[0]
            results = (best + jnp.log(sums[0]), sums[1] * inverse, sums[2] * inverse, sums[3] * inverse)
            for slot, result in enumerate(results):
                out_ref[pl.ds(64 * i + 2 * slot + half, 8, stride=8)] = result


def combine_kernel(groups, in_ref, out_ref):
    def quantity(slot, half):
        return in_ref[pl.ds(2 * slot + half, groups, stride=8)]

    rows = []
    totals = []
    for half in range(2):
        level = quantity(0, half)
        share = jnp.exp(level - jnp.max(level, axis=0, keepdims=True))
        totals.append((share, 1.0 / jnp.sum(share, axis=0, keepdims=True)))
    for slot in range(1, 4):
        for half in range(2):
            share, inverse = totals[half]
            rows.append(jnp.sum(share * quantity(slot, half), axis=0, keepdims=True) * inverse)
    rows.append(jnp.zeros((2, LANES), f32))
    result = jnp.concatenate(rows, axis=0)
    for copy in range(groups):
        out_ref[copy * 8 : (copy + 1) * 8] = result


def spread_kernel(in_ref, depth_ref, flow_ref, stored_ref):
    for slot, ref in enumerate((depth_ref, flow_ref, stored_ref)):
        for half in range(2):
            ref[:, half * LANES : (half + 1) * LANES] = in_ref[pl.ds(2 * slot + half, ROWS, stride=8)]


VMEM = pl.BlockSpec(memory_space=pltpu.VMEM)
HBM = pl.BlockSpec(memory_space=pltpu.HBM)


def call(kernel, name, in_specs, outs, scratch=(), flops=0, nbytes=0):
    return pl.pallas_call(
        kernel,
        name=name,
        in_specs=in_specs,
        out_specs=[VMEM] * len(outs),
        out_shape=[jax.ShapeDtypeStruct(shape, dtype) for shape, dtype in outs],
        scratch_shapes=list(scratch),
        compiler_params=pltpu.CompilerParams(vmem_limit_bytes=40 * 1024 * 1024),
        cost_estimate=pl.CostEstimate(flops=flops, bytes_accessed=nbytes, transcendentals=0),
    )


def local(
    surface, discharge, storage, exchange, depth_perturbation, flow_perturbation,
    sensor_cell, sensor_radius, observed, sensor_sigma,
):
    strips = lax.axis_size("strip")
    groups = lax.axis_size("dom")
    downward = [(i, i + 1) for i in range(strips - 1)]
    upward = [(i + 1, i) for i in range(strips - 1)]
    stay = lambda values: pltpu.with_memory_space_constraint(values, pltpu.HBM)
    fields = [stay(f) for f in (surface, discharge, storage, exchange, depth_perturbation, flow_perturbation)]
    sensor_cell = stay(sensor_cell)
    up, down, *fields = call(
        load_kernel, "load", [HBM] * 8, [((MESSAGE, COLS), f32)] * 2 + [(field.shape, field.dtype) for field in fields],
        [
            pltpu.VMEM((6, 2, MEMBERS * 8, LANES), f32), pltpu.VMEM((5, 2, MEMBERS * 8, LANES), f32),
            pltpu.SMEM((SENS,), jnp.int32), pltpu.SMEM((SENS,), jnp.int32), pltpu.SemaphoreType.DMA((10,)),
        ],
    )(sensor_cell, stay(sensor_radius), *fields)
    before = lax.ppermute(down, "strip", downward)
    after = lax.ppermute(up, "strip", upward)
    grid = ((2, MEMBERS * ROWS, LANES), f32)
    as_row = lambda values: stay(values.reshape(1, SENS))
    depth, flow, stored, lik = call(
        forecast_kernel, "forecast", [HBM] * 4 + [VMEM] * 10, [grid, grid, grid, ((MEMBERS, LANES), f32)],
        [
            pltpu.VMEM((4, MEMBERS, COLS), f32), pltpu.SMEM((SENS,), jnp.int32), pltpu.VMEM((1, SENS), jnp.int32),
            pltpu.VMEM((1, SENS), f32), pltpu.VMEM((1, SENS), f32), pltpu.SemaphoreType.DMA((4,)),
        ],
    )(sensor_cell, as_row(sensor_radius), as_row(observed), as_row(sensor_sigma), *fields, up, down, before, after)
    lik_before = lax.ppermute(lik, "strip", downward)
    lik_after = lax.ppermute(lik, "strip", upward)
    (taper,) = call(
        taper_kernel, "taper", [VMEM] * 3, [((ROWS, 2 * LANES, COLS), bf16)], nbytes=4 << 20, flops=8 << 20,
    )(down, before, after)
    (parts,) = call(
        weight_kernel, "weights", [VMEM] * 7, [((groups * 8, LANES), f32)],
        [pltpu.VMEM((2, ROWS * MEMBERS, LANES), f32)],
    )(taper, lik, lik_before, lik_after, depth, flow, stored)
    shared = lax.all_to_all(parts.reshape(groups, 8, LANES), "dom", 0, 0, tiled=True)
    (rows,) = call(
        lambda *refs: combine_kernel(groups, *refs), "combine", [VMEM], [((groups * 8, LANES), f32)],
    )(shared.reshape(groups * 8, LANES))
    whole = lax.all_to_all(rows.reshape(groups, 8, LANES), "dom", 0, 0, tiled=True)
    return tuple(
        call(spread_kernel, "spread", [VMEM], [((ROWS, COLS), f32)] * 3)(whole.reshape(groups * 8, LANES))
    )


def solution(mesh):
    return jax.shard_map(
        local,
        mesh=mesh,
        in_specs=(
            P("dom", "strip", None),
            P("dom", "strip", None),
            P("dom", "strip", None),
            P("strip", None),
            P(None, "dom", "strip", None),
            P(None, "dom", "strip", None),
            P("strip"),
            P("strip"),
            P("strip"),
            P("strip"),
        ),
        out_specs=(P("strip", None), P("strip", None), P("strip", None)),
        check_vma=False,
    )
```

```python
import jax
import jax.numpy as jnp
from jax import lax
from jax.experimental import pallas as pl
from jax.experimental.pallas import tpu as pltpu
from jax.sharding import PartitionSpec as P

advection = 0.4
gravity = 0.5
diffusion = 0.15
friction = 0.3
drainage = 0.1

MEMBERS = 24
ROWS = 32
COLS = 256
SENS = 32
LANES = 128
HALO = 3 * MEMBERS
MESSAGE = HALO + SENS

f32 = jnp.float32
bf16 = jnp.bfloat16


def column_spread(field):
    width = field.shape[-1]
    lane = lax.broadcasted_iota(jnp.int32, field.shape, field.ndim - 1)
    left_side = jnp.where(lane == 0, field, pltpu.roll(field, 1, field.ndim - 1))
    right_side = jnp.where(lane == width - 1, field, pltpu.roll(field, width - 1, field.ndim - 1))
    return left_side - 2.0 * field + right_side


def sides(left_half, right_half):
    lane = lax.broadcasted_iota(jnp.int32, left_half.shape, 1)
    first, last = lane == 0, lane == LANES - 1
    left_back, right_back = pltpu.roll(left_half, 1, 1), pltpu.roll(right_half, 1, 1)
    left_on, right_on = pltpu.roll(left_half, LANES - 1, 1), pltpu.roll(right_half, LANES - 1, 1)
    return (
        jnp.where(first, left_half, left_back) + jnp.where(last, right_on, left_on),
        jnp.where(first, left_back, right_back) + jnp.where(last, right_half, right_on),
    )


def load_kernel(
    cell_hbm, radius_hbm, surface_hbm, discharge_hbm, storage_hbm, exchange_hbm, depth_noise_hbm, flow_noise_hbm,
    up_ref, down_ref, surface_ref, discharge_ref, storage_ref, exchange_ref, depth_noise_ref, flow_noise_ref,
    first_ref, last_ref, cell_ref, radius_ref, sems,
):
    pairs = [
        (surface_hbm, surface_ref), (discharge_hbm, discharge_ref), (storage_hbm, storage_ref),
        (depth_noise_hbm.at[0], depth_noise_ref.at[0]), (flow_noise_hbm.at[0], flow_noise_ref.at[0]),
        (depth_noise_hbm.at[1], depth_noise_ref.at[1]), (exchange_hbm, exchange_ref),
        (cell_hbm, cell_ref), (radius_hbm, radius_ref), (flow_noise_hbm.at[1], flow_noise_ref.at[1]),
    ]
    copies = [pltpu.make_async_copy(source, target, sems.at[i]) for i, (source, target) in enumerate(pairs)]
    for copy in copies:
        copy.start()

    def keep(scratch, slot, rows):
        flat = rows.reshape(MEMBERS * 8, COLS)
        scratch[slot, 0] = flat[:, :LANES]
        scratch[slot, 1] = flat[:, LANES:]

    def take(ref, lead, slot):
        copies[slot].wait()
        keep(first_ref, slot, ref[lead + (slice(None), slice(0, 16), slice(None))].astype(f32)[:, :8])
        keep(last_ref, slot, ref[lead + (slice(None), slice(16, 32), slice(None))].astype(f32)[:, 8:])

    take(surface_ref, (), 0)
    take(discharge_ref, (), 1)
    take(storage_ref, (), 2)
    take(depth_noise_ref, (0,), 3)
    take(flow_noise_ref, (0,), 4)
    copies[5].wait()
    keep(first_ref, 5, depth_noise_ref[1, :, 0:16, :].astype(f32)[:, :8])
    for copy in copies[6:9]:
        copy.wait()

    def row_of(ref, slot, row):
        halves = [ref[slot, half, pl.ds(row, MEMBERS, stride=8)] for half in range(2)]
        return jnp.concatenate(halves, axis=1)

    rate = exchange_ref[...].astype(f32)
    surface_0, surface_1 = row_of(first_ref, 0, 0), row_of(first_ref, 0, 1)
    flow_0, flow_1 = row_of(first_ref, 1, 0), row_of(first_ref, 1, 1)
    stored_0, stored_1 = row_of(first_ref, 2, 0), row_of(first_ref, 2, 1)
    noise_0, noise_1 = row_of(first_ref, 3, 0), row_of(first_ref, 3, 1)
    flow_noise_0, late_0 = row_of(first_ref, 4, 0), row_of(first_ref, 5, 0)
    rate_0, rate_1 = rate[0:1], rate[1:2]
    inflow_0 = rate_0 * (surface_0 - stored_0)
    partial_0 = surface_0 - advection * flow_0 + diffusion * column_spread(surface_0) - inflow_0 + noise_0
    stored_next = (1.0 - drainage) * stored_0 + inflow_0
    depth_1 = (
        surface_1 - advection * (flow_1 - flow_0) + diffusion * column_spread(surface_1)
        - rate_1 * (surface_1 - stored_1) + noise_1
    )
    inverse_0 = 1.0 / (1.0 + friction * jnp.abs(flow_0))
    flow_part = (flow_0 - gravity * depth_1 + flow_noise_0) * inverse_0
    up_ref[0:MEMBERS] = partial_0
    up_ref[MEMBERS : 2 * MEMBERS] = 1.0 - rate_0 - (advection * gravity) * inverse_0
    up_ref[2 * MEMBERS : HALO] = rate_0 * stored_next + late_0 - advection * flow_part
    surface_31, flow_30, flow_31 = row_of(last_ref, 0, 7), row_of(last_ref, 1, 6), row_of(last_ref, 1, 7)
    stored_31, noise_31, flow_noise_31 = row_of(last_ref, 2, 7), row_of(last_ref, 3, 7), row_of(last_ref, 4, 7)
    rate_31 = rate[ROWS - 1 : ROWS]
    depth_31 = (
        surface_31 - advection * (flow_31 - flow_30) + diffusion * column_spread(surface_31)
        - rate_31 * (surface_31 - stored_31) + noise_31
    )
    inverse_31 = 1.0 / (1.0 + friction * jnp.abs(flow_31))
    down_ref[0:MEMBERS] = flow_31
    down_ref[MEMBERS : 2 * MEMBERS] = (flow_31 + gravity * depth_31 + flow_noise_31) * inverse_31
    down_ref[2 * MEMBERS : HALO] = gravity * inverse_31
    lane = lax.broadcasted_iota(jnp.int32, (1, COLS), 1)
    for k in range(SENS):
        cell = cell_ref[k]
        row = ((cell >> 8) & (ROWS - 1)).astype(f32)
        column = (cell & (COLS - 1)).astype(f32)
        reach = radius_ref[k].astype(f32)
        strip = (cell >> 13).astype(f32)
        entry = jnp.where(lane == 0, row, jnp.where(lane == 1, column, jnp.where(lane == 2, reach * reach, strip)))
        up_ref[HALO + k : HALO + k + 1] = entry
        down_ref[HALO + k : HALO + k + 1] = entry
    copies[9].wait()


def forecast_kernel(
    cell_hbm, radius_hbm, observed_hbm, sigma_hbm,
    surface_ref, discharge_ref, storage_ref, exchange_ref, depth_noise_ref, flow_noise_ref,
    up_ref, down_ref, before_ref, after_ref,
    depth_ref, flow_ref, stored_ref, lik_ref,
    edge_ref, cell_ref, radius_ref, observed_ref, sigma_ref, sems,
):
    pairs = [(cell_hbm, cell_ref), (radius_hbm, radius_ref), (observed_hbm, observed_ref), (sigma_hbm, sigma_ref)]
    copies = [pltpu.make_async_copy(source, target, sems.at[i]) for i, (source, target) in enumerate(pairs)]
    for copy in copies:
        copy.start()
    third = lambda ref, i: ref[i * MEMBERS : (i + 1) * MEMBERS]
    strip_of = lambda ref: ref[HALO : HALO + 1, 3:4]
    has_before = strip_of(before_ref) == strip_of(down_ref) - 1.0
    has_after = strip_of(after_ref) == strip_of(down_ref) + 1.0
    flow_before = jnp.where(has_before, third(before_ref, 0), 0.0)
    depth_0 = third(up_ref, 0) + advection * flow_before
    next_before = jnp.where(has_before, third(before_ref, 1) - third(before_ref, 2) * depth_0, 0.0)
    depth_32 = jnp.where(has_after, third(after_ref, 0) + advection * third(down_ref, 0), 0.0)
    flow_31 = third(down_ref, 1) - third(down_ref, 2) * depth_32
    late_32 = jnp.where(
        has_after,
        depth_32 * third(after_ref, 1) + diffusion * column_spread(depth_32) + third(after_ref, 2) + advection * flow_31,
        0.0,
    )
    edge_ref[0] = flow_before
    edge_ref[1] = next_before
    edge_ref[2] = depth_32
    edge_ref[3] = late_32
    row = lax.broadcasted_iota(jnp.int32, (ROWS, LANES), 0)

    def halves(values):
        return [values[:, :LANES], values[:, LANES:]]

    rates = halves(exchange_ref[...].astype(f32))

    def member(p, carry):
        depth, flow, stored = [halves(ref[p].astype(f32)) for ref in (surface_ref, discharge_ref, storage_ref)]
        for step in range(2):
            depth_noise, flow_noise = [halves(ref[step, p].astype(f32)) for ref in (depth_noise_ref, flow_noise_ref)]
            row_before, row_after = [halves(edge_ref[slot, pl.ds(p, 1)]) for slot in (step, 2 + step)]
            beside = sides(*depth)
            for h in range(2):
                flow_below = jnp.where(row == 0, row_before[h], pltpu.roll(flow[h], 1, 0))
                inflow = rates[h] * (depth[h] - stored[h])
                depth_next = (
                    (1.0 - 2.0 * diffusion) * depth[h] + diffusion * beside[h]
                    - advection * (flow[h] - flow_below) - inflow + depth_noise[h]
                )
                stored[h] = (1.0 - drainage) * stored[h] + inflow
                depth_above = jnp.where(row == ROWS - 1, row_after[h], pltpu.roll(depth_next, ROWS - 1, 0))
                flow[h] = (flow[h] - gravity * (depth_above - depth_next) + flow_noise[h]) * (
                    1.0 / (1.0 + friction * jnp.abs(flow[h]))
                )
                depth[h] = depth_next
        at = pl.ds(pl.multiple_of(p * ROWS, ROWS), ROWS)
        for ref, value in ((depth_ref, depth), (flow_ref, flow), (stored_ref, stored)):
            for h in range(2):
                ref[h, at] = value[h]
        return carry

    lax.fori_loop(0, MEMBERS, member, 0, unroll=4)
    for copy in copies:
        copy.wait()
    lane = lax.broadcasted_iota(jnp.int32, (MEMBERS, LANES), 1)
    sampled = jnp.zeros((MEMBERS, LANES), f32)
    for k in range(SENS):
        cell = cell_ref[k]
        found = depth_ref[(cell >> 7) & 1, pl.ds((cell >> 8) & (ROWS - 1), MEMBERS, stride=ROWS)]
        found = pltpu.roll(found, (k - cell) & (LANES - 1), 1)
        sampled = jnp.where(lane == k, found, sampled)
    misfit = (sampled[:, :SENS] - observed_ref[...]) / sigma_ref[...]
    reach = radius_ref[...].astype(f32)
    lik = -0.5 * misfit * misfit / (reach * reach)
    lik_ref[...] = jnp.concatenate([lik, jnp.zeros((MEMBERS, LANES - SENS), f32)], axis=1)


def taper_kernel(down_ref, before_ref, after_ref, taper_ref):
    entries = [ref[HALO:MESSAGE, 0:LANES] for ref in (before_ref, down_ref, after_ref)]
    column_at = lax.broadcasted_iota(jnp.int32, (SENS, COLS), 1).astype(f32)
    near, rows = [], []
    for shift, entry in zip((-ROWS, 0, ROWS), entries):
        gap = column_at - entry[:, 1:2]
        beside = entry[:, 3:4] == entries[1][:, 3:4] + float(shift // ROWS)
        near.append(jnp.where(beside, entry[:, 2:3], 0.0) - gap * gap)
        rows.append(jnp.broadcast_to(entry[:, 0:1] + float(shift), (SENS, COLS)))
    blank = jnp.zeros((SENS, COLS), bf16)

    def at_row(r, carry):
        here = r.astype(f32)
        for part in range(3):
            gap = here - rows[part]
            value = jnp.maximum(near[part] - gap * gap, 0.0)
            coarse = value.astype(bf16)
            taper_ref[r, part * SENS : (part + 1) * SENS] = coarse
            taper_ref[r, LANES + part * SENS : LANES + (part + 1) * SENS] = (value - coarse.astype(f32)).astype(bf16)
        taper_ref[r, 3 * SENS : LANES] = blank
        taper_ref[r, LANES + 3 * SENS : 2 * LANES] = blank
        return carry

    lax.fori_loop(0, ROWS, at_row, 0)


def weight_kernel(taper_ref, lik_ref, before_ref, after_ref, depth_ref, flow_ref, stored_ref, out_ref, weight_ref):
    lik = before_ref[...] + pltpu.roll(lik_ref[...], SENS, 1) + pltpu.roll(after_ref[...], 2 * SENS, 1)
    high = lik.astype(bf16)
    rest = lik - high.astype(f32)
    middle = rest.astype(bf16)
    low = (rest - middle.astype(f32)).astype(bf16)
    pieces = jnp.concatenate([high.astype(f32), middle.astype(f32), low.astype(f32)], axis=0).astype(bf16)
    pieces = jnp.concatenate([pieces, pieces], axis=1)

    for i in range(ROWS // 8):
        for r in range(8 * i, 8 * i + 8):
            part = jnp.dot(pieces, taper_ref[r], preferred_element_type=f32)
            weight = part[:MEMBERS] + part[MEMBERS : 2 * MEMBERS] + part[2 * MEMBERS :]
            for half in range(2):
                weight_ref[half, r * MEMBERS : (r + 1) * MEMBERS] = weight[:, half * LANES : (half + 1) * LANES]
        for half in range(2):
            weights = [weight_ref[half, pl.ds(8 * i * MEMBERS + p, 8, stride=MEMBERS)] for p in range(MEMBERS)]
            best = weights[0]
            for p in range(1, MEMBERS):
                best = jnp.maximum(best, weights[p])
            sums = [jnp.zeros((8, LANES), f32) for _ in range(4)]
            for p in range(MEMBERS):
                factor = jnp.exp(weights[p] - best)
                at = pl.ds(p * ROWS + 8 * i, 8)
                sums[0] = sums[0] + factor
                sums[1] = sums[1] + factor * depth_ref[half, at]
                sums[2] = sums[2] + factor * flow_ref[half, at]
                sums[3] = sums[3] + factor * stored_ref[half, at]
            inverse = 1.0 / sums[0]
            results = (best + jnp.log(sums[0]), sums[1] * inverse, sums[2] * inverse, sums[3] * inverse)
            for slot, result in enumerate(results):
                out_ref[pl.ds(64 * i + 2 * slot + half, 8, stride=8)] = result


def combine_kernel(groups, in_ref, out_ref):
    def quantity(slot, half):
        return in_ref[pl.ds(2 * slot + half, groups, stride=8)]

    rows = []
    totals = []
    for half in range(2):
        level = quantity(0, half)
        share = jnp.exp(level - jnp.max(level, axis=0, keepdims=True))
        totals.append((share, 1.0 / jnp.sum(share, axis=0, keepdims=True)))
    for slot in range(1, 4):
        for half in range(2):
            share, inverse = totals[half]
            rows.append(jnp.sum(share * quantity(slot, half), axis=0, keepdims=True) * inverse)
    rows.append(jnp.zeros((2, LANES), f32))
    result = jnp.concatenate(rows, axis=0)
    for copy in range(groups):
        out_ref[copy * 8 : (copy + 1) * 8] = result


def spread_kernel(in_ref, depth_ref, flow_ref, stored_ref):
    for slot, ref in enumerate((depth_ref, flow_ref, stored_ref)):
        for half in range(2):
            ref[:, half * LANES : (half + 1) * LANES] = in_ref[pl.ds(2 * slot + half, ROWS, stride=8)]


VMEM = pl.BlockSpec(memory_space=pltpu.VMEM)
HBM = pl.BlockSpec(memory_space=pltpu.HBM)


def call(kernel, name, in_specs, outs, scratch=(), flops=0, nbytes=0):
    return pl.pallas_call(
        kernel,
        name=name,
        in_specs=in_specs,
        out_specs=[VMEM] * len(outs),
        out_shape=[jax.ShapeDtypeStruct(shape, dtype) for shape, dtype in outs],
        scratch_shapes=list(scratch),
        compiler_params=pltpu.CompilerParams(vmem_limit_bytes=40 * 1024 * 1024),
        cost_estimate=pl.CostEstimate(flops=flops, bytes_accessed=nbytes, transcendentals=0),
    )


def local(
    surface, discharge, storage, exchange, depth_perturbation, flow_perturbation,
    sensor_cell, sensor_radius, observed, sensor_sigma,
):
    strips = lax.axis_size("strip")
    groups = lax.axis_size("dom")
    downward = [(i, (i + 1) % strips) for i in range(strips)]
    upward = [((i + 1) % strips, i) for i in range(strips)]
    stay = lambda values: pltpu.with_memory_space_constraint(values, pltpu.HBM)
    fields = [stay(f) for f in (surface, discharge, storage, exchange, depth_perturbation, flow_perturbation)]
    sensor_cell = stay(sensor_cell)
    up, down, *fields = call(
        load_kernel, "load", [HBM] * 8, [((MESSAGE, COLS), f32)] * 2 + [(field.shape, field.dtype) for field in fields],
        [
            pltpu.VMEM((6, 2, MEMBERS * 8, LANES), f32), pltpu.VMEM((5, 2, MEMBERS * 8, LANES), f32),
            pltpu.SMEM((SENS,), jnp.int32), pltpu.SMEM((SENS,), jnp.int32), pltpu.SemaphoreType.DMA((10,)),
        ],
    )(sensor_cell, stay(sensor_radius), *fields)
    before = lax.ppermute(down, "strip", downward)
    after = lax.ppermute(up, "strip", upward)
    grid = ((2, MEMBERS * ROWS, LANES), f32)
    as_row = lambda values: stay(values.reshape(1, SENS))
    depth, flow, stored, lik = call(
        forecast_kernel, "forecast", [HBM] * 4 + [VMEM] * 10, [grid, grid, grid, ((MEMBERS, LANES), f32)],
        [
            pltpu.VMEM((4, MEMBERS, COLS), f32), pltpu.SMEM((SENS,), jnp.int32), pltpu.VMEM((1, SENS), jnp.int32),
            pltpu.VMEM((1, SENS), f32), pltpu.VMEM((1, SENS), f32), pltpu.SemaphoreType.DMA((4,)),
        ],
    )(sensor_cell, as_row(sensor_radius), as_row(observed), as_row(sensor_sigma), *fields, up, down, before, after)
    lik_before = lax.ppermute(lik, "strip", downward)
    lik_after = lax.ppermute(lik, "strip", upward)
    (taper,) = call(
        taper_kernel, "taper", [VMEM] * 3, [((ROWS, 2 * LANES, COLS), bf16)], nbytes=4 << 20, flops=8 << 20,
    )(down, before, after)
    (parts,) = call(
        weight_kernel, "weights", [VMEM] * 7, [((groups * 8, LANES), f32)],
        [pltpu.VMEM((2, ROWS * MEMBERS, LANES), f32)],
    )(taper, lik, lik_before, lik_after, depth, flow, stored)
    shared = lax.all_to_all(parts.reshape(groups, 8, LANES), "dom", 0, 0, tiled=True)
    (rows,) = call(
        lambda *refs: combine_kernel(groups, *refs), "combine", [VMEM], [((groups * 8, LANES), f32)],
    )(shared.reshape(groups * 8, LANES))
    whole = lax.all_to_all(rows.reshape(groups, 8, LANES), "dom", 0, 0, tiled=True)
    return tuple(
        call(spread_kernel, "spread", [VMEM], [((ROWS, COLS), f32)] * 3)(whole.reshape(groups * 8, LANES))
    )


def solution(mesh):
    return jax.shard_map(
        local,
        mesh=mesh,
        in_specs=(
            P("dom", "strip", None),
            P("dom", "strip", None),
            P("dom", "strip", None),
            P("strip", None),
            P(None, "dom", "strip", None),
            P(None, "dom", "strip", None),
            P("strip"),
            P("strip"),
            P("strip"),
            P("strip"),
        ),
        out_specs=(P("strip", None), P("strip", None), P("strip", None)),
        check_vma=False,
    )
```

```python
import jax
import jax.numpy as jnp
from jax import lax
from jax.experimental import pallas as pl
from jax.experimental.pallas import tpu as pltpu
from jax.sharding import PartitionSpec as P

advection = 0.4
gravity = 0.5
diffusion = 0.15
friction = 0.3
drainage = 0.1

MEMBERS = 24
ROWS = 32
COLS = 256
SENS = 32
LANES = 128
SAMPLED = 6 * MEMBERS
SLOPE = SAMPLED + MEMBERS
ENTRY = SLOPE + MEMBERS
ACROSS = ENTRY + SENS
MESSAGE = ACROSS + 8

f32 = jnp.float32
bf16 = jnp.bfloat16


def sides(left_half, right_half):
    lane = lax.broadcasted_iota(jnp.int32, left_half.shape, 1)
    first, last = lane == 0, lane == LANES - 1
    left_back, right_back = pltpu.roll(left_half, 1, 1), pltpu.roll(right_half, 1, 1)
    left_on, right_on = pltpu.roll(left_half, LANES - 1, 1), pltpu.roll(right_half, LANES - 1, 1)
    return (
        jnp.where(first, left_half, left_back) + jnp.where(last, right_on, left_on),
        jnp.where(first, left_back, right_back) + jnp.where(last, right_half, right_on),
    )


def spread(field):
    return [diffusion * (around - 2.0 * here) for around, here in zip(sides(*field), field)]


def halves(values):
    return [values[:, :LANES], values[:, LANES:]]


def each(function, *rows):
    return [function(*parts) for parts in zip(*rows)]


def put(ref, slot, row):
    for h in range(2):
        ref[(2 * slot + h) * MEMBERS : (2 * slot + h + 1) * MEMBERS] = row[h]


def get(ref, slot):
    return [ref[(2 * slot + h) * MEMBERS : (2 * slot + h + 1) * MEMBERS] for h in range(2)]


def forecast_kernel(
    cell_hbm, radii_hbm, cells_hbm, radius_hbm, observed_hbm, sigma_hbm,
    surface_hbm, discharge_hbm, storage_hbm, exchange_hbm, depth_noise_hbm, flow_noise_hbm,
    own_ref, along_ref, across_ref, far_ref, extra_ref, depth_ref, flow_ref, stored_ref,
    surface_ref, discharge_ref, storage_ref, exchange_ref, depth_noise_ref, flow_noise_ref,
    first_ref, last_ref, slope_ref, cell_ref, radii_ref, cells_ref, radius_ref, observed_ref, sigma_ref, sems,
):
    pairs = [
        (surface_hbm, surface_ref), (discharge_hbm, discharge_ref), (storage_hbm, storage_ref),
        (depth_noise_hbm.at[0], depth_noise_ref.at[0]), (flow_noise_hbm.at[0], flow_noise_ref.at[0]),
        (depth_noise_hbm.at[1], depth_noise_ref.at[1]), (flow_noise_hbm.at[1], flow_noise_ref.at[1]),
        (exchange_hbm, exchange_ref), (cell_hbm, cell_ref), (radii_hbm, radii_ref), (cells_hbm, cells_ref), (radius_hbm, radius_ref),
        (observed_hbm, observed_ref), (sigma_hbm, sigma_ref),
    ]
    copies = [pltpu.make_async_copy(source, target, sems.at[i]) for i, (source, target) in enumerate(pairs)]
    for copy in copies:
        copy.start()

    def keep(scratch, slot, rows):
        flat = rows.reshape(MEMBERS * 8, COLS)
        scratch[slot, 0] = flat[:, :LANES]
        scratch[slot, 1] = flat[:, LANES:]

    def take(ref, lead, slot):
        copies[slot].wait()
        keep(first_ref, slot, ref[lead + (slice(None), slice(0, 16), slice(None))].astype(f32)[:, :8])
        if slot != 5:
            keep(last_ref, slot, ref[lead + (slice(None), slice(16, 32), slice(None))].astype(f32)[:, 8:])

    take(surface_ref, (), 0)
    take(discharge_ref, (), 1)
    take(storage_ref, (), 2)
    take(depth_noise_ref, (0,), 3)
    take(flow_noise_ref, (0,), 4)
    take(depth_noise_ref, (1,), 5)
    take(flow_noise_ref, (1,), 6)
    for copy in copies[7:]:
        copy.wait()

    def row_of(ref, slot, row):
        return [ref[slot, h, pl.ds(row, MEMBERS, stride=8)] for h in range(2)]

    def step_one(surface, flow, flow_below, stored, rate, noise):
        return each(
            lambda s, q, b, t, e, n, d: s - advection * (q - b) + d - e * (s - t) + n,
            surface, flow, flow_below, stored, rate, noise, spread(surface),
        )

    nothing = [jnp.zeros((MEMBERS, LANES), f32)] * 2
    rate = halves(exchange_ref[...].astype(f32))
    rate_0, rate_1, rate_31 = [[r[i : i + 1] for r in rate] for i in (0, 1, ROWS - 1)]
    surface_0, surface_1 = row_of(first_ref, 0, 0), row_of(first_ref, 0, 1)
    flow_0, flow_1 = row_of(first_ref, 1, 0), row_of(first_ref, 1, 1)
    stored_0, stored_1 = row_of(first_ref, 2, 0), row_of(first_ref, 2, 1)
    depth_0 = step_one(surface_0, flow_0, nothing, stored_0, rate_0, row_of(first_ref, 3, 0))
    depth_1 = step_one(surface_1, flow_1, flow_0, stored_1, rate_1, row_of(first_ref, 3, 1))
    stored_next = each(lambda s, t, e: (1.0 - drainage) * t + e * (s - t), surface_0, stored_0, rate_0)
    inverse_0 = each(lambda q: 1.0 / (1.0 + friction * jnp.abs(q)), flow_0)
    flow_part = each(
        lambda q, d, n, i: (q - gravity * d + n) * i, flow_0, depth_1, row_of(first_ref, 4, 0), inverse_0
    )
    up_ref, down_ref = own_ref.at[0], own_ref.at[1]
    put(up_ref, 0, depth_0)
    put(up_ref, 1, each(lambda e, i: 1.0 - e - (advection * gravity) * i, rate_0, inverse_0))
    put(up_ref, 2, each(lambda e, t, n, q: e * t + n - advection * q, rate_0, stored_next, row_of(first_ref, 5, 0), flow_part))
    flow_31 = row_of(last_ref, 1, 7)
    depth_31 = step_one(
        row_of(last_ref, 0, 7), flow_31, row_of(last_ref, 1, 6), row_of(last_ref, 2, 7), rate_31, row_of(last_ref, 3, 7)
    )
    inverse_31 = each(lambda q: 1.0 / (1.0 + friction * jnp.abs(q)), flow_31)
    put(down_ref, 0, flow_31)
    put(down_ref, 1, each(lambda q, d, n, i: (q + gravity * d + n) * i, flow_31, depth_31, row_of(last_ref, 4, 7), inverse_31))
    put(down_ref, 2, each(lambda i: gravity * i, inverse_31))
    put(far_ref, 0, flow_31)
    put(extra_ref, 0, each(lambda i: gravity * i, inverse_0))
    put(extra_ref, 1, each(lambda q, i, d: q + gravity * i * d, flow_part, inverse_0, depth_0))
    put(extra_ref, 2, row_of(first_ref, 6, 0))
    put(extra_ref, 3, row_of(last_ref, 6, 7))
    put(extra_ref, 6, each(lambda e, z: e + z, rate_0, nothing))
    for h in range(2):
        slope_ref[h] = (advection * advection * gravity) * inverse_0[h]

    row = lax.broadcasted_iota(jnp.int32, (ROWS, LANES), 0)

    def member(p, carry):
        depth, flow, stored = [halves(ref[p].astype(f32)) for ref in (surface_ref, discharge_ref, storage_ref)]
        for step in range(2):
            depth_noise, flow_noise = [halves(ref[step, p].astype(f32)) for ref in (depth_noise_ref, flow_noise_ref)]
            beside = sides(*depth)
            for h in range(2):
                flow_below = jnp.where(row == 0, 0.0, pltpu.roll(flow[h], 1, 0))
                inflow = rate[h] * (depth[h] - stored[h])
                depth_next = (
                    (1.0 - 2.0 * diffusion) * depth[h] + diffusion * beside[h]
                    - advection * (flow[h] - flow_below) - inflow + depth_noise[h]
                )
                stored[h] = (1.0 - drainage) * stored[h] + inflow
                depth_above = jnp.where(row == ROWS - 1, 0.0, pltpu.roll(depth_next, ROWS - 1, 0))
                flow[h] = (flow[h] - gravity * (depth_above - depth_next) + flow_noise[h]) * (
                    1.0 / (1.0 + friction * jnp.abs(flow[h]))
                )
                depth[h] = depth_next
                if step == 0:
                    edge = pl.ds(pl.multiple_of(p * 8, 8), 8)
                    first_ref[7, h, edge] = flow[h][:8]
                    last_ref[7, h, edge] = flow[h][ROWS - 8 :]
        at = pl.ds(pl.multiple_of(p * ROWS, ROWS), ROWS)
        for ref, value in ((depth_ref, depth), (flow_ref, flow), (stored_ref, stored)):
            for h in range(2):
                ref[h, at] = value[h]
        return carry

    lax.fori_loop(0, MEMBERS, member, 0, unroll=4)
    put(extra_ref, 4, each(lambda q: 1.0 / (1.0 + friction * jnp.abs(q)), row_of(first_ref, 7, 1)))
    put(extra_ref, 5, each(lambda q: 1.0 / (1.0 + friction * jnp.abs(q)), row_of(last_ref, 7, 6)))

    lane = lax.broadcasted_iota(jnp.int32, (MEMBERS, LANES), 1)
    one_lane = lax.broadcasted_iota(jnp.int32, (1, LANES), 1)
    sampled, slope = jnp.zeros((MEMBERS, LANES), f32), jnp.zeros((MEMBERS, LANES), f32)
    for k in range(SENS):
        cell = cell_ref[k]
        half, line, turn = (cell >> 7) & 1, (cell >> 8) & (ROWS - 1), (k - cell) & (LANES - 1)
        found = pltpu.roll(depth_ref[half, pl.ds(line, MEMBERS, stride=ROWS)], turn, 1)
        sampled = jnp.where(lane == k, found, sampled)
        slope = jnp.where(lane == k, pltpu.roll(slope_ref[half], turn, 1), slope)
        place, column = line.astype(f32), (cell & (COLS - 1)).astype(f32)
        strip = (cell >> 13).astype(f32)
        reach = radii_ref[k].astype(f32)
        entry = jnp.where(
            one_lane == 0, place, jnp.where(one_lane == 1, column, jnp.where(one_lane == 2, reach * reach, strip))
        )
        for i in range(2):
            own_ref[i, ENTRY + k : ENTRY + k + 1] = entry
    cells = cells_ref[...]
    place = ((cells >> 8) & (ROWS - 1)).astype(f32)
    reach = radius_ref[...].astype(f32)
    facts = [
        place, (cells & (COLS - 1)).astype(f32), reach * reach, (cells >> 13).astype(f32),
        observed_ref[...], sigma_ref[...], jnp.zeros((2, SENS), f32),
    ]
    facts = jnp.concatenate([jnp.concatenate(facts, axis=0), jnp.ones((8, LANES - SENS), f32)], axis=1)
    slope = jnp.where(facts[0:1] == 1.0, slope, 0.0)
    for i in range(2):
        own_ref[i, SAMPLED:SLOPE] = sampled
        own_ref[i, SLOPE:ENTRY] = slope
        own_ref[i, ACROSS:MESSAGE] = facts
    odd = (cell_ref[0] >> 13) & 1
    along_ref[...] = own_ref[odd]
    across_ref[0] = own_ref[1 - odd]


def join_kernel(across_ref, arrived_ref, joined_ref):
    del across_ref
    joined_ref[1] = arrived_ref[...]


def finish_kernel(
    own_ref, extra_ref, arrived_ref, far_ref, joined_ref, depth_in, flow_in, stored_in,
    out_ref, depth_ref, flow_ref, stored_ref,
    before_ref, after_ref, near_ref, taper_ref, weight_ref,
):
    del depth_in, flow_in, stored_in
    up_ref, down_ref = own_ref.at[0], own_ref.at[1]
    strip = own_ref[0, ACROSS + 3 : ACROSS + 4, 0:1]
    odd = strip - 2.0 * jnp.floor(0.5 * strip) > 0.5
    before_ref[...] = jnp.where(odd, joined_ref[0], joined_ref[1])
    after_ref[...] = jnp.where(odd, joined_ref[1], joined_ref[0])
    has_before = before_ref[ACROSS + 3 : ACROSS + 4, 0:1] == strip - 1.0
    has_after = after_ref[ACROSS + 3 : ACROSS + 4, 0:1] == strip + 1.0
    keep = lambda condition, row: each(lambda v: jnp.where(condition, v, 0.0), row)

    def line(ref, row):
        return [ref[h, pl.ds(row, MEMBERS, stride=ROWS)] for h in range(2)]

    def set_line(ref, row, values):
        for h in range(2):
            ref[h, pl.ds(row, MEMBERS, stride=ROWS)] = values[h]

    back = keep(has_before, get(before_ref, 0))
    start = each(lambda d, q: d + advection * q, get(up_ref, 0), back)
    back_next = keep(has_before, each(lambda f, i, d: f - i * d, get(before_ref, 1), get(before_ref, 2), start))
    depth_0 = each(
        lambda d, c, s, k, q: d * c + s + k + advection * q,
        start, get(up_ref, 1), spread(start), get(up_ref, 2), back_next,
    )
    turn_0 = get(extra_ref, 0)
    more_1 = each(lambda i, q: (advection * advection) * i * q, turn_0, back)
    depth_1 = each(lambda d, m: d + m, line(depth_ref, 1), more_1)
    flow_0 = each(lambda f, i, q: f + advection * i * q, get(extra_ref, 1), turn_0, back)
    set_line(depth_ref, 0, depth_0)
    set_line(depth_ref, 1, depth_1)
    set_line(flow_ref, 0, each(
        lambda f, a, d, n: (f - gravity * (a - d) + n) * (1.0 / (1.0 + friction * jnp.abs(f))),
        flow_0, depth_1, depth_0, get(extra_ref, 2),
    ))
    set_line(flow_ref, 1, each(lambda f, i, m: f + gravity * i * m, line(flow_ref, 1), get(extra_ref, 4), more_1))
    set_line(stored_ref, 0, each(lambda t, e, q: t + advection * e * q, line(stored_ref, 0), get(extra_ref, 6), back))
    last = get(down_ref, 0)
    end = keep(has_after, each(lambda d, q: d + advection * q, get(after_ref, 0), last))
    flow_31 = each(lambda f, i, d: f - i * d, get(down_ref, 1), get(down_ref, 2), end)
    depth_32 = keep(has_after, each(
        lambda d, c, s, k, q: d * c + s + k + advection * q,
        end, get(after_ref, 1), spread(end), get(after_ref, 2), flow_31,
    ))
    more_31 = each(lambda i, d: advection * i * d, get(down_ref, 2), end)
    depth_31 = each(lambda d, m: d + m, line(depth_ref, ROWS - 1), more_31)
    set_line(depth_ref, ROWS - 1, depth_31)
    set_line(flow_ref, ROWS - 1, each(
        lambda f, a, d, n: (f - gravity * (a - d) + n) * (1.0 / (1.0 + friction * jnp.abs(f))),
        flow_31, depth_32, depth_31, get(extra_ref, 3),
    ))
    set_line(flow_ref, ROWS - 2, each(
        lambda f, i, m: f - gravity * i * m, line(flow_ref, ROWS - 2), get(extra_ref, 5), more_31
    ))

    lane = lax.broadcasted_iota(jnp.int32, (1, LANES), 1)
    group = lane // SENS

    def beside(ref, first, count):
        parts = (before_ref[first : first + count], ref[0, first : first + count], after_ref[first : first + count])
        parts = [parts[0], pltpu.roll(parts[1], SENS, 1), pltpu.roll(parts[2], 2 * SENS, 1)]
        return jnp.where(group == 0, parts[0], jnp.where(group == 1, parts[1], parts[2]))

    facts = beside(own_ref, ACROSS, 8)
    place, column = facts[0:1], facts[1:2]
    hit = (lax.broadcasted_iota(jnp.int32, (COLS, LANES), 0).astype(f32) == column).astype(f32)

    def sample(rows):
        left, right = [], []
        for values, wanted, in_group, pieces in rows:
            values = jnp.concatenate(values, axis=1)
            stack = []
            for _ in range(pieces):
                piece = values.astype(bf16).astype(f32)
                stack.append(piece)
                values = values - piece
            left.append(jnp.concatenate(stack, axis=0).astype(bf16))
            right.append(jnp.where((place == wanted) & (group == in_group), hit, 0.0).astype(bf16))
        total = jnp.dot(jnp.concatenate(left, axis=1), jnp.concatenate(right, axis=0), preferred_element_type=f32)
        return sum(total[i * MEMBERS : (i + 1) * MEMBERS] for i in range(1, pieces)) + total[:MEMBERS] if pieces > 1 else total

    far = each(lambda a, b: jnp.where(strip > 1.5, jnp.where(odd, a, b), 0.0), get(arrived_ref, 0), get(far_ref, 0))
    added = sample([
        (each(lambda i, d: advection * i * d, keep(has_before, get(before_ref, 2)), start), ROWS - 1.0, 0, 3),
        (depth_0, 0.0, 1, 3), (more_1, 1.0, 1, 3), (more_31, ROWS - 1.0, 1, 3),
        (depth_32, 0.0, 2, 3),
    ])
    beyond = sample([(far, 1.0, 0, 1), (last, 1.0, 2, 1)])
    known = jnp.where((place == 0.0) & (group > 0), 0.0, beside(own_ref, SAMPLED, MEMBERS))
    found = known + added + beside(own_ref, SLOPE, MEMBERS) * beyond
    real = group < 3
    misfit = (found - facts[4:5]) / jnp.where(real, facts[5:6], 1.0)
    lik = jnp.where(real, -0.5 * misfit * misfit / jnp.where(real, facts[2:3], 1.0), 0.0)
    stack = []
    rest = lik
    for _ in range(3):
        piece = rest.astype(bf16).astype(f32)
        stack.append(piece)
        rest = rest - piece
    pieces = jnp.concatenate(stack, axis=0)
    turned = pltpu.roll(pieces, 3 * SENS, 1)
    pieces = jnp.concatenate(
        [jnp.where(lane < 3 * SENS, pieces, turned), jnp.where(lane < 3 * SENS, turned, 0.0)], axis=1
    )[:, : 6 * SENS].astype(bf16)

    entries = [ref[ENTRY:ACROSS] for ref in (before_ref, down_ref, after_ref)]
    column_at = lax.broadcasted_iota(jnp.int32, (SENS, COLS), 1).astype(f32)
    lines = []
    for part, (entry, offset) in enumerate(zip(entries, (-1.0, 0.0, 1.0))):
        gap = column_at - entry[:, 1:2]
        squared = jnp.where(entry[:, 3:4] == strip + offset, entry[:, 2:3], 0.0)
        near_ref[part] = squared - gap * gap
        lines.append(jnp.broadcast_to(entry[:, 0:1] + offset * ROWS, (SENS, LANES)))

    def at_row(r, carry):
        here = r.astype(f32)
        for part in range(3):
            gap = here - lines[part]
            gap = gap * gap
            value = jnp.maximum(near_ref[part] - jnp.concatenate([gap, gap], axis=1), 0.0)
            coarse = value.astype(bf16)
            taper_ref[r, part * SENS : (part + 1) * SENS] = coarse
            taper_ref[r, (3 + part) * SENS : (4 + part) * SENS] = (value - coarse.astype(f32)).astype(bf16)
        return carry

    lax.fori_loop(0, ROWS, at_row, 0, unroll=2)

    for i in range(ROWS // 8):
        for r in range(8 * i, 8 * i + 8):
            part = jnp.dot(pieces, taper_ref[r], preferred_element_type=f32)
            weight = part[:MEMBERS] + part[MEMBERS : 2 * MEMBERS] + part[2 * MEMBERS :]
            for half in range(2):
                weight_ref[half, r * MEMBERS : (r + 1) * MEMBERS] = weight[:, half * LANES : (half + 1) * LANES]
        for half in range(2):
            weights = [weight_ref[half, pl.ds(8 * i * MEMBERS + p, 8, stride=MEMBERS)] for p in range(MEMBERS)]
            best = weights[0]
            for p in range(1, MEMBERS):
                best = jnp.maximum(best, weights[p])
            sums = [jnp.zeros((8, LANES), f32) for _ in range(4)]
            for p in range(MEMBERS):
                factor = jnp.exp(weights[p] - best)
                at = pl.ds(p * ROWS + 8 * i, 8)
                sums[0] = sums[0] + factor
                sums[1] = sums[1] + factor * depth_ref[half, at]
                sums[2] = sums[2] + factor * flow_ref[half, at]
                sums[3] = sums[3] + factor * stored_ref[half, at]
            inverse = 1.0 / sums[0]
            results = (best + jnp.log(sums[0]), sums[1] * inverse, sums[2] * inverse, sums[3] * inverse)
            for slot, result in enumerate(results):
                out_ref[pl.ds(64 * i + 2 * slot + half, 8, stride=8)] = result


def combine_kernel(groups, in_ref, out_ref):
    def quantity(slot, half):
        return in_ref[pl.ds(2 * slot + half, groups, stride=8)]

    rows = []
    totals = []
    for half in range(2):
        level = quantity(0, half)
        share = jnp.exp(level - jnp.max(level, axis=0, keepdims=True))
        totals.append((share, 1.0 / jnp.sum(share, axis=0, keepdims=True)))
    for slot in range(1, 4):
        for half in range(2):
            share, inverse = totals[half]
            rows.append(jnp.sum(share * quantity(slot, half), axis=0, keepdims=True) * inverse)
    rows.append(jnp.zeros((2, LANES), f32))
    result = jnp.concatenate(rows, axis=0)
    for copy in range(groups):
        out_ref[copy * 8 : (copy + 1) * 8] = result


def spread_kernel(in_ref, depth_ref, flow_ref, stored_ref):
    for slot, ref in enumerate((depth_ref, flow_ref, stored_ref)):
        for half in range(2):
            ref[:, half * LANES : (half + 1) * LANES] = in_ref[pl.ds(2 * slot + half, ROWS, stride=8)]


VMEM = pl.BlockSpec(memory_space=pltpu.VMEM)
HBM = pl.BlockSpec(memory_space=pltpu.HBM)


def call(kernel, name, in_specs, outs, scratch=(), aliases=None):
    return pl.pallas_call(
        kernel,
        name=name,
        in_specs=in_specs,
        out_specs=[VMEM] * len(outs),
        out_shape=[jax.ShapeDtypeStruct(shape, dtype) for shape, dtype in outs],
        scratch_shapes=list(scratch),
        input_output_aliases=aliases or {},
        compiler_params=pltpu.CompilerParams(vmem_limit_bytes=40 * 1024 * 1024),
    )


def local(
    surface, discharge, storage, exchange, depth_perturbation, flow_perturbation,
    sensor_cell, sensor_radius, observed, sensor_sigma,
):
    strips = lax.axis_size("strip")
    groups = lax.axis_size("dom")
    order = list(range(0, strips, 2)) + list(range(strips - 1, 0, -2))
    onward = [(order[i], order[(i + 1) % strips]) for i in range(strips)]
    backward = [(b, a) for a, b in onward]
    swapped = [(i, i ^ 1) for i in range(strips)]
    stay = lambda values: pltpu.with_memory_space_constraint(values, pltpu.HBM)
    as_row = lambda values: stay(values.reshape(1, SENS))
    fields = [stay(f) for f in (surface, discharge, storage, exchange, depth_perturbation, flow_perturbation)]
    grid = ((2, MEMBERS * ROWS, LANES), f32)
    message = (MESSAGE, LANES)
    edges = lambda count: ((2 * count * MEMBERS, LANES), f32)
    row_of = lambda dtype: pltpu.VMEM((1, SENS), dtype)
    own, along, across, far, extra, depth, flow, stored = call(
        forecast_kernel, "forecast", [HBM] * 12,
        [((2,) + message, f32), (message, f32), ((2,) + message, f32), edges(1), edges(7), grid, grid, grid],
        [pltpu.VMEM(field.shape, field.dtype) for field in fields]
        + [
            pltpu.VMEM((8, 2, MEMBERS * 8, LANES), f32), pltpu.VMEM((8, 2, MEMBERS * 8, LANES), f32),
            pltpu.VMEM((2, MEMBERS, LANES), f32), pltpu.SMEM((SENS,), jnp.int32), pltpu.SMEM((SENS,), jnp.int32),
            row_of(jnp.int32), row_of(jnp.int32),
            row_of(f32), row_of(f32), pltpu.SemaphoreType.DMA((14,)),
        ],
    )(
        stay(sensor_cell), stay(sensor_radius), as_row(sensor_cell), as_row(sensor_radius), as_row(observed),
        as_row(sensor_sigma), *fields,
    )
    arrived = lax.ppermute(along, "strip", backward)
    far = lax.ppermute(far, "strip", onward)
    (joined,) = call(join_kernel, "join", [VMEM] * 2, [((2,) + message, f32)], aliases={0: 0})(across, arrived)
    joined = lax.ppermute(joined, "strip", swapped)
    parts, depth, flow, stored = call(
        finish_kernel, "finish", [VMEM] * 8, [((groups * 8, LANES), f32), grid, grid, grid],
        [
            pltpu.VMEM(message, f32), pltpu.VMEM(message, f32), pltpu.VMEM((3, SENS, COLS), f32),
            pltpu.VMEM((ROWS, 6 * SENS, COLS), bf16), pltpu.VMEM((2, ROWS * MEMBERS, LANES), f32),
        ],
        aliases={5: 1, 6: 2, 7: 3},
    )(own, extra, arrived, far, joined, depth, flow, stored)
    shared = lax.all_to_all(parts.reshape(groups, 8, LANES), "dom", 0, 0, tiled=True)
    (rows,) = call(
        lambda *refs: combine_kernel(groups, *refs), "combine", [VMEM], [((groups * 8, LANES), f32)],
    )(shared.reshape(groups * 8, LANES))
    whole = lax.all_to_all(rows.reshape(groups, 8, LANES), "dom", 0, 0, tiled=True)
    return tuple(
        call(spread_kernel, "spread", [VMEM], [((ROWS, COLS), f32)] * 3)(whole.reshape(groups * 8, LANES))
    )


def solution(mesh):
    return jax.shard_map(
        local,
        mesh=mesh,
        in_specs=(
            P("dom", "strip", None),
            P("dom", "strip", None),
            P("dom", "strip", None),
            P("strip", None),
            P(None, "dom", "strip", None),
            P(None, "dom", "strip", None),
            P("strip"),
            P("strip"),
            P("strip"),
            P("strip"),
        ),
        out_specs=(P("strip", None), P("strip", None), P("strip", None)),
        check_vma=False,
    )
```

```python
import jax
import jax.numpy as jnp
from jax import lax
from jax.experimental import pallas as pl
from jax.experimental.pallas import tpu as pltpu
from jax.sharding import PartitionSpec as P

advection = 0.4
gravity = 0.5
diffusion = 0.15
friction = 0.3
drainage = 0.1

MEMBERS = 24
ROWS = 32
COLS = 256
SENS = 32
LANES = 128
SAMPLED = 6 * MEMBERS
SLOPE = SAMPLED + MEMBERS
ENTRY = SLOPE + MEMBERS
ACROSS = ENTRY + SENS
MESSAGE = ACROSS + 8

f32 = jnp.float32
bf16 = jnp.bfloat16


def sides(left_half, right_half):
    lane = lax.broadcasted_iota(jnp.int32, left_half.shape, 1)
    first, last = lane == 0, lane == LANES - 1
    left_back, right_back = pltpu.roll(left_half, 1, 1), pltpu.roll(right_half, 1, 1)
    left_on, right_on = pltpu.roll(left_half, LANES - 1, 1), pltpu.roll(right_half, LANES - 1, 1)
    return (
        jnp.where(first, left_half, left_back) + jnp.where(last, right_on, left_on),
        jnp.where(first, left_back, right_back) + jnp.where(last, right_half, right_on),
    )


def spread(field):
    return [diffusion * (around - 2.0 * here) for around, here in zip(sides(*field), field)]


def halves(values):
    return [values[:, :LANES], values[:, LANES:]]


def each(function, *rows):
    return [function(*parts) for parts in zip(*rows)]


def put(ref, slot, row):
    for h in range(2):
        ref[(2 * slot + h) * MEMBERS : (2 * slot + h + 1) * MEMBERS] = row[h]


def get(ref, slot):
    return [ref[(2 * slot + h) * MEMBERS : (2 * slot + h + 1) * MEMBERS] for h in range(2)]


def forecast_kernel(
    cell_hbm, radii_hbm, cells_hbm, radius_hbm, observed_hbm, sigma_hbm,
    surface_hbm, discharge_hbm, storage_hbm, exchange_hbm, depth_noise_hbm, flow_noise_hbm,
    own_ref, along_ref, across_ref, far_ref, extra_ref, depth_ref, flow_ref, stored_ref,
    surface_ref, discharge_ref, storage_ref, exchange_ref, depth_noise_ref, flow_noise_ref,
    first_ref, last_ref, slope_ref, cell_ref, radii_ref, cells_ref, radius_ref, observed_ref, sigma_ref, sems,
):
    pairs = [
        (surface_hbm, surface_ref), (discharge_hbm, discharge_ref), (storage_hbm, storage_ref),
        (depth_noise_hbm.at[0], depth_noise_ref.at[0]), (flow_noise_hbm.at[0], flow_noise_ref.at[0]),
        (depth_noise_hbm.at[1], depth_noise_ref.at[1]), (flow_noise_hbm.at[1], flow_noise_ref.at[1]),
        (exchange_hbm, exchange_ref), (cell_hbm, cell_ref), (radii_hbm, radii_ref), (cells_hbm, cells_ref), (radius_hbm, radius_ref),
        (observed_hbm, observed_ref), (sigma_hbm, sigma_ref),
    ]
    copies = [pltpu.make_async_copy(source, target, sems.at[i]) for i, (source, target) in enumerate(pairs)]
    for copy in copies:
        copy.start()

    def keep(scratch, slot, rows):
        flat = rows.reshape(MEMBERS * 8, COLS)
        scratch[slot, 0] = flat[:, :LANES]
        scratch[slot, 1] = flat[:, LANES:]

    def take(ref, lead, slot):
        copies[slot].wait()
        keep(first_ref, slot, ref[lead + (slice(None), slice(0, 16), slice(None))].astype(f32)[:, :8])
        if slot != 5:
            keep(last_ref, slot, ref[lead + (slice(None), slice(16, 32), slice(None))].astype(f32)[:, 8:])

    take(surface_ref, (), 0)
    take(discharge_ref, (), 1)
    take(storage_ref, (), 2)
    take(depth_noise_ref, (0,), 3)
    take(flow_noise_ref, (0,), 4)
    take(depth_noise_ref, (1,), 5)
    take(flow_noise_ref, (1,), 6)
    for copy in copies[7:]:
        copy.wait()

    def row_of(ref, slot, row):
        return [ref[slot, h, pl.ds(row, MEMBERS, stride=8)] for h in range(2)]

    def step_one(surface, flow, flow_below, stored, rate, noise):
        return each(
            lambda s, q, b, t, e, n, d: s - advection * (q - b) + d - e * (s - t) + n,
            surface, flow, flow_below, stored, rate, noise, spread(surface),
        )

    nothing = [jnp.zeros((MEMBERS, LANES), f32)] * 2
    rate = halves(exchange_ref[...].astype(f32))
    rate_0, rate_1, rate_31 = [[r[i : i + 1] for r in rate] for i in (0, 1, ROWS - 1)]
    surface_0, surface_1 = row_of(first_ref, 0, 0), row_of(first_ref, 0, 1)
    flow_0, flow_1 = row_of(first_ref, 1, 0), row_of(first_ref, 1, 1)
    stored_0, stored_1 = row_of(first_ref, 2, 0), row_of(first_ref, 2, 1)
    depth_0 = step_one(surface_0, flow_0, nothing, stored_0, rate_0, row_of(first_ref, 3, 0))
    depth_1 = step_one(surface_1, flow_1, flow_0, stored_1, rate_1, row_of(first_ref, 3, 1))
    stored_next = each(lambda s, t, e: (1.0 - drainage) * t + e * (s - t), surface_0, stored_0, rate_0)
    inverse_0 = each(lambda q: 1.0 / (1.0 + friction * jnp.abs(q)), flow_0)
    flow_part = each(
        lambda q, d, n, i: (q - gravity * d + n) * i, flow_0, depth_1, row_of(first_ref, 4, 0), inverse_0
    )
    up_ref, down_ref = own_ref.at[0], own_ref.at[1]
    put(up_ref, 0, depth_0)
    put(up_ref, 1, each(lambda e, i: 1.0 - e - (advection * gravity) * i, rate_0, inverse_0))
    put(up_ref, 2, each(lambda e, t, n, q: e * t + n - advection * q, rate_0, stored_next, row_of(first_ref, 5, 0), flow_part))
    flow_31 = row_of(last_ref, 1, 7)
    depth_31 = step_one(
        row_of(last_ref, 0, 7), flow_31, row_of(last_ref, 1, 6), row_of(last_ref, 2, 7), rate_31, row_of(last_ref, 3, 7)
    )
    inverse_31 = each(lambda q: 1.0 / (1.0 + friction * jnp.abs(q)), flow_31)
    put(down_ref, 0, flow_31)
    put(down_ref, 1, each(lambda q, d, n, i: (q + gravity * d + n) * i, flow_31, depth_31, row_of(last_ref, 4, 7), inverse_31))
    put(down_ref, 2, each(lambda i: gravity * i, inverse_31))
    put(far_ref, 0, flow_31)
    put(extra_ref, 0, each(lambda i: gravity * i, inverse_0))
    put(extra_ref, 1, each(lambda q, i, d: q + gravity * i * d, flow_part, inverse_0, depth_0))
    put(extra_ref, 2, row_of(first_ref, 6, 0))
    put(extra_ref, 3, row_of(last_ref, 6, 7))
    put(extra_ref, 6, each(lambda e, z: e + z, rate_0, nothing))
    for h in range(2):
        slope_ref[h] = (advection * advection * gravity) * inverse_0[h]

    row = lax.broadcasted_iota(jnp.int32, (ROWS, LANES), 0)

    def member(p, carry):
        depth, flow, stored = [halves(ref[p].astype(f32)) for ref in (surface_ref, discharge_ref, storage_ref)]
        for step in range(2):
            depth_noise, flow_noise = [halves(ref[step, p].astype(f32)) for ref in (depth_noise_ref, flow_noise_ref)]
            beside = sides(*depth)
            for h in range(2):
                flow_below = jnp.where(row == 0, 0.0, pltpu.roll(flow[h], 1, 0))
                inflow = rate[h] * (depth[h] - stored[h])
                depth_next = (
                    (1.0 - 2.0 * diffusion) * depth[h] + diffusion * beside[h]
                    - advection * (flow[h] - flow_below) - inflow + depth_noise[h]
                )
                stored[h] = (1.0 - drainage) * stored[h] + inflow
                depth_above = jnp.where(row == ROWS - 1, 0.0, pltpu.roll(depth_next, ROWS - 1, 0))
                flow[h] = (flow[h] - gravity * (depth_above - depth_next) + flow_noise[h]) * (
                    1.0 / (1.0 + friction * jnp.abs(flow[h]))
                )
                depth[h] = depth_next
                if step == 0:
                    edge = pl.ds(pl.multiple_of(p * 8, 8), 8)
                    first_ref[7, h, edge] = flow[h][:8]
                    last_ref[7, h, edge] = flow[h][ROWS - 8 :]
        at = pl.ds(pl.multiple_of(p * ROWS, ROWS), ROWS)
        for ref, value in ((depth_ref, depth), (flow_ref, flow), (stored_ref, stored)):
            for h in range(2):
                ref[h, at] = value[h]
        return carry

    lax.fori_loop(0, MEMBERS, member, 0, unroll=4)
    put(extra_ref, 4, each(lambda q: 1.0 / (1.0 + friction * jnp.abs(q)), row_of(first_ref, 7, 1)))
    put(extra_ref, 5, each(lambda q: 1.0 / (1.0 + friction * jnp.abs(q)), row_of(last_ref, 7, 6)))

    lane = lax.broadcasted_iota(jnp.int32, (MEMBERS, LANES), 1)
    one_lane = lax.broadcasted_iota(jnp.int32, (1, LANES), 1)
    sampled, slope = jnp.zeros((MEMBERS, LANES), f32), jnp.zeros((MEMBERS, LANES), f32)
    for k in range(SENS):
        cell = cell_ref[k]
        half, line, turn = (cell >> 7) & 1, (cell >> 8) & (ROWS - 1), (k - cell) & (LANES - 1)
        found = pltpu.roll(depth_ref[half, pl.ds(line, MEMBERS, stride=ROWS)], turn, 1)
        sampled = jnp.where(lane == k, found, sampled)
        slope = jnp.where(lane == k, pltpu.roll(slope_ref[half], turn, 1), slope)
        place, column = line.astype(f32), (cell & (COLS - 1)).astype(f32)
        strip = (cell >> 13).astype(f32)
        reach = radii_ref[k].astype(f32)
        entry = jnp.where(
            one_lane == 0, place, jnp.where(one_lane == 1, column, jnp.where(one_lane == 2, reach * reach, strip))
        )
        for i in range(2):
            own_ref[i, ENTRY + k : ENTRY + k + 1] = entry
    cells = cells_ref[...]
    place = ((cells >> 8) & (ROWS - 1)).astype(f32)
    reach = radius_ref[...].astype(f32)
    facts = [
        place, (cells & (COLS - 1)).astype(f32), reach * reach, (cells >> 13).astype(f32),
        observed_ref[...], sigma_ref[...], jnp.zeros((2, SENS), f32),
    ]
    facts = jnp.concatenate([jnp.concatenate(facts, axis=0), jnp.ones((8, LANES - SENS), f32)], axis=1)
    slope = jnp.where(facts[0:1] == 1.0, slope, 0.0)
    for i in range(2):
        own_ref[i, SAMPLED:SLOPE] = sampled
        own_ref[i, SLOPE:ENTRY] = slope
        own_ref[i, ACROSS:MESSAGE] = facts
    odd = (cell_ref[0] >> 13) & 1
    along_ref[...] = own_ref[odd]
    across_ref[0] = own_ref[1 - odd]


def join_kernel(across_ref, arrived_ref, far_ref, joined_ref):
    del across_ref, far_ref
    joined_ref[1] = arrived_ref[...]


def taper_rows(messages, offsets, strip, near_ref, taper_ref):
    count = len(messages)
    column_at = lax.broadcasted_iota(jnp.int32, (SENS, COLS), 1).astype(f32)
    lines = []
    for part, (message, offset) in enumerate(zip(messages, offsets)):
        entry = message[ENTRY:ACROSS]
        gap = column_at - entry[:, 1:2]
        squared = jnp.where(entry[:, 3:4] == strip + offset, entry[:, 2:3], 0.0)
        near_ref[part] = squared - gap * gap
        lines.append(jnp.broadcast_to(entry[:, 0:1] + offset * ROWS, (SENS, LANES)))

    def at_row(r, carry):
        here = r.astype(f32)
        for part in range(count):
            gap = here - lines[part]
            gap = gap * gap
            value = jnp.maximum(near_ref[part] - jnp.concatenate([gap, gap], axis=1), 0.0)
            coarse = value.astype(bf16)
            taper_ref[r, part * SENS : (part + 1) * SENS] = coarse
            taper_ref[r, (count + part) * SENS : (count + part + 1) * SENS] = (value - coarse.astype(f32)).astype(bf16)
        return carry

    lax.fori_loop(0, ROWS, at_row, 0, unroll=4 // count)


def taper_kernel(own_ref, tapers_ref, near_ref):
    taper_rows([own_ref.at[0]], [0.0], own_ref[0, ACROSS + 3 : ACROSS + 4, 0:1], near_ref, tapers_ref)


def finish_kernel(
    own_ref, tapers_ref, extra_ref, arrived_ref, far_ref, joined_ref, depth_in, flow_in, stored_in,
    out_ref, depth_ref, flow_ref, stored_ref,
    before_ref, after_ref, near_ref, taper_ref, weight_ref,
):
    del depth_in, flow_in, stored_in
    up_ref, down_ref = own_ref.at[0], own_ref.at[1]
    strip = own_ref[0, ACROSS + 3 : ACROSS + 4, 0:1]
    odd = strip - 2.0 * jnp.floor(0.5 * strip) > 0.5
    before_ref[...] = jnp.where(odd, joined_ref[0], joined_ref[1])
    after_ref[...] = jnp.where(odd, joined_ref[1], joined_ref[0])
    has_before = before_ref[ACROSS + 3 : ACROSS + 4, 0:1] == strip - 1.0
    has_after = after_ref[ACROSS + 3 : ACROSS + 4, 0:1] == strip + 1.0
    keep = lambda condition, row: each(lambda v: jnp.where(condition, v, 0.0), row)

    def line(ref, row):
        return [ref[h, pl.ds(row, MEMBERS, stride=ROWS)] for h in range(2)]

    def set_line(ref, row, values):
        for h in range(2):
            ref[h, pl.ds(row, MEMBERS, stride=ROWS)] = values[h]

    back = keep(has_before, get(before_ref, 0))
    start = each(lambda d, q: d + advection * q, get(up_ref, 0), back)
    back_next = keep(has_before, each(lambda f, i, d: f - i * d, get(before_ref, 1), get(before_ref, 2), start))
    depth_0 = each(
        lambda d, c, s, k, q: d * c + s + k + advection * q,
        start, get(up_ref, 1), spread(start), get(up_ref, 2), back_next,
    )
    turn_0 = get(extra_ref, 0)
    more_1 = each(lambda i, q: (advection * advection) * i * q, turn_0, back)
    depth_1 = each(lambda d, m: d + m, line(depth_ref, 1), more_1)
    flow_0 = each(lambda f, i, q: f + advection * i * q, get(extra_ref, 1), turn_0, back)
    set_line(depth_ref, 0, depth_0)
    set_line(depth_ref, 1, depth_1)
    set_line(flow_ref, 0, each(
        lambda f, a, d, n: (f - gravity * (a - d) + n) * (1.0 / (1.0 + friction * jnp.abs(f))),
        flow_0, depth_1, depth_0, get(extra_ref, 2),
    ))
    set_line(flow_ref, 1, each(lambda f, i, m: f + gravity * i * m, line(flow_ref, 1), get(extra_ref, 4), more_1))
    set_line(stored_ref, 0, each(lambda t, e, q: t + advection * e * q, line(stored_ref, 0), get(extra_ref, 6), back))
    last = get(down_ref, 0)
    end = keep(has_after, each(lambda d, q: d + advection * q, get(after_ref, 0), last))
    flow_31 = each(lambda f, i, d: f - i * d, get(down_ref, 1), get(down_ref, 2), end)
    depth_32 = keep(has_after, each(
        lambda d, c, s, k, q: d * c + s + k + advection * q,
        end, get(after_ref, 1), spread(end), get(after_ref, 2), flow_31,
    ))
    more_31 = each(lambda i, d: advection * i * d, get(down_ref, 2), end)
    depth_31 = each(lambda d, m: d + m, line(depth_ref, ROWS - 1), more_31)
    set_line(depth_ref, ROWS - 1, depth_31)
    set_line(flow_ref, ROWS - 1, each(
        lambda f, a, d, n: (f - gravity * (a - d) + n) * (1.0 / (1.0 + friction * jnp.abs(f))),
        flow_31, depth_32, depth_31, get(extra_ref, 3),
    ))
    set_line(flow_ref, ROWS - 2, each(
        lambda f, i, m: f - gravity * i * m, line(flow_ref, ROWS - 2), get(extra_ref, 5), more_31
    ))

    lane = lax.broadcasted_iota(jnp.int32, (1, LANES), 1)
    group = lane // SENS

    def beside(ref, first, count):
        parts = (ref[0, first : first + count], before_ref[first : first + count], after_ref[first : first + count])
        parts = [parts[0], pltpu.roll(parts[1], SENS, 1), pltpu.roll(parts[2], 2 * SENS, 1)]
        return jnp.where(group == 0, parts[0], jnp.where(group == 1, parts[1], parts[2]))

    facts = beside(own_ref, ACROSS, 8)
    place, column = facts[0:1], facts[1:2]
    hit = (lax.broadcasted_iota(jnp.int32, (COLS, LANES), 0).astype(f32) == column).astype(f32)

    def sample(rows):
        left, right = [], []
        for values, wanted, in_group, pieces in rows:
            values = jnp.concatenate(values, axis=1)
            stack = []
            for _ in range(pieces):
                piece = values.astype(bf16).astype(f32)
                stack.append(piece)
                values = values - piece
            left.append(jnp.concatenate(stack, axis=0).astype(bf16))
            right.append(jnp.where((place == wanted) & (group == in_group), hit, 0.0).astype(bf16))
        total = jnp.dot(jnp.concatenate(left, axis=1), jnp.concatenate(right, axis=0), preferred_element_type=f32)
        return sum(total[i * MEMBERS : (i + 1) * MEMBERS] for i in range(1, pieces)) + total[:MEMBERS] if pieces > 1 else total

    far = each(lambda a, b: jnp.where(strip > 1.5, jnp.where(odd, a, b), 0.0), get(arrived_ref, 0), get(far_ref, 0))
    added = sample([
        (each(lambda i, d: advection * i * d, keep(has_before, get(before_ref, 2)), start), ROWS - 1.0, 1, 3),
        (depth_0, 0.0, 0, 3), (more_1, 1.0, 0, 3), (more_31, ROWS - 1.0, 0, 3),
        (depth_32, 0.0, 2, 3),
    ])
    beyond = sample([(far, 1.0, 1, 1), (last, 1.0, 2, 1)])
    known = jnp.where((place == 0.0) & (group != 1), 0.0, beside(own_ref, SAMPLED, MEMBERS))
    found = known + added + beside(own_ref, SLOPE, MEMBERS) * beyond
    real = group < 3
    misfit = (found - facts[4:5]) / jnp.where(real, facts[5:6], 1.0)
    lik = jnp.where(real, -0.5 * misfit * misfit / jnp.where(real, facts[2:3], 1.0), 0.0)
    stack = []
    rest = lik
    for _ in range(3):
        piece = rest.astype(bf16).astype(f32)
        stack.append(piece)
        rest = rest - piece
    pieces = jnp.concatenate(stack, axis=0)
    pieces = jnp.concatenate(
        [jnp.where(group == 0, pieces, pltpu.roll(pieces, SENS, 1)), pltpu.roll(pieces, LANES - SENS, 1)], axis=1
    )[:, : 6 * SENS].astype(bf16)

    taper_rows([before_ref, after_ref], [-1.0, 1.0], strip, near_ref, taper_ref)
    for i in range(ROWS // 8):
        for r in range(8 * i, 8 * i + 8):
            tapers = jnp.concatenate([tapers_ref[r], taper_ref[r]], axis=0)
            part = jnp.dot(pieces, tapers, preferred_element_type=f32)
            weight = part[:MEMBERS] + part[MEMBERS : 2 * MEMBERS] + part[2 * MEMBERS :]
            for half in range(2):
                weight_ref[half, r * MEMBERS : (r + 1) * MEMBERS] = weight[:, half * LANES : (half + 1) * LANES]
        for half in range(2):
            weights = [weight_ref[half, pl.ds(8 * i * MEMBERS + p, 8, stride=MEMBERS)] for p in range(MEMBERS)]
            best = weights[0]
            for p in range(1, MEMBERS):
                best = jnp.maximum(best, weights[p])
            sums = [jnp.zeros((8, LANES), f32) for _ in range(4)]
            for p in range(MEMBERS):
                factor = jnp.exp(weights[p] - best)
                at = pl.ds(p * ROWS + 8 * i, 8)
                sums[0] = sums[0] + factor
                sums[1] = sums[1] + factor * depth_ref[half, at]
                sums[2] = sums[2] + factor * flow_ref[half, at]
                sums[3] = sums[3] + factor * stored_ref[half, at]
            inverse = 1.0 / sums[0]
            results = (best + jnp.log(sums[0]), sums[1] * inverse, sums[2] * inverse, sums[3] * inverse)
            for slot, result in enumerate(results):
                out_ref[pl.ds(64 * i + 2 * slot + half, 8, stride=8)] = result


def combine_kernel(groups, in_ref, out_ref):
    def quantity(slot, half):
        return in_ref[pl.ds(2 * slot + half, groups, stride=8)]

    rows = []
    totals = []
    for half in range(2):
        level = quantity(0, half)
        share = jnp.exp(level - jnp.max(level, axis=0, keepdims=True))
        totals.append((share, 1.0 / jnp.sum(share, axis=0, keepdims=True)))
    for slot in range(1, 4):
        for half in range(2):
            share, inverse = totals[half]
            rows.append(jnp.sum(share * quantity(slot, half), axis=0, keepdims=True) * inverse)
    rows.append(jnp.zeros((2, LANES), f32))
    result = jnp.concatenate(rows, axis=0)
    for copy in range(groups):
        out_ref[copy * 8 : (copy + 1) * 8] = result


def spread_kernel(in_ref, depth_ref, flow_ref, stored_ref):
    for slot, ref in enumerate((depth_ref, flow_ref, stored_ref)):
        for half in range(2):
            ref[:, half * LANES : (half + 1) * LANES] = in_ref[pl.ds(2 * slot + half, ROWS, stride=8)]


VMEM = pl.BlockSpec(memory_space=pltpu.VMEM)
HBM = pl.BlockSpec(memory_space=pltpu.HBM)


def call(kernel, name, in_specs, outs, scratch=(), aliases=None):
    return pl.pallas_call(
        kernel,
        name=name,
        in_specs=in_specs,
        out_specs=[VMEM] * len(outs),
        out_shape=[jax.ShapeDtypeStruct(shape, dtype) for shape, dtype in outs],
        scratch_shapes=list(scratch),
        input_output_aliases=aliases or {},
        compiler_params=pltpu.CompilerParams(vmem_limit_bytes=40 * 1024 * 1024),
    )


def local(
    surface, discharge, storage, exchange, depth_perturbation, flow_perturbation,
    sensor_cell, sensor_radius, observed, sensor_sigma,
):
    strips = lax.axis_size("strip")
    groups = lax.axis_size("dom")
    order = list(range(0, strips, 2)) + list(range(strips - 1, 0, -2))
    onward = [(order[i], order[(i + 1) % strips]) for i in range(strips)]
    backward = [(b, a) for a, b in onward]
    swapped = [(i, i ^ 1) for i in range(strips)]
    stay = lambda values: pltpu.with_memory_space_constraint(values, pltpu.HBM)
    as_row = lambda values: stay(values.reshape(1, SENS))
    fields = [stay(f) for f in (surface, discharge, storage, exchange, depth_perturbation, flow_perturbation)]
    grid = ((2, MEMBERS * ROWS, LANES), f32)
    message = (MESSAGE, LANES)
    edges = lambda count: ((2 * count * MEMBERS, LANES), f32)
    row_of = lambda dtype: pltpu.VMEM((1, SENS), dtype)
    own, along, across, far, extra, depth, flow, stored = call(
        forecast_kernel, "forecast", [HBM] * 12,
        [((2,) + message, f32), (message, f32), ((2,) + message, f32), edges(1), edges(7), grid, grid, grid],
        [pltpu.VMEM(field.shape, field.dtype) for field in fields]
        + [
            pltpu.VMEM((8, 2, MEMBERS * 8, LANES), f32), pltpu.VMEM((8, 2, MEMBERS * 8, LANES), f32),
            pltpu.VMEM((2, MEMBERS, LANES), f32), pltpu.SMEM((SENS,), jnp.int32), pltpu.SMEM((SENS,), jnp.int32),
            row_of(jnp.int32), row_of(jnp.int32),
            row_of(f32), row_of(f32), pltpu.SemaphoreType.DMA((14,)),
        ],
    )(
        stay(sensor_cell), stay(sensor_radius), as_row(sensor_cell), as_row(sensor_radius), as_row(observed),
        as_row(sensor_sigma), *fields,
    )
    arrived = lax.ppermute(along, "strip", backward)
    far = lax.ppermute(far, "strip", onward)
    (joined,) = call(join_kernel, "join", [VMEM] * 3, [((2,) + message, f32)], aliases={0: 0})(across, arrived, far)
    joined = lax.ppermute(joined, "strip", swapped)
    (tapers,) = call(
        taper_kernel, "taper", [VMEM], [((ROWS, 2 * SENS, COLS), bf16)], [pltpu.VMEM((1, SENS, COLS), f32)],
    )(own)
    parts, depth, flow, stored = call(
        finish_kernel, "finish", [VMEM] * 9, [((groups * 8, LANES), f32), grid, grid, grid],
        [
            pltpu.VMEM(message, f32), pltpu.VMEM(message, f32), pltpu.VMEM((2, SENS, COLS), f32),
            pltpu.VMEM((ROWS, 4 * SENS, COLS), bf16), pltpu.VMEM((2, ROWS * MEMBERS, LANES), f32),
        ],
        aliases={6: 1, 7: 2, 8: 3},
    )(own, tapers, extra, arrived, far, joined, depth, flow, stored)
    shared = lax.all_to_all(parts.reshape(groups, 8, LANES), "dom", 0, 0, tiled=True)
    (rows,) = call(
        lambda *refs: combine_kernel(groups, *refs), "combine", [VMEM], [((groups * 8, LANES), f32)],
    )(shared.reshape(groups * 8, LANES))
    whole = lax.all_to_all(rows.reshape(groups, 8, LANES), "dom", 0, 0, tiled=True)
    return tuple(
        call(spread_kernel, "spread", [VMEM], [((ROWS, COLS), f32)] * 3)(whole.reshape(groups * 8, LANES))
    )


def solution(mesh):
    return jax.shard_map(
        local,
        mesh=mesh,
        in_specs=(
            P("dom", "strip", None),
            P("dom", "strip", None),
            P("dom", "strip", None),
            P("strip", None),
            P(None, "dom", "strip", None),
            P(None, "dom", "strip", None),
            P("strip"),
            P("strip"),
            P("strip"),
            P("strip"),
        ),
        out_specs=(P("strip", None), P("strip", None), P("strip", None)),
        check_vma=False,
    )
```

```python
import jax
import jax.numpy as jnp
from jax import lax
from jax.experimental import pallas as pl
from jax.experimental.pallas import tpu as pltpu
from jax.sharding import PartitionSpec as P

advection = 0.4
gravity = 0.5
diffusion = 0.15
friction = 0.3
drainage = 0.1

MEMBERS = 24
ROWS = 32
COLS = 256
SENS = 32
LANES = 128
CHUNK = 8
SAMPLED = 6 * MEMBERS
ACROSS = SAMPLED + MEMBERS
MESSAGE = ACROSS + 8

f32 = jnp.float32
bf16 = jnp.bfloat16


def sides(left_half, right_half):
    lane = lax.broadcasted_iota(jnp.int32, left_half.shape, 1)
    first, last = lane == 0, lane == LANES - 1
    left_back, right_back = pltpu.roll(left_half, 1, 1), pltpu.roll(right_half, 1, 1)
    left_on, right_on = pltpu.roll(left_half, LANES - 1, 1), pltpu.roll(right_half, LANES - 1, 1)
    return (
        jnp.where(first, left_half, left_back) + jnp.where(last, right_on, left_on),
        jnp.where(first, left_back, right_back) + jnp.where(last, right_half, right_on),
    )


def spread(field):
    return [diffusion * (around - 2.0 * here) for around, here in zip(sides(*field), field)]


def halves(values):
    return [values[:, :LANES], values[:, LANES:]]


def each(function, *rows):
    return [function(*parts) for parts in zip(*rows)]


def put(ref, slot, row):
    for h in range(2):
        ref[(2 * slot + h) * MEMBERS : (2 * slot + h + 1) * MEMBERS] = row[h]


def get(ref, slot):
    return [ref[(2 * slot + h) * MEMBERS : (2 * slot + h + 1) * MEMBERS] for h in range(2)]


def split(values, pieces):
    stack = []
    for _ in range(pieces):
        piece = values.astype(bf16).astype(f32)
        stack.append(piece)
        values = values - piece
    return jnp.concatenate(stack, axis=0)


def exact_product(rows, marks, pieces):
    left = jnp.concatenate([split(values, pieces) for values in rows], axis=1).astype(bf16)
    right = jnp.concatenate(marks, axis=0).astype(bf16)
    total = jnp.dot(left, right, preferred_element_type=f32)
    parts = [total[i * MEMBERS : (i + 1) * MEMBERS] for i in range(pieces)]
    return sum(parts[1:], parts[0])


def forecast_kernel(
    cell_hbm, cells_hbm, radius_hbm, observed_hbm, sigma_hbm,
    surface_hbm, discharge_hbm, storage_hbm, exchange_hbm, depth_noise_hbm, flow_noise_hbm,
    own_ref, along_ref, across_ref, far_ref, extra_ref, depth_ref, flow_ref, stored_ref,
    surface_ref, discharge_ref, storage_ref, exchange_ref, depth_noise_ref, flow_noise_ref,
    first_ref, last_ref, cell_ref, cells_ref, radius_ref, observed_ref, sigma_ref, sems,
):
    chunks = []
    for c in range(MEMBERS // CHUNK):
        some = pl.ds(c * CHUNK, CHUNK)
        pairs = [
            (ref.at[some], to.at[some])
            for ref, to in ((surface_hbm, surface_ref), (discharge_hbm, discharge_ref), (storage_hbm, storage_ref))
        ] + [
            (ref.at[:, some], to.at[:, some])
            for ref, to in ((depth_noise_hbm, depth_noise_ref), (flow_noise_hbm, flow_noise_ref))
        ]
        if c == 0:
            pairs.append((exchange_hbm, exchange_ref))
        chunks.append(pairs)
    chunks.append([
        (cell_hbm, cell_ref), (cells_hbm, cells_ref), (radius_hbm, radius_ref), (observed_hbm, observed_ref),
        (sigma_hbm, sigma_ref),
    ])
    copies, used = [], 0
    for pairs in chunks:
        copies.append([])
        for source, target in pairs:
            copies[-1].append(pltpu.make_async_copy(source, target, sems.at[used]))
            copies[-1][-1].start()
            used += 1

    row = lax.broadcasted_iota(jnp.int32, (ROWS, LANES), 0)

    def member(p, carry):
        edge = pl.ds(pl.multiple_of(p * 8, 8), 8)

        def keep(slot, value):
            for h in range(2):
                first_ref[slot, h, edge] = value[h][:8]
                if slot != 5:
                    last_ref[slot, h, edge] = value[h][ROWS - 8 :]

        depth, flow, stored = [halves(ref[p].astype(f32)) for ref in (surface_ref, discharge_ref, storage_ref)]
        keep(0, depth)
        keep(1, flow)
        keep(2, stored)
        for step in range(2):
            depth_noise, flow_noise = [halves(ref[step, p].astype(f32)) for ref in (depth_noise_ref, flow_noise_ref)]
            keep(3 + 2 * step, depth_noise)
            keep(4 + 2 * step, flow_noise)
            beside = sides(*depth)
            for h in range(2):
                flow_below = jnp.where(row == 0, 0.0, pltpu.roll(flow[h], 1, 0))
                inflow = rate[h] * (depth[h] - stored[h])
                depth_next = (
                    (1.0 - 2.0 * diffusion) * depth[h] + diffusion * beside[h]
                    - advection * (flow[h] - flow_below) - inflow + depth_noise[h]
                )
                stored[h] = (1.0 - drainage) * stored[h] + inflow
                depth_above = jnp.where(row == ROWS - 1, 0.0, pltpu.roll(depth_next, ROWS - 1, 0))
                flow[h] = (flow[h] - gravity * (depth_above - depth_next) + flow_noise[h]) * (
                    1.0 / (1.0 + friction * jnp.abs(flow[h]))
                )
                depth[h] = depth_next
            if step == 0:
                keep(7, flow)
        at = pl.ds(pl.multiple_of(p * ROWS, ROWS), ROWS)
        for ref, value in ((depth_ref, depth), (flow_ref, flow), (stored_ref, stored)):
            for h in range(2):
                ref[h, at] = value[h]
        return carry

    for c in range(MEMBERS // CHUNK):
        for copy in copies[c]:
            copy.wait()
        if c == 0:
            rate = halves(exchange_ref[...].astype(f32))
        lax.fori_loop(c * CHUNK, (c + 1) * CHUNK, member, 0, unroll=4)

    def row_of(ref, slot, row):
        return [ref[slot, h, pl.ds(row, MEMBERS, stride=8)] for h in range(2)]

    def step_one(surface, flow, flow_below, stored, rate, noise):
        return each(
            lambda s, q, b, t, e, n, d: s - advection * (q - b) + d - e * (s - t) + n,
            surface, flow, flow_below, stored, rate, noise, spread(surface),
        )

    nothing = [jnp.zeros((MEMBERS, LANES), f32)] * 2
    rate_0, rate_1, rate_31 = [[r[i : i + 1] for r in rate] for i in (0, 1, ROWS - 1)]
    surface_0, surface_1 = row_of(first_ref, 0, 0), row_of(first_ref, 0, 1)
    flow_0, flow_1 = row_of(first_ref, 1, 0), row_of(first_ref, 1, 1)
    stored_0, stored_1 = row_of(first_ref, 2, 0), row_of(first_ref, 2, 1)
    depth_0 = step_one(surface_0, flow_0, nothing, stored_0, rate_0, row_of(first_ref, 3, 0))
    depth_1 = step_one(surface_1, flow_1, flow_0, stored_1, rate_1, row_of(first_ref, 3, 1))
    stored_next = each(lambda s, t, e: (1.0 - drainage) * t + e * (s - t), surface_0, stored_0, rate_0)
    inverse_0 = each(lambda q: 1.0 / (1.0 + friction * jnp.abs(q)), flow_0)
    flow_part = each(
        lambda q, d, n, i: (q - gravity * d + n) * i, flow_0, depth_1, row_of(first_ref, 4, 0), inverse_0
    )
    up_ref, down_ref = own_ref.at[0], own_ref.at[1]
    put(up_ref, 0, depth_0)
    put(up_ref, 1, each(lambda e, i: 1.0 - e - (advection * gravity) * i, rate_0, inverse_0))
    put(up_ref, 2, each(lambda e, t, n, q: e * t + n - advection * q, rate_0, stored_next, row_of(first_ref, 5, 0), flow_part))
    flow_31 = row_of(last_ref, 1, 7)
    depth_31 = step_one(
        row_of(last_ref, 0, 7), flow_31, row_of(last_ref, 1, 6), row_of(last_ref, 2, 7), rate_31, row_of(last_ref, 3, 7)
    )
    inverse_31 = each(lambda q: 1.0 / (1.0 + friction * jnp.abs(q)), flow_31)
    put(down_ref, 0, flow_31)
    put(down_ref, 1, each(lambda q, d, n, i: (q + gravity * d + n) * i, flow_31, depth_31, row_of(last_ref, 4, 7), inverse_31))
    put(down_ref, 2, each(lambda i: gravity * i, inverse_31))
    put(far_ref, 0, flow_31)
    put(extra_ref, 0, each(lambda i: gravity * i, inverse_0))
    put(extra_ref, 1, each(lambda q, i, d: q + gravity * i * d, flow_part, inverse_0, depth_0))
    put(extra_ref, 2, row_of(first_ref, 6, 0))
    put(extra_ref, 3, row_of(last_ref, 6, 7))
    put(extra_ref, 6, each(lambda e, z: e + z, rate_0, nothing))
    put(extra_ref, 4, each(lambda q: 1.0 / (1.0 + friction * jnp.abs(q)), row_of(first_ref, 7, 1)))
    put(extra_ref, 5, each(lambda q: 1.0 / (1.0 + friction * jnp.abs(q)), row_of(last_ref, 7, 6)))

    for copy in copies[-1]:
        copy.wait()
    cells = cells_ref[...]
    reach = radius_ref[...].astype(f32)
    facts = [
        ((cells >> 8) & (ROWS - 1)).astype(f32), (cells & (COLS - 1)).astype(f32), reach * reach,
        (cells >> 13).astype(f32), observed_ref[...], sigma_ref[...], jnp.zeros((2, SENS), f32),
    ]
    facts = jnp.concatenate([jnp.concatenate(facts, axis=0), jnp.ones((8, LANES - SENS), f32)], axis=1)
    lane = lax.broadcasted_iota(jnp.int32, (MEMBERS, LANES), 1)
    hit = lax.broadcasted_iota(jnp.int32, (COLS, LANES), 0).astype(f32) == facts[1:2]
    slope = exact_product(
        [jnp.concatenate(each(lambda i: (advection * advection * gravity) * i, inverse_0), axis=1)],
        [jnp.where((facts[0:1] == 1.0) & (lane[0:1] < SENS), hit.astype(f32), 0.0)], 3,
    )
    sampled = pltpu.roll(slope, SENS, 1)
    for k in range(SENS):
        cell = cell_ref[k]
        found = depth_ref[(cell >> 7) & 1, pl.ds((cell >> 8) & (ROWS - 1), MEMBERS, stride=ROWS)]
        sampled = jnp.where(lane == k, pltpu.roll(found, (k - cell) & (LANES - 1), 1), sampled)
    for i in range(2):
        own_ref[i, SAMPLED:ACROSS] = sampled
        own_ref[i, ACROSS:MESSAGE] = facts
    odd = (cell_ref[0] >> 13) & 1
    along_ref[...] = own_ref[odd]
    across_ref[0] = own_ref[1 - odd]


def join_kernel(across_ref, arrived_ref, far_ref, joined_ref):
    del across_ref, far_ref
    joined_ref[1] = arrived_ref[...]


def taper_rows(facts, at, offsets, strip, near_ref, taper_ref):
    count = len(offsets)
    entries = jnp.transpose(facts)
    column_at = lax.broadcasted_iota(jnp.int32, (SENS, COLS), 1).astype(f32)
    lines = []
    for part, offset in enumerate(offsets):
        entry = entries[at + part * SENS : at + (part + 1) * SENS]
        gap = column_at - entry[:, 1:2]
        squared = jnp.where(entry[:, 3:4] == strip + offset, entry[:, 2:3], 0.0)
        near_ref[part] = squared - gap * gap
        lines.append(jnp.broadcast_to(entry[:, 0:1] + offset * ROWS, (SENS, LANES)))

    def at_row(r, carry):
        here = r.astype(f32)
        for part in range(count):
            gap = here - lines[part]
            gap = gap * gap
            value = jnp.maximum(near_ref[part] - jnp.concatenate([gap, gap], axis=1), 0.0)
            coarse = value.astype(bf16)
            taper_ref[r, part * SENS : (part + 1) * SENS] = coarse
            taper_ref[r, (count + part) * SENS : (count + part + 1) * SENS] = (value - coarse.astype(f32)).astype(bf16)
        return carry

    lax.fori_loop(0, ROWS, at_row, 0, unroll=4 // count)


def taper_kernel(own_ref, tapers_ref, near_ref):
    facts = own_ref[0, ACROSS:MESSAGE]
    taper_rows(facts, 0, [0.0], facts[3:4, 0:1], near_ref, tapers_ref)


def finish_kernel(
    own_ref, tapers_ref, extra_ref, arrived_ref, far_ref, joined_ref, depth_in, flow_in, stored_in,
    out_ref, depth_ref, flow_ref, stored_ref,
    before_ref, after_ref, near_ref, taper_ref, weight_ref,
):
    del depth_in, flow_in, stored_in
    up_ref, down_ref = own_ref.at[0], own_ref.at[1]
    strip = own_ref[0, ACROSS + 3 : ACROSS + 4, 0:1]
    odd = strip - 2.0 * jnp.floor(0.5 * strip) > 0.5
    before_ref[...] = jnp.where(odd, joined_ref[0], joined_ref[1])
    after_ref[...] = jnp.where(odd, joined_ref[1], joined_ref[0])
    has_before = before_ref[ACROSS + 3 : ACROSS + 4, 0:1] == strip - 1.0
    has_after = after_ref[ACROSS + 3 : ACROSS + 4, 0:1] == strip + 1.0
    keep = lambda condition, row: each(lambda v: jnp.where(condition, v, 0.0), row)

    def line(ref, row):
        return [ref[h, pl.ds(row, MEMBERS, stride=ROWS)] for h in range(2)]

    def set_line(ref, row, values):
        for h in range(2):
            ref[h, pl.ds(row, MEMBERS, stride=ROWS)] = values[h]

    back = keep(has_before, get(before_ref, 0))
    start = each(lambda d, q: d + advection * q, get(up_ref, 0), back)
    back_next = keep(has_before, each(lambda f, i, d: f - i * d, get(before_ref, 1), get(before_ref, 2), start))
    depth_0 = each(
        lambda d, c, s, k, q: d * c + s + k + advection * q,
        start, get(up_ref, 1), spread(start), get(up_ref, 2), back_next,
    )
    turn_0 = get(extra_ref, 0)
    more_1 = each(lambda i, q: (advection * advection) * i * q, turn_0, back)
    depth_1 = each(lambda d, m: d + m, line(depth_ref, 1), more_1)
    flow_0 = each(lambda f, i, q: f + advection * i * q, get(extra_ref, 1), turn_0, back)
    set_line(depth_ref, 0, depth_0)
    set_line(depth_ref, 1, depth_1)
    set_line(flow_ref, 0, each(
        lambda f, a, d, n: (f - gravity * (a - d) + n) * (1.0 / (1.0 + friction * jnp.abs(f))),
        flow_0, depth_1, depth_0, get(extra_ref, 2),
    ))
    set_line(flow_ref, 1, each(lambda f, i, m: f + gravity * i * m, line(flow_ref, 1), get(extra_ref, 4), more_1))
    set_line(stored_ref, 0, each(lambda t, e, q: t + advection * e * q, line(stored_ref, 0), get(extra_ref, 6), back))
    last = get(down_ref, 0)
    end = keep(has_after, each(lambda d, q: d + advection * q, get(after_ref, 0), last))
    flow_31 = each(lambda f, i, d: f - i * d, get(down_ref, 1), get(down_ref, 2), end)
    depth_32 = keep(has_after, each(
        lambda d, c, s, k, q: d * c + s + k + advection * q,
        end, get(after_ref, 1), spread(end), get(after_ref, 2), flow_31,
    ))
    more_31 = each(lambda i, d: advection * i * d, get(down_ref, 2), end)
    depth_31 = each(lambda d, m: d + m, line(depth_ref, ROWS - 1), more_31)
    set_line(depth_ref, ROWS - 1, depth_31)
    set_line(flow_ref, ROWS - 1, each(
        lambda f, a, d, n: (f - gravity * (a - d) + n) * (1.0 / (1.0 + friction * jnp.abs(f))),
        flow_31, depth_32, depth_31, get(extra_ref, 3),
    ))
    set_line(flow_ref, ROWS - 2, each(
        lambda f, i, m: f - gravity * i * m, line(flow_ref, ROWS - 2), get(extra_ref, 5), more_31
    ))

    lane = lax.broadcasted_iota(jnp.int32, (1, LANES), 1)
    group = lane // SENS

    def beside(first, end, shift=0):
        parts = (own_ref[0, first:end], before_ref[first:end], after_ref[first:end])
        parts = [pltpu.roll(part, (i * SENS - shift) % LANES, 1) for i, part in enumerate(parts)]
        return jnp.where(group == 0, parts[0], jnp.where(group == 1, parts[1], parts[2]))

    facts = beside(ACROSS, MESSAGE)
    place = facts[0:1]
    hit = (lax.broadcasted_iota(jnp.int32, (COLS, LANES), 0).astype(f32) == facts[1:2]).astype(f32)

    def sample(rows, pieces):
        marks = [jnp.where((place == wanted) & (group == of), hit, 0.0) for _, wanted, of in rows]
        return exact_product([jnp.concatenate(values, axis=1) for values, _, _ in rows], marks, pieces)

    far = each(lambda a, b: jnp.where(strip > 1.5, jnp.where(odd, a, b), 0.0), get(arrived_ref, 0), get(far_ref, 0))
    added = sample([
        (each(lambda i, d: advection * i * d, keep(has_before, get(before_ref, 2)), start), ROWS - 1.0, 1),
        (depth_0, 0.0, 0), (more_1, 1.0, 0), (more_31, ROWS - 1.0, 0),
        (depth_32, 0.0, 2),
    ], 3)
    beyond = sample([(far, 1.0, 1), (last, 1.0, 2)], 1)
    known = jnp.where((place == 0.0) & (group != 1), 0.0, beside(SAMPLED, ACROSS))
    found = known + added + beside(SAMPLED, ACROSS, SENS) * beyond
    real = group < 3
    misfit = (found - facts[4:5]) / jnp.where(real, facts[5:6], 1.0)
    lik = jnp.where(real, -0.5 * misfit * misfit / jnp.where(real, facts[2:3], 1.0), 0.0)
    pieces = split(lik, 3)
    pieces = jnp.concatenate(
        [jnp.where(group == 0, pieces, pltpu.roll(pieces, SENS, 1)), pltpu.roll(pieces, LANES - SENS, 1)], axis=1
    )[:, : 6 * SENS].astype(bf16)

    taper_rows(facts, SENS, [-1.0, 1.0], strip, near_ref, taper_ref)
    for i in range(ROWS // 8):
        for r in range(8 * i, 8 * i + 8):
            tapers = jnp.concatenate([tapers_ref[r], taper_ref[r]], axis=0)
            part = jnp.dot(pieces, tapers, preferred_element_type=f32)
            weight = part[:MEMBERS] + part[MEMBERS : 2 * MEMBERS] + part[2 * MEMBERS :]
            for half in range(2):
                weight_ref[half, r * MEMBERS : (r + 1) * MEMBERS] = weight[:, half * LANES : (half + 1) * LANES]
        for half in range(2):
            weights = [weight_ref[half, pl.ds(8 * i * MEMBERS + p, 8, stride=MEMBERS)] for p in range(MEMBERS)]
            best = weights[0]
            for p in range(1, MEMBERS):
                best = jnp.maximum(best, weights[p])
            sums = [jnp.zeros((8, LANES), f32) for _ in range(4)]
            for p in range(MEMBERS):
                factor = jnp.exp(weights[p] - best)
                at = pl.ds(p * ROWS + 8 * i, 8)
                sums[0] = sums[0] + factor
                sums[1] = sums[1] + factor * depth_ref[half, at]
                sums[2] = sums[2] + factor * flow_ref[half, at]
                sums[3] = sums[3] + factor * stored_ref[half, at]
            inverse = 1.0 / sums[0]
            results = (best + jnp.log(sums[0]), sums[1] * inverse, sums[2] * inverse, sums[3] * inverse)
            for slot, result in enumerate(results):
                out_ref[pl.ds(64 * i + 2 * slot + half, 8, stride=8)] = result


def combine_kernel(groups, in_ref, out_ref):
    def quantity(slot, half):
        return in_ref[pl.ds(2 * slot + half, groups, stride=8)]

    rows = []
    totals = []
    for half in range(2):
        level = quantity(0, half)
        share = jnp.exp(level - jnp.max(level, axis=0, keepdims=True))
        totals.append((share, 1.0 / jnp.sum(share, axis=0, keepdims=True)))
    for slot in range(1, 4):
        for half in range(2):
            share, inverse = totals[half]
            rows.append(jnp.sum(share * quantity(slot, half), axis=0, keepdims=True) * inverse)
    rows.append(jnp.zeros((2, LANES), f32))
    result = jnp.concatenate(rows, axis=0)
    for copy in range(groups):
        out_ref[copy * 8 : (copy + 1) * 8] = result


def spread_kernel(in_ref, depth_ref, flow_ref, stored_ref):
    for slot, ref in enumerate((depth_ref, flow_ref, stored_ref)):
        for half in range(2):
            ref[:, half * LANES : (half + 1) * LANES] = in_ref[pl.ds(2 * slot + half, ROWS, stride=8)]


VMEM = pl.BlockSpec(memory_space=pltpu.VMEM)
HBM = pl.BlockSpec(memory_space=pltpu.HBM)


def call(kernel, name, in_specs, outs, scratch=(), aliases=None):
    return pl.pallas_call(
        kernel,
        name=name,
        in_specs=in_specs,
        out_specs=[VMEM] * len(outs),
        out_shape=[jax.ShapeDtypeStruct(shape, dtype) for shape, dtype in outs],
        scratch_shapes=list(scratch),
        input_output_aliases=aliases or {},
        compiler_params=pltpu.CompilerParams(vmem_limit_bytes=40 * 1024 * 1024),
    )


def local(
    surface, discharge, storage, exchange, depth_perturbation, flow_perturbation,
    sensor_cell, sensor_radius, observed, sensor_sigma,
):
    strips = lax.axis_size("strip")
    groups = lax.axis_size("dom")
    order = list(range(0, strips, 2)) + list(range(strips - 1, 0, -2))
    onward = [(order[i], order[(i + 1) % strips]) for i in range(strips)]
    backward = [(b, a) for a, b in onward]
    swapped = [(i, i ^ 1) for i in range(strips)]
    stay = lambda values: pltpu.with_memory_space_constraint(values, pltpu.HBM)
    as_row = lambda values: stay(values.reshape(1, SENS))
    fields = [stay(f) for f in (surface, discharge, storage, exchange, depth_perturbation, flow_perturbation)]
    grid = ((2, MEMBERS * ROWS, LANES), f32)
    message = (MESSAGE, LANES)
    edges = lambda count: ((2 * count * MEMBERS, LANES), f32)
    row_of = lambda dtype: pltpu.VMEM((1, SENS), dtype)
    own, along, across, far, extra, depth, flow, stored = call(
        forecast_kernel, "forecast", [HBM] * 11,
        [((2,) + message, f32), (message, f32), ((2,) + message, f32), edges(1), edges(7), grid, grid, grid],
        [pltpu.VMEM(field.shape, field.dtype) for field in fields]
        + [
            pltpu.VMEM((8, 2, MEMBERS * 8, LANES), f32), pltpu.VMEM((8, 2, MEMBERS * 8, LANES), f32),
            pltpu.SMEM((SENS,), jnp.int32), row_of(jnp.int32), row_of(jnp.int32), row_of(f32), row_of(f32),
            pltpu.SemaphoreType.DMA((21,)),
        ],
    )(stay(sensor_cell), as_row(sensor_cell), as_row(sensor_radius), as_row(observed), as_row(sensor_sigma), *fields)
    arrived = lax.ppermute(along, "strip", backward)
    far = lax.ppermute(far, "strip", onward)
    (joined,) = call(join_kernel, "join", [VMEM] * 3, [((2,) + message, f32)], aliases={0: 0})(across, arrived, far)
    joined = lax.ppermute(joined, "strip", swapped)
    (tapers,) = call(
        taper_kernel, "taper", [VMEM], [((ROWS, 2 * SENS, COLS), bf16)], [pltpu.VMEM((1, SENS, COLS), f32)],
    )(own)
    parts, depth, flow, stored = call(
        finish_kernel, "finish", [VMEM] * 9, [((groups * 8, LANES), f32), grid, grid, grid],
        [
            pltpu.VMEM(message, f32), pltpu.VMEM(message, f32), pltpu.VMEM((2, SENS, COLS), f32),
            pltpu.VMEM((ROWS, 4 * SENS, COLS), bf16), pltpu.VMEM((2, ROWS * MEMBERS, LANES), f32),
        ],
        aliases={6: 1, 7: 2, 8: 3},
    )(own, tapers, extra, arrived, far, joined, depth, flow, stored)
    shared = lax.all_to_all(parts.reshape(groups, 8, LANES), "dom", 0, 0, tiled=True)
    (rows,) = call(
        lambda *refs: combine_kernel(groups, *refs), "combine", [VMEM], [((groups * 8, LANES), f32)],
    )(shared.reshape(groups * 8, LANES))
    whole = lax.all_to_all(rows.reshape(groups, 8, LANES), "dom", 0, 0, tiled=True)
    return tuple(
        call(spread_kernel, "spread", [VMEM], [((ROWS, COLS), f32)] * 3)(whole.reshape(groups * 8, LANES))
    )


def solution(mesh):
    return jax.shard_map(
        local,
        mesh=mesh,
        in_specs=(
            P("dom", "strip", None),
            P("dom", "strip", None),
            P("dom", "strip", None),
            P("strip", None),
            P(None, "dom", "strip", None),
            P(None, "dom", "strip", None),
            P("strip"),
            P("strip"),
            P("strip"),
            P("strip"),
        ),
        out_specs=(P("strip", None), P("strip", None), P("strip", None)),
        check_vma=False,
    )
```

```python
import jax
import jax.numpy as jnp
from jax import lax
from jax.experimental import pallas as pl
from jax.experimental.pallas import tpu as pltpu
from jax.sharding import PartitionSpec as P

advection = 0.4
gravity = 0.5
diffusion = 0.15
friction = 0.3
drainage = 0.1

MEMBERS = 24
ROWS = 32
COLS = 256
SENS = 32
LANES = 128
CHUNK = 8
PITCH = 40
SAMPLED = 6 * MEMBERS
ACROSS = SAMPLED + MEMBERS
MESSAGE = ACROSS + 8

f32 = jnp.float32
bf16 = jnp.bfloat16


def sides(left_half, right_half):
    lane = lax.broadcasted_iota(jnp.int32, left_half.shape, 1)
    first, last = lane == 0, lane == LANES - 1
    left_back, right_back = pltpu.roll(left_half, 1, 1), pltpu.roll(right_half, 1, 1)
    left_on, right_on = pltpu.roll(left_half, LANES - 1, 1), pltpu.roll(right_half, LANES - 1, 1)
    return (
        jnp.where(first, left_half, left_back) + jnp.where(last, right_on, left_on),
        jnp.where(first, left_back, right_back) + jnp.where(last, right_half, right_on),
    )


def spread(field):
    return [diffusion * (around - 2.0 * here) for around, here in zip(sides(*field), field)]


def halves(values):
    return [values[:, :LANES], values[:, LANES:]]


def each(function, *rows):
    return [function(*parts) for parts in zip(*rows)]


def put(ref, slot, row):
    for h in range(2):
        ref[(2 * slot + h) * MEMBERS : (2 * slot + h + 1) * MEMBERS] = row[h]


def get(ref, slot):
    return [ref[(2 * slot + h) * MEMBERS : (2 * slot + h + 1) * MEMBERS] for h in range(2)]


def split(values, pieces):
    stack = []
    for _ in range(pieces):
        piece = values.astype(bf16).astype(f32)
        stack.append(piece)
        values = values - piece
    return jnp.concatenate(stack, axis=0)


def pick(rows, hit):
    left = jnp.concatenate([split(jnp.concatenate(values, axis=1), pieces) for values, pieces in rows], axis=0)
    total = jnp.dot(left.astype(bf16), hit, preferred_element_type=f32)
    found, at = [], 0
    for _, pieces in rows:
        parts = [total[at + i * MEMBERS : at + (i + 1) * MEMBERS] for i in range(pieces)]
        found.append(sum(parts[1:], parts[0]))
        at += pieces * MEMBERS
    return found


def forecast_kernel(
    cell_hbm, cells_hbm, radius_hbm, observed_hbm, sigma_hbm,
    surface_hbm, discharge_hbm, storage_hbm, exchange_hbm, depth_noise_hbm, flow_noise_hbm,
    own_ref, along_ref, across_ref, far_ref, extra_ref, depth_ref, flow_ref, stored_ref,
    surface_ref, discharge_ref, storage_ref, exchange_ref, depth_noise_ref, flow_noise_ref,
    first_ref, last_ref, cell_ref, cells_ref, radius_ref, observed_ref, sigma_ref, sems,
):
    chunks = []
    for c in range(MEMBERS // CHUNK):
        some = pl.ds(c * CHUNK, CHUNK)
        pairs = [
            (ref.at[some], to.at[some])
            for ref, to in ((surface_hbm, surface_ref), (discharge_hbm, discharge_ref), (storage_hbm, storage_ref))
        ] + [
            (ref.at[:, some], to.at[:, some])
            for ref, to in ((depth_noise_hbm, depth_noise_ref), (flow_noise_hbm, flow_noise_ref))
        ]
        if c == 0:
            pairs.append((exchange_hbm, exchange_ref))
        chunks.append(pairs)
    chunks.append([
        (cell_hbm, cell_ref), (cells_hbm, cells_ref), (radius_hbm, radius_ref), (observed_hbm, observed_ref),
        (sigma_hbm, sigma_ref),
    ])
    copies, used = [], 0
    for pairs in chunks:
        copies.append([])
        for source, target in pairs:
            copies[-1].append(pltpu.make_async_copy(source, target, sems.at[used]))
            copies[-1][-1].start()
            used += 1

    row = lax.broadcasted_iota(jnp.int32, (ROWS, LANES), 0)

    def member(p, carry):
        edge = pl.ds(pl.multiple_of(p * 8, 8), 8)

        def keep(slot, value):
            for h in range(2):
                first_ref[slot, h, edge] = value[h][:8]
                if slot != 5:
                    last_ref[slot, h, edge] = value[h][ROWS - 8 :]

        depth, flow, stored = [halves(ref[p].astype(f32)) for ref in (surface_ref, discharge_ref, storage_ref)]
        keep(0, depth)
        keep(1, flow)
        keep(2, stored)
        for step in range(2):
            depth_noise, flow_noise = [halves(ref[step, p].astype(f32)) for ref in (depth_noise_ref, flow_noise_ref)]
            keep(3 + 2 * step, depth_noise)
            keep(4 + 2 * step, flow_noise)
            beside = sides(*depth)
            for h in range(2):
                flow_below = jnp.where(row == 0, 0.0, pltpu.roll(flow[h], 1, 0))
                inflow = rate[h] * (depth[h] - stored[h])
                depth_next = (
                    (1.0 - 2.0 * diffusion) * depth[h] + diffusion * beside[h]
                    - advection * (flow[h] - flow_below) - inflow + depth_noise[h]
                )
                stored[h] = (1.0 - drainage) * stored[h] + inflow
                depth_above = jnp.where(row == ROWS - 1, 0.0, pltpu.roll(depth_next, ROWS - 1, 0))
                flow[h] = (flow[h] - gravity * (depth_above - depth_next) + flow_noise[h]) * (
                    1.0 / (1.0 + friction * jnp.abs(flow[h]))
                )
                depth[h] = depth_next
            if step == 0:
                keep(7, flow)
        at = pl.ds(pl.multiple_of(p * PITCH, 8), ROWS)
        for ref, value in ((depth_ref, depth), (flow_ref, flow), (stored_ref, stored)):
            for h in range(2):
                ref[h, at] = value[h]
        return carry

    for c in range(MEMBERS // CHUNK):
        for copy in copies[c]:
            copy.wait()
        if c == 0:
            rate = halves(exchange_ref[...].astype(f32))
        lax.fori_loop(c * CHUNK, (c + 1) * CHUNK, member, 0, unroll=4)

    def row_of(ref, slot, row):
        return [ref[slot, h, pl.ds(row, MEMBERS, stride=8)] for h in range(2)]

    def step_one(surface, flow, flow_below, stored, rate, noise):
        return each(
            lambda s, q, b, t, e, n, d: s - advection * (q - b) + d - e * (s - t) + n,
            surface, flow, flow_below, stored, rate, noise, spread(surface),
        )

    nothing = [jnp.zeros((MEMBERS, LANES), f32)] * 2
    rate_0, rate_1, rate_31 = [[r[i : i + 1] for r in rate] for i in (0, 1, ROWS - 1)]
    surface_0, surface_1 = row_of(first_ref, 0, 0), row_of(first_ref, 0, 1)
    flow_0, flow_1 = row_of(first_ref, 1, 0), row_of(first_ref, 1, 1)
    stored_0, stored_1 = row_of(first_ref, 2, 0), row_of(first_ref, 2, 1)
    depth_0 = step_one(surface_0, flow_0, nothing, stored_0, rate_0, row_of(first_ref, 3, 0))
    depth_1 = step_one(surface_1, flow_1, flow_0, stored_1, rate_1, row_of(first_ref, 3, 1))
    stored_next = each(lambda s, t, e: (1.0 - drainage) * t + e * (s - t), surface_0, stored_0, rate_0)
    inverse_0 = each(lambda q: 1.0 / (1.0 + friction * jnp.abs(q)), flow_0)
    flow_part = each(
        lambda q, d, n, i: (q - gravity * d + n) * i, flow_0, depth_1, row_of(first_ref, 4, 0), inverse_0
    )
    up_ref, down_ref = own_ref.at[0], own_ref.at[1]
    put(up_ref, 0, depth_0)
    put(up_ref, 1, each(lambda e, i: 1.0 - e - (advection * gravity) * i, rate_0, inverse_0))
    put(up_ref, 2, each(lambda e, t, n, q: e * t + n - advection * q, rate_0, stored_next, row_of(first_ref, 5, 0), flow_part))
    flow_31 = row_of(last_ref, 1, 7)
    depth_31 = step_one(
        row_of(last_ref, 0, 7), flow_31, row_of(last_ref, 1, 6), row_of(last_ref, 2, 7), rate_31, row_of(last_ref, 3, 7)
    )
    inverse_31 = each(lambda q: 1.0 / (1.0 + friction * jnp.abs(q)), flow_31)
    put(down_ref, 0, flow_31)
    put(down_ref, 1, each(lambda q, d, n, i: (q + gravity * d + n) * i, flow_31, depth_31, row_of(last_ref, 4, 7), inverse_31))
    put(down_ref, 2, each(lambda i: gravity * i, inverse_31))
    put(far_ref, 0, flow_31)
    put(extra_ref, 0, each(lambda i: gravity * i, inverse_0))
    put(extra_ref, 1, each(lambda q, i, d: q + gravity * i * d, flow_part, inverse_0, depth_0))
    put(extra_ref, 2, row_of(first_ref, 6, 0))
    put(extra_ref, 3, row_of(last_ref, 6, 7))
    put(extra_ref, 6, each(lambda e, z: e + z, rate_0, nothing))
    put(extra_ref, 4, each(lambda q: 1.0 / (1.0 + friction * jnp.abs(q)), row_of(first_ref, 7, 1)))
    put(extra_ref, 5, each(lambda q: 1.0 / (1.0 + friction * jnp.abs(q)), row_of(last_ref, 7, 6)))

    for copy in copies[-1]:
        copy.wait()
    cells = cells_ref[...]
    reach = radius_ref[...].astype(f32)
    facts = [
        ((cells >> 8) & (ROWS - 1)).astype(f32), (cells & (COLS - 1)).astype(f32), reach * reach,
        (cells >> 13).astype(f32), observed_ref[...], sigma_ref[...], jnp.zeros((2, SENS), f32),
    ]
    facts = jnp.concatenate([jnp.concatenate(facts, axis=0), jnp.ones((8, LANES - SENS), f32)], axis=1)
    lane = lax.broadcasted_iota(jnp.int32, (MEMBERS, LANES), 1)
    hit = (lax.broadcasted_iota(jnp.int32, (COLS, LANES), 0).astype(f32) == facts[1:2]).astype(f32).astype(bf16)
    (slope,) = pick([(each(lambda i: (advection * advection * gravity) * i, inverse_0), 3)], hit)
    sampled = pltpu.roll(jnp.where((facts[0:1] == 1.0) & (lane < SENS), slope, 0.0), SENS, 1)
    for k in range(SENS):
        cell = cell_ref[k]
        found = depth_ref[(cell >> 7) & 1, pl.ds((cell >> 8) & (ROWS - 1), MEMBERS, stride=PITCH)]
        sampled = jnp.where(lane == k, pltpu.roll(found, (k - cell) & (LANES - 1), 1), sampled)
    for i in range(2):
        own_ref[i, SAMPLED:ACROSS] = sampled
        own_ref[i, ACROSS:MESSAGE] = facts
    odd = (cell_ref[0] >> 13) & 1
    along_ref[...] = own_ref[odd]
    across_ref[0] = own_ref[1 - odd]


def join_kernel(across_ref, arrived_ref, far_ref, joined_ref):
    del across_ref, far_ref
    joined_ref[1] = arrived_ref[...]


def taper_rows(facts, at, offsets, strip, near_ref, taper_ref):
    count = len(offsets)
    entries = jnp.transpose(facts)
    column_at = lax.broadcasted_iota(jnp.int32, (SENS, COLS), 1).astype(f32)
    lines = []
    for part, offset in enumerate(offsets):
        entry = entries[at + part * SENS : at + (part + 1) * SENS]
        gap = column_at - entry[:, 1:2]
        squared = jnp.where(entry[:, 3:4] == strip + offset, entry[:, 2:3], 0.0)
        near_ref[part] = squared - gap * gap
        lines.append(jnp.broadcast_to(entry[:, 0:1] + offset * ROWS, (SENS, LANES)))

    def at_row(r, carry):
        here = r.astype(f32)
        for part in range(count):
            gap = here - lines[part]
            gap = gap * gap
            value = jnp.maximum(near_ref[part] - jnp.concatenate([gap, gap], axis=1), 0.0)
            coarse = value.astype(bf16)
            taper_ref[r, part * SENS : (part + 1) * SENS] = coarse
            taper_ref[r, (count + part) * SENS : (count + part + 1) * SENS] = (value - coarse.astype(f32)).astype(bf16)
        return carry

    lax.fori_loop(0, ROWS, at_row, 0, unroll=4 // count)


def taper_kernel(own_ref, tapers_ref, near_ref):
    facts = own_ref[0, ACROSS:MESSAGE]
    taper_rows(facts, 0, [0.0], facts[3:4, 0:1], near_ref, tapers_ref)


def finish_kernel(
    own_ref, tapers_ref, extra_ref, arrived_ref, far_ref, joined_ref, depth_in, flow_in, stored_in,
    out_ref, depth_ref, flow_ref, stored_ref,
    before_ref, after_ref, near_ref, taper_ref, weight_ref,
):
    del depth_in, flow_in, stored_in
    up_ref, down_ref = own_ref.at[0], own_ref.at[1]
    strip = own_ref[0, ACROSS + 3 : ACROSS + 4, 0:1]
    odd = strip - 2.0 * jnp.floor(0.5 * strip) > 0.5
    before_ref[...] = jnp.where(odd, joined_ref[0], joined_ref[1])
    after_ref[...] = jnp.where(odd, joined_ref[1], joined_ref[0])
    has_before = before_ref[ACROSS + 3 : ACROSS + 4, 0:1] == strip - 1.0
    has_after = after_ref[ACROSS + 3 : ACROSS + 4, 0:1] == strip + 1.0
    keep = lambda condition, row: each(lambda v: jnp.where(condition, v, 0.0), row)

    def line(ref, row):
        return [ref[h, pl.ds(row, MEMBERS, stride=PITCH)] for h in range(2)]

    def set_line(ref, row, values):
        for h in range(2):
            ref[h, pl.ds(row, MEMBERS, stride=PITCH)] = values[h]

    back = keep(has_before, get(before_ref, 0))
    start = each(lambda d, q: d + advection * q, get(up_ref, 0), back)
    back_next = keep(has_before, each(lambda f, i, d: f - i * d, get(before_ref, 1), get(before_ref, 2), start))
    depth_0 = each(
        lambda d, c, s, k, q: d * c + s + k + advection * q,
        start, get(up_ref, 1), spread(start), get(up_ref, 2), back_next,
    )
    turn_0 = get(extra_ref, 0)
    more_1 = each(lambda i, q: (advection * advection) * i * q, turn_0, back)
    depth_1 = each(lambda d, m: d + m, line(depth_ref, 1), more_1)
    flow_0 = each(lambda f, i, q: f + advection * i * q, get(extra_ref, 1), turn_0, back)
    set_line(depth_ref, 0, depth_0)
    set_line(depth_ref, 1, depth_1)
    set_line(flow_ref, 0, each(
        lambda f, a, d, n: (f - gravity * (a - d) + n) * (1.0 / (1.0 + friction * jnp.abs(f))),
        flow_0, depth_1, depth_0, get(extra_ref, 2),
    ))
    set_line(flow_ref, 1, each(lambda f, i, m: f + gravity * i * m, line(flow_ref, 1), get(extra_ref, 4), more_1))
    set_line(stored_ref, 0, each(lambda t, e, q: t + advection * e * q, line(stored_ref, 0), get(extra_ref, 6), back))
    last = get(down_ref, 0)
    end = keep(has_after, each(lambda d, q: d + advection * q, get(after_ref, 0), last))
    flow_31 = each(lambda f, i, d: f - i * d, get(down_ref, 1), get(down_ref, 2), end)
    depth_32 = keep(has_after, each(
        lambda d, c, s, k, q: d * c + s + k + advection * q,
        end, get(after_ref, 1), spread(end), get(after_ref, 2), flow_31,
    ))
    more_31 = each(lambda i, d: advection * i * d, get(down_ref, 2), end)
    depth_31 = each(lambda d, m: d + m, line(depth_ref, ROWS - 1), more_31)
    set_line(depth_ref, ROWS - 1, depth_31)
    set_line(flow_ref, ROWS - 1, each(
        lambda f, a, d, n: (f - gravity * (a - d) + n) * (1.0 / (1.0 + friction * jnp.abs(f))),
        flow_31, depth_32, depth_31, get(extra_ref, 3),
    ))
    set_line(flow_ref, ROWS - 2, each(
        lambda f, i, m: f - gravity * i * m, line(flow_ref, ROWS - 2), get(extra_ref, 5), more_31
    ))

    lane = lax.broadcasted_iota(jnp.int32, (1, LANES), 1)
    group = lane // SENS

    def beside(first, end, shift=0):
        parts = (own_ref[0, first:end], before_ref[first:end], after_ref[first:end])
        parts = [pltpu.roll(part, (i * SENS - shift) % LANES, 1) for i, part in enumerate(parts)]
        return jnp.where(group == 0, parts[0], jnp.where(group == 1, parts[1], parts[2]))

    facts = beside(ACROSS, MESSAGE)
    place = facts[0:1]
    hit = (lax.broadcasted_iota(jnp.int32, (COLS, LANES), 0).astype(f32) == facts[1:2]).astype(f32).astype(bf16)

    far = each(lambda a, b: jnp.where(strip > 1.5, jnp.where(odd, a, b), 0.0), get(arrived_ref, 0), get(far_ref, 0))
    beyond_31 = each(lambda i, d: advection * i * d, keep(has_before, get(before_ref, 2)), start)
    wanted = [
        (beyond_31, 3, ROWS - 1.0, 1), (depth_0, 3, 0.0, 0), (more_1, 3, 1.0, 0), (more_31, 3, ROWS - 1.0, 0),
        (depth_32, 3, 0.0, 2), (far, 1, 1.0, 1), (last, 1, 1.0, 2),
    ]
    found = pick([(values, pieces) for values, pieces, _, _ in wanted], hit)
    found = [jnp.where((place == row) & (group == of), value, 0.0) for value, (_, _, row, of) in zip(found, wanted)]
    added, beyond = sum(found[1:5], found[0]), found[5] + found[6]
    known = jnp.where((place == 0.0) & (group != 1), 0.0, beside(SAMPLED, ACROSS))
    found = known + added + beside(SAMPLED, ACROSS, SENS) * beyond
    real = group < 3
    misfit = (found - facts[4:5]) / jnp.where(real, facts[5:6], 1.0)
    lik = jnp.where(real, -0.5 * misfit * misfit / jnp.where(real, facts[2:3], 1.0), 0.0)
    pieces = split(lik, 3)
    pieces = jnp.concatenate(
        [jnp.where(group == 0, pieces, pltpu.roll(pieces, SENS, 1)), pltpu.roll(pieces, LANES - SENS, 1)], axis=1
    )[:, : 6 * SENS].astype(bf16)

    taper_rows(facts, SENS, [-1.0, 1.0], strip, near_ref, taper_ref)
    for i in range(ROWS // 8):
        for r in range(8 * i, 8 * i + 8):
            tapers = jnp.concatenate([tapers_ref[r], taper_ref[r]], axis=0)
            part = jnp.dot(pieces, tapers, preferred_element_type=f32)
            weight = part[:MEMBERS] + part[MEMBERS : 2 * MEMBERS] + part[2 * MEMBERS :]
            for half in range(2):
                weight_ref[half, r * MEMBERS : (r + 1) * MEMBERS] = weight[:, half * LANES : (half + 1) * LANES]
        for half in range(2):
            weights = [weight_ref[half, pl.ds(8 * i * MEMBERS + p, 8, stride=MEMBERS)] for p in range(MEMBERS)]
            best = weights[0]
            for p in range(1, MEMBERS):
                best = jnp.maximum(best, weights[p])
            sums = [jnp.zeros((8, LANES), f32) for _ in range(4)]
            for p in range(MEMBERS):
                factor = jnp.exp(weights[p] - best)
                at = pl.ds(p * PITCH + 8 * i, 8)
                sums[0] = sums[0] + factor
                sums[1] = sums[1] + factor * depth_ref[half, at]
                sums[2] = sums[2] + factor * flow_ref[half, at]
                sums[3] = sums[3] + factor * stored_ref[half, at]
            inverse = 1.0 / sums[0]
            results = (best + jnp.log(sums[0]), sums[1] * inverse, sums[2] * inverse, sums[3] * inverse)
            for slot, result in enumerate(results):
                out_ref[pl.ds(64 * i + 2 * slot + half, 8, stride=8)] = result


def combine_kernel(groups, in_ref, out_ref):
    def quantity(slot, half):
        return in_ref[pl.ds(2 * slot + half, groups, stride=8)]

    rows = []
    totals = []
    for half in range(2):
        level = quantity(0, half)
        share = jnp.exp(level - jnp.max(level, axis=0, keepdims=True))
        totals.append((share, 1.0 / jnp.sum(share, axis=0, keepdims=True)))
    for slot in range(1, 4):
        for half in range(2):
            share, inverse = totals[half]
            rows.append(jnp.sum(share * quantity(slot, half), axis=0, keepdims=True) * inverse)
    rows.append(jnp.zeros((2, LANES), f32))
    result = jnp.concatenate(rows, axis=0)
    for copy in range(groups):
        out_ref[copy * 8 : (copy + 1) * 8] = result


def spread_kernel(in_ref, depth_ref, flow_ref, stored_ref):
    for slot, ref in enumerate((depth_ref, flow_ref, stored_ref)):
        for half in range(2):
            ref[:, half * LANES : (half + 1) * LANES] = in_ref[pl.ds(2 * slot + half, ROWS, stride=8)]


VMEM = pl.BlockSpec(memory_space=pltpu.VMEM)
HBM = pl.BlockSpec(memory_space=pltpu.HBM)


def call(kernel, name, in_specs, outs, scratch=(), aliases=None):
    return pl.pallas_call(
        kernel,
        name=name,
        in_specs=in_specs,
        out_specs=[VMEM] * len(outs),
        out_shape=[jax.ShapeDtypeStruct(shape, dtype) for shape, dtype in outs],
        scratch_shapes=list(scratch),
        input_output_aliases=aliases or {},
        compiler_params=pltpu.CompilerParams(vmem_limit_bytes=40 * 1024 * 1024),
    )


def local(
    surface, discharge, storage, exchange, depth_perturbation, flow_perturbation,
    sensor_cell, sensor_radius, observed, sensor_sigma,
):
    strips = lax.axis_size("strip")
    groups = lax.axis_size("dom")
    order = list(range(0, strips, 2)) + list(range(strips - 1, 0, -2))
    onward = [(order[i], order[(i + 1) % strips]) for i in range(strips)]
    backward = [(b, a) for a, b in onward]
    swapped = [(i, i ^ 1) for i in range(strips)]
    stay = lambda values: pltpu.with_memory_space_constraint(values, pltpu.HBM)
    as_row = lambda values: stay(values.reshape(1, SENS))
    fields = [stay(f) for f in (surface, discharge, storage, exchange, depth_perturbation, flow_perturbation)]
    grid = ((2, MEMBERS * PITCH, LANES), f32)
    message = (MESSAGE, LANES)
    edges = lambda count: ((2 * count * MEMBERS, LANES), f32)
    row_of = lambda dtype: pltpu.VMEM((1, SENS), dtype)
    own, along, across, far, extra, depth, flow, stored = call(
        forecast_kernel, "forecast", [HBM] * 11,
        [((2,) + message, f32), (message, f32), ((2,) + message, f32), edges(1), edges(7), grid, grid, grid],
        [pltpu.VMEM(field.shape, field.dtype) for field in fields]
        + [
            pltpu.VMEM((8, 2, MEMBERS * 8, LANES), f32), pltpu.VMEM((8, 2, MEMBERS * 8, LANES), f32),
            pltpu.SMEM((SENS,), jnp.int32), row_of(jnp.int32), row_of(jnp.int32), row_of(f32), row_of(f32),
            pltpu.SemaphoreType.DMA((21,)),
        ],
    )(stay(sensor_cell), as_row(sensor_cell), as_row(sensor_radius), as_row(observed), as_row(sensor_sigma), *fields)
    arrived = lax.ppermute(along, "strip", backward)
    far = lax.ppermute(far, "strip", onward)
    (joined,) = call(join_kernel, "join", [VMEM] * 3, [((2,) + message, f32)], aliases={0: 0})(across, arrived, far)
    joined = lax.ppermute(joined, "strip", swapped)
    (tapers,) = call(
        taper_kernel, "taper", [VMEM], [((ROWS, 2 * SENS, COLS), bf16)], [pltpu.VMEM((1, SENS, COLS), f32)],
    )(own)
    parts, depth, flow, stored = call(
        finish_kernel, "finish", [VMEM] * 9, [((groups * 8, LANES), f32), grid, grid, grid],
        [
            pltpu.VMEM(message, f32), pltpu.VMEM(message, f32), pltpu.VMEM((2, SENS, COLS), f32),
            pltpu.VMEM((ROWS, 4 * SENS, COLS), bf16), pltpu.VMEM((2, ROWS * MEMBERS, LANES), f32),
        ],
        aliases={6: 1, 7: 2, 8: 3},
    )(own, tapers, extra, arrived, far, joined, depth, flow, stored)
    shared = lax.all_to_all(parts.reshape(groups, 8, LANES), "dom", 0, 0, tiled=True)
    (rows,) = call(
        lambda *refs: combine_kernel(groups, *refs), "combine", [VMEM], [((groups * 8, LANES), f32)],
    )(shared.reshape(groups * 8, LANES))
    whole = lax.all_to_all(rows.reshape(groups, 8, LANES), "dom", 0, 0, tiled=True)
    return tuple(
        call(spread_kernel, "spread", [VMEM], [((ROWS, COLS), f32)] * 3)(whole.reshape(groups * 8, LANES))
    )


def solution(mesh):
    return jax.shard_map(
        local,
        mesh=mesh,
        in_specs=(
            P("dom", "strip", None),
            P("dom", "strip", None),
            P("dom", "strip", None),
            P("strip", None),
            P(None, "dom", "strip", None),
            P(None, "dom", "strip", None),
            P("strip"),
            P("strip"),
            P("strip"),
            P("strip"),
        ),
        out_specs=(P("strip", None), P("strip", None), P("strip", None)),
        check_vma=False,
    )
```

```python
import jax
import jax.numpy as jnp
from jax import lax
from jax.experimental import pallas as pl
from jax.experimental.pallas import tpu as pltpu
from jax.sharding import PartitionSpec as P

advection = 0.4
gravity = 0.5
diffusion = 0.15
friction = 0.3
drainage = 0.1

MEMBERS = 24
ROWS = 32
COLS = 256
SENS = 32
LANES = 128
CHUNK = 8
PITCH = 40
SAMPLED = 6 * MEMBERS
ACROSS = SAMPLED + MEMBERS
MESSAGE = ACROSS + 8

f32 = jnp.float32
bf16 = jnp.bfloat16


def sides(left_half, right_half):
    lane = lax.broadcasted_iota(jnp.int32, left_half.shape, 1)
    first, last = lane == 0, lane == LANES - 1
    left_back, right_back = pltpu.roll(left_half, 1, 1), pltpu.roll(right_half, 1, 1)
    left_on, right_on = pltpu.roll(left_half, LANES - 1, 1), pltpu.roll(right_half, LANES - 1, 1)
    return (
        jnp.where(first, left_half, left_back) + jnp.where(last, right_on, left_on),
        jnp.where(first, left_back, right_back) + jnp.where(last, right_half, right_on),
    )


def spread(field):
    return [diffusion * (around - 2.0 * here) for around, here in zip(sides(*field), field)]


def halves(values):
    return [values[:, :LANES], values[:, LANES:]]


def each(function, *rows):
    return [function(*parts) for parts in zip(*rows)]


def put(ref, slot, row):
    for h in range(2):
        ref[(2 * slot + h) * MEMBERS : (2 * slot + h + 1) * MEMBERS] = row[h]


def get(ref, slot):
    return [ref[(2 * slot + h) * MEMBERS : (2 * slot + h + 1) * MEMBERS] for h in range(2)]


def split(values, pieces):
    stack = []
    for _ in range(pieces):
        piece = values.astype(bf16).astype(f32)
        stack.append(piece)
        values = values - piece
    return jnp.concatenate(stack, axis=0)


def pick(rows, hit):
    left = jnp.concatenate([split(jnp.concatenate(values, axis=1), pieces) for values, pieces in rows], axis=0)
    total = jnp.dot(left.astype(bf16), hit, preferred_element_type=f32)
    found, at = [], 0
    for _, pieces in rows:
        parts = [total[at + i * MEMBERS : at + (i + 1) * MEMBERS] for i in range(pieces)]
        found.append(sum(parts[1:], parts[0]))
        at += pieces * MEMBERS
    return found


def forecast_kernel(
    cell_hbm, cells_hbm, radius_hbm, observed_hbm, sigma_hbm,
    surface_hbm, discharge_hbm, storage_hbm, exchange_hbm, depth_noise_hbm, flow_noise_hbm,
    own_ref, along_ref, across_ref, far_ref, extra_ref, depth_ref, flow_ref, stored_ref,
    surface_ref, discharge_ref, storage_ref, exchange_ref, depth_noise_ref, flow_noise_ref,
    first_ref, last_ref, cell_ref, cells_ref, radius_ref, observed_ref, sigma_ref, sems,
):
    chunks = []
    for c in range(MEMBERS // CHUNK):
        some = pl.ds(c * CHUNK, CHUNK)
        pairs = [
            (ref.at[some], to.at[some])
            for ref, to in ((surface_hbm, surface_ref), (discharge_hbm, discharge_ref), (storage_hbm, storage_ref))
        ] + [
            (ref.at[:, some], to.at[:, some])
            for ref, to in ((depth_noise_hbm, depth_noise_ref), (flow_noise_hbm, flow_noise_ref))
        ]
        if c == 0:
            pairs.append((exchange_hbm, exchange_ref))
        chunks.append(pairs)
    chunks.append([
        (cell_hbm, cell_ref), (cells_hbm, cells_ref), (radius_hbm, radius_ref), (observed_hbm, observed_ref),
        (sigma_hbm, sigma_ref),
    ])
    copies, used = [], 0
    for pairs in chunks:
        copies.append([])
        for source, target in pairs:
            copies[-1].append(pltpu.make_async_copy(source, target, sems.at[used]))
            copies[-1][-1].start()
            used += 1

    row = lax.broadcasted_iota(jnp.int32, (ROWS, LANES), 0)

    def member(p, carry):
        edge = pl.ds(pl.multiple_of(p * 8, 8), 8)

        def keep(slot, value):
            for h in range(2):
                first_ref[slot, h, edge] = value[h][:8]
                if slot != 5:
                    last_ref[slot, h, edge] = value[h][ROWS - 8 :]

        depth, flow, stored = [halves(ref[p].astype(f32)) for ref in (surface_ref, discharge_ref, storage_ref)]
        keep(0, depth)
        keep(1, flow)
        keep(2, stored)
        for step in range(2):
            depth_noise, flow_noise = [halves(ref[step, p].astype(f32)) for ref in (depth_noise_ref, flow_noise_ref)]
            keep(3 + 2 * step, depth_noise)
            keep(4 + 2 * step, flow_noise)
            beside = sides(*depth)
            for h in range(2):
                flow_below = jnp.where(row == 0, 0.0, pltpu.roll(flow[h], 1, 0))
                inflow = rate[h] * (depth[h] - stored[h])
                depth_next = (
                    (1.0 - 2.0 * diffusion) * depth[h] + diffusion * beside[h]
                    - advection * (flow[h] - flow_below) - inflow + depth_noise[h]
                )
                stored[h] = (1.0 - drainage) * stored[h] + inflow
                depth_above = jnp.where(row == ROWS - 1, 0.0, pltpu.roll(depth_next, ROWS - 1, 0))
                flow[h] = (flow[h] - gravity * (depth_above - depth_next) + flow_noise[h]) * (
                    1.0 / (1.0 + friction * jnp.abs(flow[h]))
                )
                depth[h] = depth_next
            if step == 0:
                keep(7, flow)
        at = pl.ds(pl.multiple_of(p * PITCH, 8), ROWS)
        for ref, value in ((depth_ref, depth), (flow_ref, flow), (stored_ref, stored)):
            for h in range(2):
                ref[h, at] = value[h]
        return carry

    for c in range(MEMBERS // CHUNK):
        for copy in copies[c]:
            copy.wait()
        if c == 0:
            rate = halves(exchange_ref[...].astype(f32))
        lax.fori_loop(c * CHUNK, (c + 1) * CHUNK, member, 0, unroll=4)

    def row_of(ref, slot, row):
        return [ref[slot, h, pl.ds(row, MEMBERS, stride=8)] for h in range(2)]

    def step_one(surface, flow, flow_below, stored, rate, noise):
        return each(
            lambda s, q, b, t, e, n, d: s - advection * (q - b) + d - e * (s - t) + n,
            surface, flow, flow_below, stored, rate, noise, spread(surface),
        )

    nothing = [jnp.zeros((MEMBERS, LANES), f32)] * 2
    rate_0, rate_1, rate_31 = [[r[i : i + 1] for r in rate] for i in (0, 1, ROWS - 1)]
    surface_0, surface_1 = row_of(first_ref, 0, 0), row_of(first_ref, 0, 1)
    flow_0, flow_1 = row_of(first_ref, 1, 0), row_of(first_ref, 1, 1)
    stored_0, stored_1 = row_of(first_ref, 2, 0), row_of(first_ref, 2, 1)
    depth_0 = step_one(surface_0, flow_0, nothing, stored_0, rate_0, row_of(first_ref, 3, 0))
    depth_1 = step_one(surface_1, flow_1, flow_0, stored_1, rate_1, row_of(first_ref, 3, 1))
    stored_next = each(lambda s, t, e: (1.0 - drainage) * t + e * (s - t), surface_0, stored_0, rate_0)
    inverse_0 = each(lambda q: 1.0 / (1.0 + friction * jnp.abs(q)), flow_0)
    flow_part = each(
        lambda q, d, n, i: (q - gravity * d + n) * i, flow_0, depth_1, row_of(first_ref, 4, 0), inverse_0
    )
    up_ref, down_ref = own_ref.at[0], own_ref.at[1]
    put(up_ref, 0, depth_0)
    put(up_ref, 1, each(lambda e, i: 1.0 - e - (advection * gravity) * i, rate_0, inverse_0))
    put(up_ref, 2, each(lambda e, t, n, q: e * t + n - advection * q, rate_0, stored_next, row_of(first_ref, 5, 0), flow_part))
    flow_31 = row_of(last_ref, 1, 7)
    depth_31 = step_one(
        row_of(last_ref, 0, 7), flow_31, row_of(last_ref, 1, 6), row_of(last_ref, 2, 7), rate_31, row_of(last_ref, 3, 7)
    )
    inverse_31 = each(lambda q: 1.0 / (1.0 + friction * jnp.abs(q)), flow_31)
    put(down_ref, 0, flow_31)
    put(down_ref, 1, each(lambda q, d, n, i: (q + gravity * d + n) * i, flow_31, depth_31, row_of(last_ref, 4, 7), inverse_31))
    put(down_ref, 2, each(lambda i: gravity * i, inverse_31))
    put(far_ref, 0, flow_31)
    put(extra_ref, 0, each(lambda i: gravity * i, inverse_0))
    put(extra_ref, 1, each(lambda q, i, d: q + gravity * i * d, flow_part, inverse_0, depth_0))
    put(extra_ref, 2, row_of(first_ref, 6, 0))
    put(extra_ref, 3, row_of(last_ref, 6, 7))
    put(extra_ref, 6, each(lambda e, z: e + z, rate_0, nothing))
    put(extra_ref, 4, each(lambda q: 1.0 / (1.0 + friction * jnp.abs(q)), row_of(first_ref, 7, 1)))
    put(extra_ref, 5, each(lambda q: 1.0 / (1.0 + friction * jnp.abs(q)), row_of(last_ref, 7, 6)))

    for copy in copies[-1]:
        copy.wait()
    cells = cells_ref[...]
    reach = radius_ref[...].astype(f32)
    facts = [
        ((cells >> 8) & (ROWS - 1)).astype(f32), (cells & (COLS - 1)).astype(f32), reach * reach,
        (cells >> 13).astype(f32), observed_ref[...], sigma_ref[...], jnp.zeros((2, SENS), f32),
    ]
    facts = jnp.concatenate([jnp.concatenate(facts, axis=0), jnp.ones((8, LANES - SENS), f32)], axis=1)
    lane = lax.broadcasted_iota(jnp.int32, (MEMBERS, LANES), 1)
    hit = (lax.broadcasted_iota(jnp.int32, (COLS, LANES), 0).astype(f32) == facts[1:2]).astype(f32).astype(bf16)
    (slope,) = pick([(each(lambda i: (advection * advection * gravity) * i, inverse_0), 3)], hit)
    sampled = pltpu.roll(jnp.where((facts[0:1] == 1.0) & (lane < SENS), slope, 0.0), SENS, 1)
    for k in range(SENS):
        cell = cell_ref[k]
        found = depth_ref[(cell >> 7) & 1, pl.ds((cell >> 8) & (ROWS - 1), MEMBERS, stride=PITCH)]
        sampled = jnp.where(lane == k, pltpu.roll(found, (k - cell) & (LANES - 1), 1), sampled)
    for i in range(2):
        own_ref[i, SAMPLED:ACROSS] = sampled
        own_ref[i, ACROSS:MESSAGE] = facts
    odd = (cell_ref[0] >> 13) & 1
    along_ref[...] = own_ref[odd]
    across_ref[0] = own_ref[1 - odd]


def join_kernel(across_ref, arrived_ref, far_ref, joined_ref):
    del across_ref, far_ref
    joined_ref[1] = arrived_ref[...]


def taper_rows(facts, at, offsets, strip, near_ref, taper_ref):
    count = len(offsets)
    entries = jnp.transpose(facts)
    column_at = lax.broadcasted_iota(jnp.int32, (SENS, COLS), 1).astype(f32)
    lines = []
    for part, offset in enumerate(offsets):
        entry = entries[at + part * SENS : at + (part + 1) * SENS]
        gap = column_at - entry[:, 1:2]
        squared = jnp.where(entry[:, 3:4] == strip + offset, entry[:, 2:3], 0.0)
        near_ref[part] = squared - gap * gap
        lines.append(jnp.broadcast_to(entry[:, 0:1] + offset * ROWS, (SENS, LANES)))

    def at_row(r, carry):
        here = r.astype(f32)
        for part in range(count):
            gap = here - lines[part]
            gap = gap * gap
            value = jnp.maximum(near_ref[part] - jnp.concatenate([gap, gap], axis=1), 0.0)
            coarse = value.astype(bf16)
            taper_ref[r, part * SENS : (part + 1) * SENS] = coarse
            taper_ref[r, (count + part) * SENS : (count + part + 1) * SENS] = (value - coarse.astype(f32)).astype(bf16)
        return carry

    lax.fori_loop(0, ROWS, at_row, 0, unroll=4 // count)


def taper_kernel(own_ref, tapers_ref, near_ref):
    facts = own_ref[0, ACROSS:MESSAGE]
    taper_rows(facts, 0, [0.0], facts[3:4, 0:1], near_ref, tapers_ref)


def finish_kernel(
    own_ref, tapers_ref, extra_ref, arrived_ref, far_ref, joined_ref, depth_in, flow_in, stored_in,
    out_ref, depth_ref, flow_ref, stored_ref,
    before_ref, after_ref, near_ref, taper_ref, weight_ref,
):
    del depth_in, flow_in, stored_in
    up_ref, down_ref = own_ref.at[0], own_ref.at[1]
    strip = own_ref[0, ACROSS + 3 : ACROSS + 4, 0:1]
    odd = strip - 2.0 * jnp.floor(0.5 * strip) > 0.5
    before_ref[...] = jnp.where(odd, joined_ref[0], joined_ref[1])
    after_ref[...] = jnp.where(odd, joined_ref[1], joined_ref[0])
    has_before = before_ref[ACROSS + 3 : ACROSS + 4, 0:1] == strip - 1.0
    has_after = after_ref[ACROSS + 3 : ACROSS + 4, 0:1] == strip + 1.0
    keep = lambda condition, row: each(lambda v: jnp.where(condition, v, 0.0), row)

    def line(ref, row):
        return [ref[h, pl.ds(row, MEMBERS, stride=PITCH)] for h in range(2)]

    def set_line(ref, row, values):
        for h in range(2):
            ref[h, pl.ds(row, MEMBERS, stride=PITCH)] = values[h]

    back = keep(has_before, get(before_ref, 0))
    start = each(lambda d, q: d + advection * q, get(up_ref, 0), back)
    back_next = keep(has_before, each(lambda f, i, d: f - i * d, get(before_ref, 1), get(before_ref, 2), start))
    depth_0 = each(
        lambda d, c, s, k, q: d * c + s + k + advection * q,
        start, get(up_ref, 1), spread(start), get(up_ref, 2), back_next,
    )
    turn_0 = get(extra_ref, 0)
    more_1 = each(lambda i, q: (advection * advection) * i * q, turn_0, back)
    depth_1 = each(lambda d, m: d + m, line(depth_ref, 1), more_1)
    flow_0 = each(lambda f, i, q: f + advection * i * q, get(extra_ref, 1), turn_0, back)
    set_line(depth_ref, 0, depth_0)
    set_line(depth_ref, 1, depth_1)
    set_line(flow_ref, 0, each(
        lambda f, a, d, n: (f - gravity * (a - d) + n) * (1.0 / (1.0 + friction * jnp.abs(f))),
        flow_0, depth_1, depth_0, get(extra_ref, 2),
    ))
    set_line(flow_ref, 1, each(lambda f, i, m: f + gravity * i * m, line(flow_ref, 1), get(extra_ref, 4), more_1))
    set_line(stored_ref, 0, each(lambda t, e, q: t + advection * e * q, line(stored_ref, 0), get(extra_ref, 6), back))
    last = get(down_ref, 0)
    end = keep(has_after, each(lambda d, q: d + advection * q, get(after_ref, 0), last))
    flow_31 = each(lambda f, i, d: f - i * d, get(down_ref, 1), get(down_ref, 2), end)
    depth_32 = keep(has_after, each(
        lambda d, c, s, k, q: d * c + s + k + advection * q,
        end, get(after_ref, 1), spread(end), get(after_ref, 2), flow_31,
    ))
    more_31 = each(lambda i, d: advection * i * d, get(down_ref, 2), end)
    depth_31 = each(lambda d, m: d + m, line(depth_ref, ROWS - 1), more_31)
    set_line(depth_ref, ROWS - 1, depth_31)
    set_line(flow_ref, ROWS - 1, each(
        lambda f, a, d, n: (f - gravity * (a - d) + n) * (1.0 / (1.0 + friction * jnp.abs(f))),
        flow_31, depth_32, depth_31, get(extra_ref, 3),
    ))
    set_line(flow_ref, ROWS - 2, each(
        lambda f, i, m: f - gravity * i * m, line(flow_ref, ROWS - 2), get(extra_ref, 5), more_31
    ))

    lane = lax.broadcasted_iota(jnp.int32, (1, LANES), 1)
    group = lane // SENS

    def beside(first, end, shift=0):
        parts = (own_ref[0, first:end], before_ref[first:end], after_ref[first:end])
        parts = [pltpu.roll(part, (i * SENS - shift) % LANES, 1) for i, part in enumerate(parts)]
        return jnp.where(group == 0, parts[0], jnp.where(group == 1, parts[1], parts[2]))

    facts = beside(ACROSS, MESSAGE)
    place = facts[0:1]
    hit = (lax.broadcasted_iota(jnp.int32, (COLS, LANES), 0).astype(f32) == facts[1:2]).astype(f32).astype(bf16)

    far = each(lambda a, b: jnp.where(strip > 1.5, jnp.where(odd, a, b), 0.0), get(arrived_ref, 0), get(far_ref, 0))
    beyond_31 = each(lambda i, d: advection * i * d, keep(has_before, get(before_ref, 2)), start)
    wanted = [
        (beyond_31, 3, ROWS - 1.0, 1), (depth_0, 3, 0.0, 0), (more_1, 3, 1.0, 0), (more_31, 3, ROWS - 1.0, 0),
        (depth_32, 3, 0.0, 2), (far, 1, 1.0, 1), (last, 1, 1.0, 2),
    ]
    found = pick([(values, pieces) for values, pieces, _, _ in wanted], hit)
    found = [jnp.where((place == row) & (group == of), value, 0.0) for value, (_, _, row, of) in zip(found, wanted)]
    added, beyond = sum(found[1:5], found[0]), found[5] + found[6]
    known = jnp.where((place == 0.0) & (group != 1), 0.0, beside(SAMPLED, ACROSS))
    found = known + added + beside(SAMPLED, ACROSS, SENS) * beyond
    real = group < 3
    misfit = (found - facts[4:5]) / jnp.where(real, facts[5:6], 1.0)
    lik = jnp.where(real, -0.5 * misfit * misfit / jnp.where(real, facts[2:3], 1.0), 0.0)
    pieces = split(lik, 3)
    pieces = jnp.concatenate(
        [jnp.where(group == 0, pieces, pltpu.roll(pieces, SENS, 1)), pltpu.roll(pieces, LANES - SENS, 1)], axis=1
    )[:, : 6 * SENS].astype(bf16)

    taper_rows(facts, SENS, [-1.0, 1.0], strip, near_ref, taper_ref)
    for i in range(ROWS // 8):
        for r in range(8 * i, 8 * i + 8):
            tapers = jnp.concatenate([tapers_ref[r], taper_ref[r]], axis=0)
            part = jnp.dot(pieces, tapers, preferred_element_type=f32)
            weight = part[:MEMBERS] + part[MEMBERS : 2 * MEMBERS] + part[2 * MEMBERS :]
            for half in range(2):
                weight_ref[half, r * MEMBERS : (r + 1) * MEMBERS] = weight[:, half * LANES : (half + 1) * LANES]
        for half in range(2):
            weights = [weight_ref[half, pl.ds(8 * i * MEMBERS + p, 8, stride=MEMBERS)] for p in range(MEMBERS)]
            best = weights[0]
            for p in range(1, MEMBERS):
                best = jnp.maximum(best, weights[p])
            sums = [jnp.zeros((8, LANES), f32) for _ in range(4)]
            for p in range(MEMBERS):
                factor = jnp.exp(weights[p] - best)
                at = pl.ds(p * PITCH + 8 * i, 8)
                sums[0] = sums[0] + factor
                sums[1] = sums[1] + factor * depth_ref[half, at]
                sums[2] = sums[2] + factor * flow_ref[half, at]
                sums[3] = sums[3] + factor * stored_ref[half, at]
            inverse = 1.0 / sums[0]
            results = (best + jnp.log(sums[0]), sums[1] * inverse, sums[2] * inverse, sums[3] * inverse)
            for slot, result in enumerate(results):
                out_ref[pl.ds(64 * i + 2 * slot + half, 8, stride=8)] = result


def combine_kernel(groups, in_ref, out_ref):
    def quantity(slot, half):
        return in_ref[pl.ds(2 * slot + half, groups, stride=8)]

    rows = []
    totals = []
    for half in range(2):
        level = quantity(0, half)
        share = jnp.exp(level - jnp.max(level, axis=0, keepdims=True))
        totals.append((share, 1.0 / jnp.sum(share, axis=0, keepdims=True)))
    for slot in range(1, 4):
        for half in range(2):
            share, inverse = totals[half]
            rows.append(jnp.sum(share * quantity(slot, half), axis=0, keepdims=True) * inverse)
    rows.append(jnp.zeros((2, LANES), f32))
    result = jnp.concatenate(rows, axis=0)
    for copy in range(groups):
        out_ref[copy * 8 : (copy + 1) * 8] = result


def spread_kernel(in_ref, depth_ref, flow_ref, stored_ref):
    for slot, ref in enumerate((depth_ref, flow_ref, stored_ref)):
        for half in range(2):
            ref[:, half * LANES : (half + 1) * LANES] = in_ref[pl.ds(2 * slot + half, ROWS, stride=8)]


VMEM = pl.BlockSpec(memory_space=pltpu.VMEM)
HBM = pl.BlockSpec(memory_space=pltpu.HBM)


def call(kernel, name, in_specs, outs, scratch=(), aliases=None):
    return pl.pallas_call(
        kernel,
        name=name,
        in_specs=in_specs,
        out_specs=[VMEM] * len(outs),
        out_shape=[jax.ShapeDtypeStruct(shape, dtype) for shape, dtype in outs],
        scratch_shapes=list(scratch),
        input_output_aliases=aliases or {},
        compiler_params=pltpu.CompilerParams(vmem_limit_bytes=40 * 1024 * 1024),
    )


def local(
    surface, discharge, storage, exchange, depth_perturbation, flow_perturbation,
    sensor_cell, sensor_radius, observed, sensor_sigma,
):
    strips = lax.axis_size("strip")
    groups = lax.axis_size("dom")
    order = list(range(0, strips, 2)) + list(range(strips - 1, 0, -2))
    onward = [(order[i], order[(i + 1) % strips]) for i in range(strips)]
    backward = [(b, a) for a, b in onward]
    swapped = [(i, i ^ 1) for i in range(strips)]
    stay = lambda values: pltpu.with_memory_space_constraint(values, pltpu.HBM)
    as_row = lambda values: stay(values.reshape(1, SENS))
    fields = [stay(f) for f in (surface, discharge, storage, exchange, depth_perturbation, flow_perturbation)]
    grid = ((2, MEMBERS * PITCH, LANES), f32)
    message = (MESSAGE, LANES)
    edges = lambda count: ((2 * count * MEMBERS, LANES), f32)
    row_of = lambda dtype: pltpu.VMEM((1, SENS), dtype)
    own, along, across, far, extra, depth, flow, stored = call(
        forecast_kernel, "forecast", [HBM] * 11,
        [((2,) + message, f32), (message, f32), ((2,) + message, f32), edges(1), edges(7), grid, grid, grid],
        [pltpu.VMEM(field.shape, field.dtype) for field in fields]
        + [
            pltpu.VMEM((8, 2, MEMBERS * 8, LANES), f32), pltpu.VMEM((8, 2, MEMBERS * 8, LANES), f32),
            pltpu.SMEM((SENS,), jnp.int32), row_of(jnp.int32), row_of(jnp.int32), row_of(f32), row_of(f32),
            pltpu.SemaphoreType.DMA((21,)),
        ],
    )(stay(sensor_cell), as_row(sensor_cell), as_row(sensor_radius), as_row(observed), as_row(sensor_sigma), *fields)
    arrived = lax.ppermute(along, "strip", backward)
    far = lax.ppermute(far, "strip", onward)
    (joined,) = call(join_kernel, "join", [VMEM] * 3, [((2,) + message, f32)], aliases={0: 0})(across, arrived, far)
    joined = lax.ppermute(joined, "strip", swapped)
    (tapers,) = call(
        taper_kernel, "taper", [VMEM], [((ROWS, 2 * SENS, COLS), bf16)], [pltpu.VMEM((1, SENS, COLS), f32)],
    )(own)
    parts, depth, flow, stored = call(
        finish_kernel, "finish", [VMEM] * 9, [((groups * 8, LANES), f32), grid, grid, grid],
        [
            pltpu.VMEM(message, f32), pltpu.VMEM(message, f32), pltpu.VMEM((2, SENS, COLS), f32),
            pltpu.VMEM((ROWS, 4 * SENS, COLS), bf16), pltpu.VMEM((2, ROWS * MEMBERS, LANES), f32),
        ],
        aliases={6: 1, 7: 2, 8: 3},
    )(own, tapers, extra, arrived, far, joined, depth, flow, stored)
    turned = [(20 + i) % groups for i in range(groups)]
    shared = lax.all_to_all(parts.reshape(groups, 8, LANES), "dom", 0, 0, tiled=True, axis_index_groups=[turned])
    (rows,) = call(
        lambda *refs: combine_kernel(groups, *refs), "combine", [VMEM], [((groups * 8, LANES), f32)],
    )(shared.reshape(groups * 8, LANES))
    whole = lax.all_to_all(
        rows.reshape(groups, 8, LANES), "dom", 0, 0, tiled=True, axis_index_groups=[turned]
    )
    return tuple(
        call(spread_kernel, "spread", [VMEM], [((ROWS, COLS), f32)] * 3)(whole.reshape(groups * 8, LANES))
    )


def solution(mesh):
    return jax.shard_map(
        local,
        mesh=mesh,
        in_specs=(
            P("dom", "strip", None),
            P("dom", "strip", None),
            P("dom", "strip", None),
            P("strip", None),
            P(None, "dom", "strip", None),
            P(None, "dom", "strip", None),
            P("strip"),
            P("strip"),
            P("strip"),
            P("strip"),
        ),
        out_specs=(P("strip", None), P("strip", None), P("strip", None)),
        check_vma=False,
    )
```

```python
import jax
import jax.numpy as jnp
from jax import lax
from jax.experimental import pallas as pl
from jax.experimental.pallas import tpu as pltpu
from jax.sharding import PartitionSpec as P

advection = 0.4
gravity = 0.5
diffusion = 0.15
friction = 0.3
drainage = 0.1

MEMBERS = 24
ROWS = 32
COLS = 256
SENS = 32
LANES = 128
CHUNK = 8
PITCH = 40
SAMPLED = 6 * MEMBERS
ACROSS = SAMPLED + MEMBERS
MESSAGE = ACROSS + 8

f32 = jnp.float32
bf16 = jnp.bfloat16


def sides(left_half, right_half):
    lane = lax.broadcasted_iota(jnp.int32, left_half.shape, 1)
    first, last = lane == 0, lane == LANES - 1
    left_back, right_back = pltpu.roll(left_half, 1, 1), pltpu.roll(right_half, 1, 1)
    left_on, right_on = pltpu.roll(left_half, LANES - 1, 1), pltpu.roll(right_half, LANES - 1, 1)
    return (
        jnp.where(first, left_half, left_back) + jnp.where(last, right_on, left_on),
        jnp.where(first, left_back, right_back) + jnp.where(last, right_half, right_on),
    )


def spread(field):
    return [diffusion * (around - 2.0 * here) for around, here in zip(sides(*field), field)]


def halves(values):
    return [values[:, :LANES], values[:, LANES:]]


def each(function, *rows):
    return [function(*parts) for parts in zip(*rows)]


def put(ref, slot, row):
    for h in range(2):
        ref[(2 * slot + h) * MEMBERS : (2 * slot + h + 1) * MEMBERS] = row[h]


def get(ref, slot):
    return [ref[(2 * slot + h) * MEMBERS : (2 * slot + h + 1) * MEMBERS] for h in range(2)]


def split(values, pieces):
    stack = []
    for _ in range(pieces):
        piece = values.astype(bf16).astype(f32)
        stack.append(piece)
        values = values - piece
    return jnp.concatenate(stack, axis=0)


def pick(rows, hit):
    left = jnp.concatenate([split(jnp.concatenate(values, axis=1), pieces) for values, pieces in rows], axis=0)
    total = jnp.dot(left.astype(bf16), hit, preferred_element_type=f32)
    found, at = [], 0
    for _, pieces in rows:
        parts = [total[at + i * MEMBERS : at + (i + 1) * MEMBERS] for i in range(pieces)]
        found.append(sum(parts[1:], parts[0]))
        at += pieces * MEMBERS
    return found


def next_flow(flow, depth, noise, row):
    depth_above = jnp.where(row == ROWS - 1, 0.0, pltpu.roll(depth, ROWS - 1, 0))
    return (flow - gravity * (depth_above - depth) + noise) * (1.0 / (1.0 + friction * jnp.abs(flow)))


def forecast_kernel(
    cell_hbm, cells_hbm, radius_hbm, observed_hbm, sigma_hbm,
    surface_hbm, discharge_hbm, storage_hbm, exchange_hbm, depth_noise_hbm, flow_noise_hbm,
    own_ref, along_ref, across_ref, far_ref, extra_ref, depth_ref, flow_ref, stored_ref,
    surface_ref, discharge_ref, storage_ref, exchange_ref, depth_noise_ref, flow_noise_ref,
    first_ref, last_ref, cell_ref, cells_ref, radius_ref, observed_ref, sigma_ref, sems,
):
    chunks = []
    for c in range(MEMBERS // CHUNK):
        some = pl.ds(c * CHUNK, CHUNK)
        pairs = [
            (ref.at[some], to.at[some])
            for ref, to in ((surface_hbm, surface_ref), (discharge_hbm, discharge_ref), (storage_hbm, storage_ref))
        ] + [
            (depth_noise_hbm.at[:, some], depth_noise_ref.at[:, some]),
            (flow_noise_hbm.at[0, some], flow_noise_ref.at[some]),
        ]
        if c == 0:
            pairs.append((exchange_hbm, exchange_ref))
        chunks.append(pairs)
    chunks.append([
        (cell_hbm, cell_ref), (cells_hbm, cells_ref), (radius_hbm, radius_ref), (observed_hbm, observed_ref),
        (sigma_hbm, sigma_ref),
    ])
    copies, used = [], 0
    for pairs in chunks:
        copies.append([])
        for source, target in pairs:
            copies[-1].append(pltpu.make_async_copy(source, target, sems.at[used]))
            copies[-1][-1].start()
            used += 1

    row = lax.broadcasted_iota(jnp.int32, (ROWS, LANES), 0)

    def member(p, carry):
        edge = pl.ds(pl.multiple_of(p * 8, 8), 8)

        def keep(slot, value):
            for h in range(2):
                first_ref[slot, h, edge] = value[h][:8]
                if slot != 5:
                    last_ref[slot, h, edge] = value[h][ROWS - 8 :]

        depth, flow, stored = [halves(ref[p].astype(f32)) for ref in (surface_ref, discharge_ref, storage_ref)]
        keep(0, depth)
        keep(1, flow)
        keep(2, stored)
        for step in range(2):
            depth_noise = halves(depth_noise_ref[step, p].astype(f32))
            keep(3 + 2 * step, depth_noise)
            beside = sides(*depth)
            for h in range(2):
                flow_below = jnp.where(row == 0, 0.0, pltpu.roll(flow[h], 1, 0))
                inflow = rate[h] * (depth[h] - stored[h])
                depth[h] = (
                    (1.0 - 2.0 * diffusion) * depth[h] + diffusion * beside[h]
                    - advection * (flow[h] - flow_below) - inflow + depth_noise[h]
                )
                stored[h] = (1.0 - drainage) * stored[h] + inflow
            if step == 0:
                flow_noise = halves(flow_noise_ref[p].astype(f32))
                keep(4, flow_noise)
                flow = each(lambda q, d, n: next_flow(q, d, n, row), flow, depth, flow_noise)
        at = pl.ds(pl.multiple_of(p * PITCH, 8), ROWS)
        for ref, value in ((depth_ref, depth), (flow_ref, flow), (stored_ref, stored)):
            for h in range(2):
                ref[h, at] = value[h]
        return carry

    for c in range(MEMBERS // CHUNK):
        for copy in copies[c]:
            copy.wait()
        if c == 0:
            rate = halves(exchange_ref[...].astype(f32))
        lax.fori_loop(c * CHUNK, (c + 1) * CHUNK, member, 0, unroll=4)

    def row_of(ref, slot, row):
        return [ref[slot, h, pl.ds(row, MEMBERS, stride=8)] for h in range(2)]

    def step_one(surface, flow, flow_below, stored, rate, noise):
        return each(
            lambda s, q, b, t, e, n, d: s - advection * (q - b) + d - e * (s - t) + n,
            surface, flow, flow_below, stored, rate, noise, spread(surface),
        )

    nothing = [jnp.zeros((MEMBERS, LANES), f32)] * 2
    rate_0, rate_1, rate_31 = [[r[i : i + 1] for r in rate] for i in (0, 1, ROWS - 1)]
    surface_0, surface_1 = row_of(first_ref, 0, 0), row_of(first_ref, 0, 1)
    flow_0, flow_1 = row_of(first_ref, 1, 0), row_of(first_ref, 1, 1)
    stored_0, stored_1 = row_of(first_ref, 2, 0), row_of(first_ref, 2, 1)
    depth_0 = step_one(surface_0, flow_0, nothing, stored_0, rate_0, row_of(first_ref, 3, 0))
    depth_1 = step_one(surface_1, flow_1, flow_0, stored_1, rate_1, row_of(first_ref, 3, 1))
    stored_next = each(lambda s, t, e: (1.0 - drainage) * t + e * (s - t), surface_0, stored_0, rate_0)
    inverse_0 = each(lambda q: 1.0 / (1.0 + friction * jnp.abs(q)), flow_0)
    flow_part = each(
        lambda q, d, n, i: (q - gravity * d + n) * i, flow_0, depth_1, row_of(first_ref, 4, 0), inverse_0
    )
    up_ref, down_ref = own_ref.at[0], own_ref.at[1]
    put(up_ref, 0, depth_0)
    put(up_ref, 1, each(lambda e, i: 1.0 - e - (advection * gravity) * i, rate_0, inverse_0))
    put(up_ref, 2, each(lambda e, t, n, q: e * t + n - advection * q, rate_0, stored_next, row_of(first_ref, 5, 0), flow_part))
    flow_31 = row_of(last_ref, 1, 7)
    depth_31 = step_one(
        row_of(last_ref, 0, 7), flow_31, row_of(last_ref, 1, 6), row_of(last_ref, 2, 7), rate_31, row_of(last_ref, 3, 7)
    )
    inverse_31 = each(lambda q: 1.0 / (1.0 + friction * jnp.abs(q)), flow_31)
    put(down_ref, 0, flow_31)
    put(down_ref, 1, each(lambda q, d, n, i: (q + gravity * d + n) * i, flow_31, depth_31, row_of(last_ref, 4, 7), inverse_31))
    put(down_ref, 2, each(lambda i: gravity * i, inverse_31))
    put(far_ref, 0, flow_31)
    put(extra_ref, 0, each(lambda i: gravity * i, inverse_0))
    put(extra_ref, 1, each(lambda q, i, d: q + gravity * i * d, flow_part, inverse_0, depth_0))
    put(extra_ref, 2, each(lambda e, z: e + z, rate_0, nothing))
    for copy in copies[-1]:
        copy.wait()
    cells = cells_ref[...]
    reach = radius_ref[...].astype(f32)
    facts = [
        ((cells >> 8) & (ROWS - 1)).astype(f32), (cells & (COLS - 1)).astype(f32), reach * reach,
        (cells >> 13).astype(f32), observed_ref[...], sigma_ref[...], jnp.zeros((2, SENS), f32),
    ]
    facts = jnp.concatenate([jnp.concatenate(facts, axis=0), jnp.ones((8, LANES - SENS), f32)], axis=1)
    lane = lax.broadcasted_iota(jnp.int32, (MEMBERS, LANES), 1)
    hit = (lax.broadcasted_iota(jnp.int32, (COLS, LANES), 0).astype(f32) == facts[1:2]).astype(f32).astype(bf16)
    (slope,) = pick([(each(lambda i: (advection * advection * gravity) * i, inverse_0), 3)], hit)
    sampled = pltpu.roll(jnp.where((facts[0:1] == 1.0) & (lane < SENS), slope, 0.0), SENS, 1)
    for k in range(SENS):
        cell = cell_ref[k]
        found = depth_ref[(cell >> 7) & 1, pl.ds((cell >> 8) & (ROWS - 1), MEMBERS, stride=PITCH)]
        sampled = jnp.where(lane == k, pltpu.roll(found, (k - cell) & (LANES - 1), 1), sampled)
    for i in range(2):
        own_ref[i, SAMPLED:ACROSS] = sampled
        own_ref[i, ACROSS:MESSAGE] = facts
    odd = (cell_ref[0] >> 13) & 1
    along_ref[...] = own_ref[odd]
    across_ref[0] = own_ref[1 - odd]


def line(ref, row):
    return [ref[h, pl.ds(row, MEMBERS, stride=PITCH)] for h in range(2)]


def set_line(ref, row, values):
    for h in range(2):
        ref[h, pl.ds(row, MEMBERS, stride=PITCH)] = values[h]


def flow_kernel(flow_noise_hbm, depth_ref, flow_in, flow_ref, late_ref, flow_noise_ref, first_ref, last_ref, sems):
    del flow_in
    copies = []
    for c in range(MEMBERS // CHUNK):
        some = pl.ds(c * CHUNK, CHUNK)
        copies.append(pltpu.make_async_copy(flow_noise_hbm.at[1, some], flow_noise_ref.at[some], sems.at[c]))
        copies[c].start()
    for slot, row in ((2, 1), (3, ROWS - 2)):
        put(late_ref, slot, each(lambda q: 1.0 / (1.0 + friction * jnp.abs(q)), line(flow_ref, row)))
    row = lax.broadcasted_iota(jnp.int32, (ROWS, LANES), 0)

    def member(p, carry):
        at, edge = pl.ds(pl.multiple_of(p * PITCH, 8), ROWS), pl.ds(pl.multiple_of(p * 8, 8), 8)
        noise = halves(flow_noise_ref[p].astype(f32))
        for h in range(2):
            first_ref[h, edge] = noise[h][:8]
            last_ref[h, edge] = noise[h][ROWS - 8 :]
            flow_ref[h, at] = next_flow(flow_ref[h, at], depth_ref[h, at], noise[h], row)
        return carry

    for c in range(MEMBERS // CHUNK):
        copies[c].wait()
        lax.fori_loop(c * CHUNK, (c + 1) * CHUNK, member, 0, unroll=4)
    put(late_ref, 0, [first_ref[h, pl.ds(0, MEMBERS, stride=8)] for h in range(2)])
    put(late_ref, 1, [last_ref[h, pl.ds(7, MEMBERS, stride=8)] for h in range(2)])


def join_kernel(across_ref, arrived_ref, far_ref, late_ref, joined_ref):
    del across_ref, far_ref, late_ref
    joined_ref[1] = arrived_ref[...]


def taper_rows(facts, at, offsets, strip, near_ref, taper_ref):
    count = len(offsets)
    entries = jnp.transpose(facts)
    column_at = lax.broadcasted_iota(jnp.int32, (SENS, COLS), 1).astype(f32)
    lines = []
    for part, offset in enumerate(offsets):
        entry = entries[at + part * SENS : at + (part + 1) * SENS]
        gap = column_at - entry[:, 1:2]
        squared = jnp.where(entry[:, 3:4] == strip + offset, entry[:, 2:3], 0.0)
        near_ref[part] = squared - gap * gap
        lines.append(jnp.broadcast_to(entry[:, 0:1] + offset * ROWS, (SENS, LANES)))

    def at_row(r, carry):
        here = r.astype(f32)
        for part in range(count):
            gap = here - lines[part]
            gap = gap * gap
            value = jnp.maximum(near_ref[part] - jnp.concatenate([gap, gap], axis=1), 0.0)
            coarse = value.astype(bf16)
            taper_ref[r, part * SENS : (part + 1) * SENS] = coarse
            taper_ref[r, (count + part) * SENS : (count + part + 1) * SENS] = (value - coarse.astype(f32)).astype(bf16)
        return carry

    lax.fori_loop(0, ROWS, at_row, 0, unroll=4 // count)


def taper_kernel(own_ref, tapers_ref, near_ref):
    facts = own_ref[0, ACROSS:MESSAGE]
    taper_rows(facts, 0, [0.0], facts[3:4, 0:1], near_ref, tapers_ref)


def finish_kernel(
    own_ref, tapers_ref, extra_ref, late_ref, arrived_ref, far_ref, joined_ref, depth_in, flow_in, stored_in,
    out_ref, depth_ref, flow_ref, stored_ref,
    before_ref, after_ref, near_ref, taper_ref, weight_ref,
):
    del depth_in, flow_in, stored_in
    up_ref, down_ref = own_ref.at[0], own_ref.at[1]
    strip = own_ref[0, ACROSS + 3 : ACROSS + 4, 0:1]
    odd = strip - 2.0 * jnp.floor(0.5 * strip) > 0.5
    before_ref[...] = jnp.where(odd, joined_ref[0], joined_ref[1])
    after_ref[...] = jnp.where(odd, joined_ref[1], joined_ref[0])
    has_before = before_ref[ACROSS + 3 : ACROSS + 4, 0:1] == strip - 1.0
    has_after = after_ref[ACROSS + 3 : ACROSS + 4, 0:1] == strip + 1.0
    keep = lambda condition, row: each(lambda v: jnp.where(condition, v, 0.0), row)

    back = keep(has_before, get(before_ref, 0))
    start = each(lambda d, q: d + advection * q, get(up_ref, 0), back)
    back_next = keep(has_before, each(lambda f, i, d: f - i * d, get(before_ref, 1), get(before_ref, 2), start))
    depth_0 = each(
        lambda d, c, s, k, q: d * c + s + k + advection * q,
        start, get(up_ref, 1), spread(start), get(up_ref, 2), back_next,
    )
    turn_0 = get(extra_ref, 0)
    more_1 = each(lambda i, q: (advection * advection) * i * q, turn_0, back)
    depth_1 = each(lambda d, m: d + m, line(depth_ref, 1), more_1)
    flow_0 = each(lambda f, i, q: f + advection * i * q, get(extra_ref, 1), turn_0, back)
    set_line(depth_ref, 0, depth_0)
    set_line(depth_ref, 1, depth_1)
    set_line(flow_ref, 0, each(
        lambda f, a, d, n: (f - gravity * (a - d) + n) * (1.0 / (1.0 + friction * jnp.abs(f))),
        flow_0, depth_1, depth_0, get(late_ref, 0),
    ))
    set_line(flow_ref, 1, each(lambda f, i, m: f + gravity * i * m, line(flow_ref, 1), get(late_ref, 2), more_1))
    set_line(stored_ref, 0, each(lambda t, e, q: t + advection * e * q, line(stored_ref, 0), get(extra_ref, 2), back))
    last = get(down_ref, 0)
    end = keep(has_after, each(lambda d, q: d + advection * q, get(after_ref, 0), last))
    flow_31 = each(lambda f, i, d: f - i * d, get(down_ref, 1), get(down_ref, 2), end)
    depth_32 = keep(has_after, each(
        lambda d, c, s, k, q: d * c + s + k + advection * q,
        end, get(after_ref, 1), spread(end), get(after_ref, 2), flow_31,
    ))
    more_31 = each(lambda i, d: advection * i * d, get(down_ref, 2), end)
    depth_31 = each(lambda d, m: d + m, line(depth_ref, ROWS - 1), more_31)
    set_line(depth_ref, ROWS - 1, depth_31)
    set_line(flow_ref, ROWS - 1, each(
        lambda f, a, d, n: (f - gravity * (a - d) + n) * (1.0 / (1.0 + friction * jnp.abs(f))),
        flow_31, depth_32, depth_31, get(late_ref, 1),
    ))
    set_line(flow_ref, ROWS - 2, each(
        lambda f, i, m: f - gravity * i * m, line(flow_ref, ROWS - 2), get(late_ref, 3), more_31
    ))

    lane = lax.broadcasted_iota(jnp.int32, (1, LANES), 1)
    group = lane // SENS

    def beside(first, end, shift=0):
        parts = (own_ref[0, first:end], before_ref[first:end], after_ref[first:end])
        parts = [pltpu.roll(part, (i * SENS - shift) % LANES, 1) for i, part in enumerate(parts)]
        return jnp.where(group == 0, parts[0], jnp.where(group == 1, parts[1], parts[2]))

    facts = beside(ACROSS, MESSAGE)
    place = facts[0:1]
    hit = (lax.broadcasted_iota(jnp.int32, (COLS, LANES), 0).astype(f32) == facts[1:2]).astype(f32).astype(bf16)

    far = each(lambda a, b: jnp.where(strip > 1.5, jnp.where(odd, a, b), 0.0), get(arrived_ref, 0), get(far_ref, 0))
    beyond_31 = each(lambda i, d: advection * i * d, keep(has_before, get(before_ref, 2)), start)
    wanted = [
        (beyond_31, 3, ROWS - 1.0, 1), (depth_0, 3, 0.0, 0), (more_1, 3, 1.0, 0), (more_31, 3, ROWS - 1.0, 0),
        (depth_32, 3, 0.0, 2), (far, 1, 1.0, 1), (last, 1, 1.0, 2),
    ]
    found = pick([(values, pieces) for values, pieces, _, _ in wanted], hit)
    found = [jnp.where((place == row) & (group == of), value, 0.0) for value, (_, _, row, of) in zip(found, wanted)]
    added, beyond = sum(found[1:5], found[0]), found[5] + found[6]
    known = jnp.where((place == 0.0) & (group != 1), 0.0, beside(SAMPLED, ACROSS))
    found = known + added + beside(SAMPLED, ACROSS, SENS) * beyond
    real = group < 3
    misfit = (found - facts[4:5]) / jnp.where(real, facts[5:6], 1.0)
    lik = jnp.where(real, -0.5 * misfit * misfit / jnp.where(real, facts[2:3], 1.0), 0.0)
    pieces = split(lik, 3)
    pieces = jnp.concatenate(
        [jnp.where(group == 0, pieces, pltpu.roll(pieces, SENS, 1)), pltpu.roll(pieces, LANES - SENS, 1)], axis=1
    )[:, : 6 * SENS].astype(bf16)

    taper_rows(facts, SENS, [-1.0, 1.0], strip, near_ref, taper_ref)
    for i in range(ROWS // 8):
        for r in range(8 * i, 8 * i + 8):
            tapers = jnp.concatenate([tapers_ref[r], taper_ref[r]], axis=0)
            part = jnp.dot(pieces, tapers, preferred_element_type=f32)
            weight = part[:MEMBERS] + part[MEMBERS : 2 * MEMBERS] + part[2 * MEMBERS :]
            for half in range(2):
                weight_ref[half, r * MEMBERS : (r + 1) * MEMBERS] = weight[:, half * LANES : (half + 1) * LANES]
        for half in range(2):
            weights = [weight_ref[half, pl.ds(8 * i * MEMBERS + p, 8, stride=MEMBERS)] for p in range(MEMBERS)]
            best = weights[0]
            for p in range(1, MEMBERS):
                best = jnp.maximum(best, weights[p])
            sums = [jnp.zeros((8, LANES), f32) for _ in range(4)]
            for p in range(MEMBERS):
                factor = jnp.exp(weights[p] - best)
                at = pl.ds(p * PITCH + 8 * i, 8)
                sums[0] = sums[0] + factor
                sums[1] = sums[1] + factor * depth_ref[half, at]
                sums[2] = sums[2] + factor * flow_ref[half, at]
                sums[3] = sums[3] + factor * stored_ref[half, at]
            inverse = 1.0 / sums[0]
            results = (best + jnp.log(sums[0]), sums[1] * inverse, sums[2] * inverse, sums[3] * inverse)
            for slot, result in enumerate(results):
                out_ref[pl.ds(64 * i + 2 * slot + half, 8, stride=8)] = result


def combine_kernel(groups, in_ref, out_ref):
    def quantity(slot, half):
        return in_ref[pl.ds(2 * slot + half, groups, stride=8)]

    rows = []
    totals = []
    for half in range(2):
        level = quantity(0, half)
        share = jnp.exp(level - jnp.max(level, axis=0, keepdims=True))
        totals.append((share, 1.0 / jnp.sum(share, axis=0, keepdims=True)))
    for slot in range(1, 4):
        for half in range(2):
            share, inverse = totals[half]
            rows.append(jnp.sum(share * quantity(slot, half), axis=0, keepdims=True) * inverse)
    rows.append(jnp.zeros((2, LANES), f32))
    result = jnp.concatenate(rows, axis=0)
    for copy in range(groups):
        out_ref[copy * 8 : (copy + 1) * 8] = result


def spread_kernel(in_ref, depth_ref, flow_ref, stored_ref):
    for slot, ref in enumerate((depth_ref, flow_ref, stored_ref)):
        for half in range(2):
            ref[:, half * LANES : (half + 1) * LANES] = in_ref[pl.ds(2 * slot + half, ROWS, stride=8)]


VMEM = pl.BlockSpec(memory_space=pltpu.VMEM)
HBM = pl.BlockSpec(memory_space=pltpu.HBM)


def call(kernel, name, in_specs, outs, scratch=(), aliases=None):
    return pl.pallas_call(
        kernel,
        name=name,
        in_specs=in_specs,
        out_specs=[VMEM] * len(outs),
        out_shape=[jax.ShapeDtypeStruct(shape, dtype) for shape, dtype in outs],
        scratch_shapes=list(scratch),
        input_output_aliases=aliases or {},
        compiler_params=pltpu.CompilerParams(vmem_limit_bytes=40 * 1024 * 1024),
    )


def local(
    surface, discharge, storage, exchange, depth_perturbation, flow_perturbation,
    sensor_cell, sensor_radius, observed, sensor_sigma,
):
    strips = lax.axis_size("strip")
    groups = lax.axis_size("dom")
    order = list(range(0, strips, 2)) + list(range(strips - 1, 0, -2))
    onward = [(order[i], order[(i + 1) % strips]) for i in range(strips)]
    backward = [(b, a) for a, b in onward]
    swapped = [(i, i ^ 1) for i in range(strips)]
    stay = lambda values: pltpu.with_memory_space_constraint(values, pltpu.HBM)
    as_row = lambda values: stay(values.reshape(1, SENS))
    fields = [stay(f) for f in (surface, discharge, storage, exchange, depth_perturbation, flow_perturbation)]
    grid = ((2, MEMBERS * PITCH, LANES), f32)
    message = (MESSAGE, LANES)
    edges = lambda count: ((2 * count * MEMBERS, LANES), f32)
    row_of = lambda dtype: pltpu.VMEM((1, SENS), dtype)
    own, along, across, far, extra, depth, flow, stored = call(
        forecast_kernel, "forecast", [HBM] * 11,
        [((2,) + message, f32), (message, f32), ((2,) + message, f32), edges(1), edges(3), grid, grid, grid],
        [pltpu.VMEM(field.shape, field.dtype) for field in fields[:-1]]
        + [
            pltpu.VMEM(fields[0].shape, bf16),
            pltpu.VMEM((8, 2, MEMBERS * 8, LANES), f32), pltpu.VMEM((8, 2, MEMBERS * 8, LANES), f32),
            pltpu.SMEM((SENS,), jnp.int32), row_of(jnp.int32), row_of(jnp.int32), row_of(f32), row_of(f32),
            pltpu.SemaphoreType.DMA((21,)),
        ],
    )(stay(sensor_cell), as_row(sensor_cell), as_row(sensor_radius), as_row(observed), as_row(sensor_sigma), *fields)
    strip_edges = pltpu.VMEM((2, MEMBERS * 8, LANES), f32)
    flow, late = call(
        flow_kernel, "flow", [HBM] + [VMEM] * 2, [grid, edges(4)],
        [
            pltpu.VMEM(fields[0].shape, bf16), strip_edges, strip_edges, pltpu.SemaphoreType.DMA((MEMBERS // CHUNK,)),
        ],
        aliases={2: 0},
    )(fields[-1], depth, flow)
    arrived = lax.ppermute(along, "strip", backward)
    far = lax.ppermute(far, "strip", onward)
    (joined,) = call(join_kernel, "join", [VMEM] * 4, [((2,) + message, f32)], aliases={0: 0})(across, arrived, far, late)
    joined = lax.ppermute(joined, "strip", swapped)
    (tapers,) = call(
        taper_kernel, "taper", [VMEM], [((ROWS, 2 * SENS, COLS), bf16)], [pltpu.VMEM((1, SENS, COLS), f32)],
    )(own)
    parts, depth, flow, stored = call(
        finish_kernel, "finish", [VMEM] * 10, [((groups * 8, LANES), f32), grid, grid, grid],
        [
            pltpu.VMEM(message, f32), pltpu.VMEM(message, f32), pltpu.VMEM((2, SENS, COLS), f32),
            pltpu.VMEM((ROWS, 4 * SENS, COLS), bf16), pltpu.VMEM((2, ROWS * MEMBERS, LANES), f32),
        ],
        aliases={7: 1, 8: 2, 9: 3},
    )(own, tapers, extra, late, arrived, far, joined, depth, flow, stored)
    turned = [(20 + i) % groups for i in range(groups)]
    shared = lax.all_to_all(parts.reshape(groups, 8, LANES), "dom", 0, 0, tiled=True, axis_index_groups=[turned])
    (rows,) = call(
        lambda *refs: combine_kernel(groups, *refs), "combine", [VMEM], [((groups * 8, LANES), f32)],
    )(shared.reshape(groups * 8, LANES))
    whole = lax.all_to_all(
        rows.reshape(groups, 8, LANES), "dom", 0, 0, tiled=True, axis_index_groups=[turned]
    )
    return tuple(
        call(spread_kernel, "spread", [VMEM], [((ROWS, COLS), f32)] * 3)(whole.reshape(groups * 8, LANES))
    )


def solution(mesh):
    return jax.shard_map(
        local,
        mesh=mesh,
        in_specs=(
            P("dom", "strip", None),
            P("dom", "strip", None),
            P("dom", "strip", None),
            P("strip", None),
            P(None, "dom", "strip", None),
            P(None, "dom", "strip", None),
            P("strip"),
            P("strip"),
            P("strip"),
            P("strip"),
        ),
        out_specs=(P("strip", None), P("strip", None), P("strip", None)),
        check_vma=False,
    )
```

```python
import jax
import jax.numpy as jnp
from jax import lax
from jax.experimental import pallas as pl
from jax.experimental.pallas import tpu as pltpu
from jax.sharding import PartitionSpec as P

advection = 0.4
gravity = 0.5
diffusion = 0.15
friction = 0.3
drainage = 0.1

MEMBERS = 24
ROWS = 32
COLS = 256
SENS = 32
LANES = 128
CHUNK = 8
PITCH = 40
SAMPLED = 6 * MEMBERS
ACROSS = SAMPLED + MEMBERS
MESSAGE = ACROSS + 8

f32 = jnp.float32
bf16 = jnp.bfloat16


def sides(left_half, right_half):
    lane = lax.broadcasted_iota(jnp.int32, left_half.shape, 1)
    first, last = lane == 0, lane == LANES - 1
    left_back, right_back = pltpu.roll(left_half, 1, 1), pltpu.roll(right_half, 1, 1)
    left_on, right_on = pltpu.roll(left_half, LANES - 1, 1), pltpu.roll(right_half, LANES - 1, 1)
    return (
        jnp.where(first, left_half, left_back) + jnp.where(last, right_on, left_on),
        jnp.where(first, left_back, right_back) + jnp.where(last, right_half, right_on),
    )


def spread(field):
    return [diffusion * (around - 2.0 * here) for around, here in zip(sides(*field), field)]


def halves(values):
    return [values[:, :LANES], values[:, LANES:]]


def each(function, *rows):
    return [function(*parts) for parts in zip(*rows)]


def put(ref, slot, row):
    for h in range(2):
        ref[(2 * slot + h) * MEMBERS : (2 * slot + h + 1) * MEMBERS] = row[h]


def get(ref, slot):
    return [ref[(2 * slot + h) * MEMBERS : (2 * slot + h + 1) * MEMBERS] for h in range(2)]


def split(values, pieces):
    stack = []
    for _ in range(pieces):
        piece = values.astype(bf16).astype(f32)
        stack.append(piece)
        values = values - piece
    return jnp.concatenate(stack, axis=0)


def pick(rows, hit):
    left = jnp.concatenate([split(jnp.concatenate(values, axis=1), pieces) for values, pieces in rows], axis=0)
    total = jnp.dot(left.astype(bf16), hit, preferred_element_type=f32)
    found, at = [], 0
    for _, pieces in rows:
        parts = [total[at + i * MEMBERS : at + (i + 1) * MEMBERS] for i in range(pieces)]
        found.append(sum(parts[1:], parts[0]))
        at += pieces * MEMBERS
    return found


def next_flow(flow, depth, noise, row):
    depth_above = jnp.where(row == ROWS - 1, 0.0, pltpu.roll(depth, ROWS - 1, 0))
    return (flow - gravity * (depth_above - depth) + noise) * (1.0 / (1.0 + friction * jnp.abs(flow)))


def forecast_kernel(
    cell_hbm, cells_hbm, radius_hbm, observed_hbm, sigma_hbm,
    surface_hbm, discharge_hbm, storage_hbm, exchange_hbm, depth_noise_hbm, flow_noise_hbm,
    own_ref, along_ref, far_ref, extra_ref, depth_ref, flow_ref, stored_ref,
    surface_ref, discharge_ref, storage_ref, exchange_ref, depth_noise_ref, flow_noise_ref,
    first_ref, last_ref, cell_ref, cells_ref, radius_ref, observed_ref, sigma_ref, sems,
):
    chunks = []
    for c in range(MEMBERS // CHUNK):
        some = pl.ds(c * CHUNK, CHUNK)
        pairs = [
            (ref.at[some], to.at[some])
            for ref, to in ((surface_hbm, surface_ref), (discharge_hbm, discharge_ref), (storage_hbm, storage_ref))
        ] + [
            (depth_noise_hbm.at[:, some], depth_noise_ref.at[:, some]),
            (flow_noise_hbm.at[0, some], flow_noise_ref.at[some]),
        ]
        if c == 0:
            pairs.append((exchange_hbm, exchange_ref))
        chunks.append(pairs)
    chunks.append([
        (cell_hbm, cell_ref), (cells_hbm, cells_ref), (radius_hbm, radius_ref), (observed_hbm, observed_ref),
        (sigma_hbm, sigma_ref),
    ])
    copies, used = [], 0
    for pairs in chunks:
        copies.append([])
        for source, target in pairs:
            copies[-1].append(pltpu.make_async_copy(source, target, sems.at[used]))
            copies[-1][-1].start()
            used += 1

    row = lax.broadcasted_iota(jnp.int32, (ROWS, LANES), 0)

    def member(p, carry):
        edge = pl.ds(pl.multiple_of(p * 8, 8), 8)

        def keep(slot, value):
            for h in range(2):
                first_ref[slot, h, edge] = value[h][:8]
                if slot != 5:
                    last_ref[slot, h, edge] = value[h][ROWS - 8 :]

        depth, flow, stored = [halves(ref[p].astype(f32)) for ref in (surface_ref, discharge_ref, storage_ref)]
        keep(0, depth)
        keep(1, flow)
        keep(2, stored)
        for step in range(2):
            depth_noise = halves(depth_noise_ref[step, p].astype(f32))
            keep(3 + 2 * step, depth_noise)
            beside = sides(*depth)
            for h in range(2):
                flow_below = jnp.where(row == 0, 0.0, pltpu.roll(flow[h], 1, 0))
                inflow = rate[h] * (depth[h] - stored[h])
                depth[h] = (
                    (1.0 - 2.0 * diffusion) * depth[h] + diffusion * beside[h]
                    - advection * (flow[h] - flow_below) - inflow + depth_noise[h]
                )
                stored[h] = (1.0 - drainage) * stored[h] + inflow
            if step == 0:
                flow_noise = halves(flow_noise_ref[p].astype(f32))
                keep(4, flow_noise)
                flow = each(lambda q, d, n: next_flow(q, d, n, row), flow, depth, flow_noise)
        at = pl.ds(pl.multiple_of(p * PITCH, 8), ROWS)
        for ref, value in ((depth_ref, depth), (flow_ref, flow), (stored_ref, stored)):
            for h in range(2):
                ref[h, at] = value[h]
        return carry

    for c in range(MEMBERS // CHUNK):
        for copy in copies[c]:
            copy.wait()
        if c == 0:
            rate = halves(exchange_ref[...].astype(f32))
        lax.fori_loop(c * CHUNK, (c + 1) * CHUNK, member, 0, unroll=4)

    def row_of(ref, slot, row):
        return [ref[slot, h, pl.ds(row, MEMBERS, stride=8)] for h in range(2)]

    def step_one(surface, flow, flow_below, stored, rate, noise):
        return each(
            lambda s, q, b, t, e, n, d: s - advection * (q - b) + d - e * (s - t) + n,
            surface, flow, flow_below, stored, rate, noise, spread(surface),
        )

    nothing = [jnp.zeros((MEMBERS, LANES), f32)] * 2
    rate_0, rate_1, rate_31 = [[r[i : i + 1] for r in rate] for i in (0, 1, ROWS - 1)]
    surface_0, surface_1 = row_of(first_ref, 0, 0), row_of(first_ref, 0, 1)
    flow_0, flow_1 = row_of(first_ref, 1, 0), row_of(first_ref, 1, 1)
    stored_0, stored_1 = row_of(first_ref, 2, 0), row_of(first_ref, 2, 1)
    depth_0 = step_one(surface_0, flow_0, nothing, stored_0, rate_0, row_of(first_ref, 3, 0))
    depth_1 = step_one(surface_1, flow_1, flow_0, stored_1, rate_1, row_of(first_ref, 3, 1))
    stored_next = each(lambda s, t, e: (1.0 - drainage) * t + e * (s - t), surface_0, stored_0, rate_0)
    inverse_0 = each(lambda q: 1.0 / (1.0 + friction * jnp.abs(q)), flow_0)
    flow_part = each(
        lambda q, d, n, i: (q - gravity * d + n) * i, flow_0, depth_1, row_of(first_ref, 4, 0), inverse_0
    )
    up_ref, down_ref = own_ref.at[0], own_ref.at[1]
    put(up_ref, 0, depth_0)
    put(up_ref, 1, each(lambda e, i: 1.0 - e - (advection * gravity) * i, rate_0, inverse_0))
    put(up_ref, 2, each(lambda e, t, n, q: e * t + n - advection * q, rate_0, stored_next, row_of(first_ref, 5, 0), flow_part))
    flow_31 = row_of(last_ref, 1, 7)
    depth_31 = step_one(
        row_of(last_ref, 0, 7), flow_31, row_of(last_ref, 1, 6), row_of(last_ref, 2, 7), rate_31, row_of(last_ref, 3, 7)
    )
    inverse_31 = each(lambda q: 1.0 / (1.0 + friction * jnp.abs(q)), flow_31)
    put(down_ref, 0, flow_31)
    put(down_ref, 1, each(lambda q, d, n, i: (q + gravity * d + n) * i, flow_31, depth_31, row_of(last_ref, 4, 7), inverse_31))
    put(down_ref, 2, each(lambda i: gravity * i, inverse_31))
    put(far_ref, 0, flow_31)
    put(extra_ref, 0, each(lambda i: gravity * i, inverse_0))
    put(extra_ref, 1, each(lambda q, i, d: q + gravity * i * d, flow_part, inverse_0, depth_0))
    put(extra_ref, 2, each(lambda e, z: e + z, rate_0, nothing))
    for copy in copies[-1]:
        copy.wait()
    cells = cells_ref[...]
    reach = radius_ref[...].astype(f32)
    facts = [
        ((cells >> 8) & (ROWS - 1)).astype(f32), (cells & (COLS - 1)).astype(f32), reach * reach,
        (cells >> 13).astype(f32), observed_ref[...], sigma_ref[...], jnp.zeros((2, SENS), f32),
    ]
    facts = jnp.concatenate([jnp.concatenate(facts, axis=0), jnp.ones((8, LANES - SENS), f32)], axis=1)
    lane = lax.broadcasted_iota(jnp.int32, (MEMBERS, LANES), 1)
    hit = (lax.broadcasted_iota(jnp.int32, (COLS, LANES), 0).astype(f32) == facts[1:2]).astype(f32).astype(bf16)
    (slope,) = pick([(each(lambda i: (advection * advection * gravity) * i, inverse_0), 3)], hit)
    sampled = pltpu.roll(jnp.where((facts[0:1] == 1.0) & (lane < SENS), slope, 0.0), SENS, 1)
    for k in range(SENS):
        cell = cell_ref[k]
        found = depth_ref[(cell >> 7) & 1, pl.ds((cell >> 8) & (ROWS - 1), MEMBERS, stride=PITCH)]
        sampled = jnp.where(lane == k, pltpu.roll(found, (k - cell) & (LANES - 1), 1), sampled)
    for i in range(2):
        own_ref[i, SAMPLED:ACROSS] = sampled
        own_ref[i, ACROSS:MESSAGE] = facts
    along_ref[...] = own_ref[(cell_ref[0] >> 13) & 1]


def line(ref, row):
    return [ref[h, pl.ds(row, MEMBERS, stride=PITCH)] for h in range(2)]


def set_line(ref, row, values):
    for h in range(2):
        ref[h, pl.ds(row, MEMBERS, stride=PITCH)] = values[h]


def is_odd(strip):
    return strip - 2.0 * jnp.floor(0.5 * strip) > 0.5


def flow_kernel(
    flow_noise_hbm, own_ref, depth_ref, flow_in, flow_ref, late_ref, across_ref, flow_noise_ref, first_ref, last_ref, sems
):
    del flow_in
    copies = []
    for c in range(MEMBERS // CHUNK):
        some = pl.ds(c * CHUNK, CHUNK)
        copies.append(pltpu.make_async_copy(flow_noise_hbm.at[1, some], flow_noise_ref.at[some], sems.at[c]))
        copies[c].start()
    across_ref[0] = jnp.where(is_odd(own_ref[0, ACROSS + 3 : ACROSS + 4, 0:1]), own_ref[0], own_ref[1])
    for slot, row in ((2, 1), (3, ROWS - 2)):
        put(late_ref, slot, each(lambda q: 1.0 / (1.0 + friction * jnp.abs(q)), line(flow_ref, row)))
    row = lax.broadcasted_iota(jnp.int32, (ROWS, LANES), 0)

    def member(p, carry):
        at, edge = pl.ds(pl.multiple_of(p * PITCH, 8), ROWS), pl.ds(pl.multiple_of(p * 8, 8), 8)
        noise = halves(flow_noise_ref[p].astype(f32))
        for h in range(2):
            first_ref[h, edge] = noise[h][:8]
            last_ref[h, edge] = noise[h][ROWS - 8 :]
            flow_ref[h, at] = next_flow(flow_ref[h, at], depth_ref[h, at], noise[h], row)
        return carry

    for c in range(MEMBERS // CHUNK):
        copies[c].wait()
        lax.fori_loop(c * CHUNK, (c + 1) * CHUNK, member, 0, unroll=4)
    put(late_ref, 0, [first_ref[h, pl.ds(0, MEMBERS, stride=8)] for h in range(2)])
    put(late_ref, 1, [last_ref[h, pl.ds(7, MEMBERS, stride=8)] for h in range(2)])


def join_kernel(across_ref, arrived_ref, far_ref, joined_ref):
    del across_ref, far_ref
    joined_ref[1] = arrived_ref[...]


def taper_terms(entry, offset, strip):
    gap = lax.broadcasted_iota(jnp.int32, (SENS, COLS), 1).astype(f32) - entry[:, 1:2]
    squared = jnp.where(entry[:, 3:4] == strip + offset, entry[:, 2:3], 0.0)
    return squared - gap * gap, jnp.broadcast_to(entry[:, 0:1] + offset * ROWS, (SENS, LANES))


def taper_pieces(near, lines, here):
    gap = here - lines
    gap = gap * gap
    value = jnp.maximum(near - jnp.concatenate([gap, gap], axis=1), 0.0)
    coarse = value.astype(bf16)
    return coarse, (value - coarse.astype(f32)).astype(bf16)


def taper_kernel(own_ref, tapers_ref, near_ref):
    facts = own_ref[0, ACROSS:MESSAGE]
    near_ref[...], lines = taper_terms(jnp.transpose(facts)[:SENS], 0.0, facts[3:4, 0:1])

    def at_row(r, carry):
        tapers_ref[r, :SENS], tapers_ref[r, SENS:] = taper_pieces(near_ref[...], lines, r.astype(f32))
        return carry

    lax.fori_loop(0, ROWS, at_row, 0, unroll=4)


def finish_kernel(
    own_ref, tapers_ref, extra_ref, late_ref, arrived_ref, far_ref, joined_ref, depth_in, flow_in, stored_in,
    out_ref, depth_ref, flow_ref, stored_ref,
    before_ref, after_ref, near_ref, weight_ref,
):
    del depth_in, flow_in, stored_in
    up_ref, down_ref = own_ref.at[0], own_ref.at[1]
    strip = own_ref[0, ACROSS + 3 : ACROSS + 4, 0:1]
    odd = is_odd(strip)
    before_ref[...] = jnp.where(odd, joined_ref[0], joined_ref[1])
    after_ref[...] = jnp.where(odd, joined_ref[1], joined_ref[0])
    has_before = before_ref[ACROSS + 3 : ACROSS + 4, 0:1] == strip - 1.0
    has_after = after_ref[ACROSS + 3 : ACROSS + 4, 0:1] == strip + 1.0
    keep = lambda condition, row: each(lambda v: jnp.where(condition, v, 0.0), row)

    back = keep(has_before, get(before_ref, 0))
    start = each(lambda d, q: d + advection * q, get(up_ref, 0), back)
    back_next = keep(has_before, each(lambda f, i, d: f - i * d, get(before_ref, 1), get(before_ref, 2), start))
    depth_0 = each(
        lambda d, c, s, k, q: d * c + s + k + advection * q,
        start, get(up_ref, 1), spread(start), get(up_ref, 2), back_next,
    )
    turn_0 = get(extra_ref, 0)
    more_1 = each(lambda i, q: (advection * advection) * i * q, turn_0, back)
    depth_1 = each(lambda d, m: d + m, line(depth_ref, 1), more_1)
    flow_0 = each(lambda f, i, q: f + advection * i * q, get(extra_ref, 1), turn_0, back)
    set_line(depth_ref, 0, depth_0)
    set_line(depth_ref, 1, depth_1)
    set_line(flow_ref, 0, each(
        lambda f, a, d, n: (f - gravity * (a - d) + n) * (1.0 / (1.0 + friction * jnp.abs(f))),
        flow_0, depth_1, depth_0, get(late_ref, 0),
    ))
    set_line(flow_ref, 1, each(lambda f, i, m: f + gravity * i * m, line(flow_ref, 1), get(late_ref, 2), more_1))
    set_line(stored_ref, 0, each(lambda t, e, q: t + advection * e * q, line(stored_ref, 0), get(extra_ref, 2), back))
    last = get(down_ref, 0)
    end = keep(has_after, each(lambda d, q: d + advection * q, get(after_ref, 0), last))
    flow_31 = each(lambda f, i, d: f - i * d, get(down_ref, 1), get(down_ref, 2), end)
    depth_32 = keep(has_after, each(
        lambda d, c, s, k, q: d * c + s + k + advection * q,
        end, get(after_ref, 1), spread(end), get(after_ref, 2), flow_31,
    ))
    more_31 = each(lambda i, d: advection * i * d, get(down_ref, 2), end)
    depth_31 = each(lambda d, m: d + m, line(depth_ref, ROWS - 1), more_31)
    set_line(depth_ref, ROWS - 1, depth_31)
    set_line(flow_ref, ROWS - 1, each(
        lambda f, a, d, n: (f - gravity * (a - d) + n) * (1.0 / (1.0 + friction * jnp.abs(f))),
        flow_31, depth_32, depth_31, get(late_ref, 1),
    ))
    set_line(flow_ref, ROWS - 2, each(
        lambda f, i, m: f - gravity * i * m, line(flow_ref, ROWS - 2), get(late_ref, 3), more_31
    ))

    lane = lax.broadcasted_iota(jnp.int32, (1, LANES), 1)
    group = lane // SENS

    def beside(first, end, shift=0):
        parts = (own_ref[0, first:end], before_ref[first:end], after_ref[first:end])
        parts = [pltpu.roll(part, (i * SENS - shift) % LANES, 1) for i, part in enumerate(parts)]
        return jnp.where(group == 0, parts[0], jnp.where(group == 1, parts[1], parts[2]))

    facts = beside(ACROSS, MESSAGE)
    place = facts[0:1]
    hit = (lax.broadcasted_iota(jnp.int32, (COLS, LANES), 0).astype(f32) == facts[1:2]).astype(f32).astype(bf16)

    far = each(lambda a, b: jnp.where(strip > 1.5, jnp.where(odd, a, b), 0.0), get(arrived_ref, 0), get(far_ref, 0))
    beyond_31 = each(lambda i, d: advection * i * d, keep(has_before, get(before_ref, 2)), start)
    wanted = [
        (beyond_31, 3, ROWS - 1.0, 1), (depth_0, 3, 0.0, 0), (more_1, 3, 1.0, 0), (more_31, 3, ROWS - 1.0, 0),
        (depth_32, 3, 0.0, 2), (far, 1, 1.0, 1), (last, 1, 1.0, 2),
    ]
    found = pick([(values, pieces) for values, pieces, _, _ in wanted], hit)
    found = [jnp.where((place == row) & (group == of), value, 0.0) for value, (_, _, row, of) in zip(found, wanted)]
    added, beyond = sum(found[1:5], found[0]), found[5] + found[6]
    known = jnp.where((place == 0.0) & (group != 1), 0.0, beside(SAMPLED, ACROSS))
    found = known + added + beside(SAMPLED, ACROSS, SENS) * beyond
    real = group < 3
    misfit = (found - facts[4:5]) / jnp.where(real, facts[5:6], 1.0)
    lik = jnp.where(real, -0.5 * misfit * misfit / jnp.where(real, facts[2:3], 1.0), 0.0)
    pieces = split(lik, 3)
    pieces = jnp.concatenate(
        [jnp.where(group == 0, pieces, pltpu.roll(pieces, SENS, 1)), pltpu.roll(pieces, LANES - SENS, 1)], axis=1
    )[:, : 6 * SENS].astype(bf16)

    entries = jnp.transpose(facts)
    lines = []
    for part, offset in enumerate((-1.0, 1.0)):
        near_ref[part], rows = taper_terms(entries[(part + 1) * SENS : (part + 2) * SENS], offset, strip)
        lines.append(rows)
    for i in range(ROWS // 8):
        for r in range(8 * i, 8 * i + 8):
            fringe = [taper_pieces(near_ref[part], lines[part], float(r)) for part in range(2)]
            tapers = jnp.concatenate([tapers_ref[r]] + [piece for pieced in zip(*fringe) for piece in pieced], axis=0)
            part = jnp.dot(pieces, tapers, preferred_element_type=f32)
            weight = part[:MEMBERS] + part[MEMBERS : 2 * MEMBERS] + part[2 * MEMBERS :]
            for half in range(2):
                weight_ref[half, r * MEMBERS : (r + 1) * MEMBERS] = weight[:, half * LANES : (half + 1) * LANES]
        for half in range(2):
            weights = [weight_ref[half, pl.ds(8 * i * MEMBERS + p, 8, stride=MEMBERS)] for p in range(MEMBERS)]
            best = weights[0]
            for p in range(1, MEMBERS):
                best = jnp.maximum(best, weights[p])
            sums = [jnp.zeros((8, LANES), f32) for _ in range(4)]
            for p in range(MEMBERS):
                factor = jnp.exp(weights[p] - best)
                at = pl.ds(p * PITCH + 8 * i, 8)
                sums[0] = sums[0] + factor
                sums[1] = sums[1] + factor * depth_ref[half, at]
                sums[2] = sums[2] + factor * flow_ref[half, at]
                sums[3] = sums[3] + factor * stored_ref[half, at]
            inverse = 1.0 / sums[0]
            results = (best + jnp.log(sums[0]), sums[1] * inverse, sums[2] * inverse, sums[3] * inverse)
            for slot, result in enumerate(results):
                out_ref[pl.ds(64 * i + 2 * slot + half, 8, stride=8)] = result


def combine_kernel(groups, in_ref, out_ref):
    def quantity(slot, half):
        return in_ref[pl.ds(2 * slot + half, groups, stride=8)]

    rows = []
    totals = []
    for half in range(2):
        level = quantity(0, half)
        share = jnp.exp(level - jnp.max(level, axis=0, keepdims=True))
        totals.append((share, 1.0 / jnp.sum(share, axis=0, keepdims=True)))
    for slot in range(1, 4):
        for half in range(2):
            share, inverse = totals[half]
            rows.append(jnp.sum(share * quantity(slot, half), axis=0, keepdims=True) * inverse)
    rows.append(jnp.zeros((2, LANES), f32))
    result = jnp.concatenate(rows, axis=0)
    for copy in range(groups):
        out_ref[copy * 8 : (copy + 1) * 8] = result


def spread_kernel(in_ref, depth_ref, flow_ref, stored_ref):
    for slot, ref in enumerate((depth_ref, flow_ref, stored_ref)):
        for half in range(2):
            ref[:, half * LANES : (half + 1) * LANES] = in_ref[pl.ds(2 * slot + half, ROWS, stride=8)]


VMEM = pl.BlockSpec(memory_space=pltpu.VMEM)
HBM = pl.BlockSpec(memory_space=pltpu.HBM)


def call(kernel, name, in_specs, outs, scratch=(), aliases=None):
    return pl.pallas_call(
        kernel,
        name=name,
        in_specs=in_specs,
        out_specs=[VMEM] * len(outs),
        out_shape=[jax.ShapeDtypeStruct(shape, dtype) for shape, dtype in outs],
        scratch_shapes=list(scratch),
        input_output_aliases=aliases or {},
        compiler_params=pltpu.CompilerParams(vmem_limit_bytes=40 * 1024 * 1024),
    )


def local(
    surface, discharge, storage, exchange, depth_perturbation, flow_perturbation,
    sensor_cell, sensor_radius, observed, sensor_sigma,
):
    strips = lax.axis_size("strip")
    groups = lax.axis_size("dom")
    order = list(range(0, strips, 2)) + list(range(strips - 1, 0, -2))
    onward = [(order[i], order[(i + 1) % strips]) for i in range(strips)]
    backward = [(b, a) for a, b in onward]
    swapped = [(i, i ^ 1) for i in range(strips)]
    stay = lambda values: pltpu.with_memory_space_constraint(values, pltpu.HBM)
    as_row = lambda values: stay(values.reshape(1, SENS))
    fields = [stay(f) for f in (surface, discharge, storage, exchange, depth_perturbation, flow_perturbation)]
    grid = ((2, MEMBERS * PITCH, LANES), f32)
    message = (MESSAGE, LANES)
    edges = lambda count: ((2 * count * MEMBERS, LANES), f32)
    row_of = lambda dtype: pltpu.VMEM((1, SENS), dtype)
    own, along, far, extra, depth, flow, stored = call(
        forecast_kernel, "forecast", [HBM] * 11,
        [((2,) + message, f32), (message, f32), edges(1), edges(3), grid, grid, grid],
        [pltpu.VMEM(field.shape, field.dtype) for field in fields[:-1]]
        + [
            pltpu.VMEM(fields[0].shape, bf16),
            pltpu.VMEM((8, 2, MEMBERS * 8, LANES), f32), pltpu.VMEM((8, 2, MEMBERS * 8, LANES), f32),
            pltpu.SMEM((SENS,), jnp.int32), row_of(jnp.int32), row_of(jnp.int32), row_of(f32), row_of(f32),
            pltpu.SemaphoreType.DMA((21,)),
        ],
    )(stay(sensor_cell), as_row(sensor_cell), as_row(sensor_radius), as_row(observed), as_row(sensor_sigma), *fields)
    strip_edges = pltpu.VMEM((2, MEMBERS * 8, LANES), f32)
    flow, late, across = call(
        flow_kernel, "flow", [HBM] + [VMEM] * 3, [grid, edges(4), ((2,) + message, f32)],
        [
            pltpu.VMEM(fields[0].shape, bf16), strip_edges, strip_edges, pltpu.SemaphoreType.DMA((MEMBERS // CHUNK,)),
        ],
        aliases={3: 0},
    )(fields[-1], own, depth, flow)
    arrived = lax.ppermute(along, "strip", backward)
    far = lax.ppermute(far, "strip", onward)
    (joined,) = call(join_kernel, "join", [VMEM] * 3, [((2,) + message, f32)], aliases={0: 0})(across, arrived, far)
    joined = lax.ppermute(joined, "strip", swapped)
    (tapers,) = call(
        taper_kernel, "taper", [VMEM], [((ROWS, 2 * SENS, COLS), bf16)], [pltpu.VMEM((SENS, COLS), f32)],
    )(own)
    parts, depth, flow, stored = call(
        finish_kernel, "finish", [VMEM] * 10, [((groups * 8, LANES), f32), grid, grid, grid],
        [
            pltpu.VMEM(message, f32), pltpu.VMEM(message, f32), pltpu.VMEM((2, SENS, COLS), f32),
 pltpu.VMEM((2, ROWS * MEMBERS, LANES), f32),
        ],
        aliases={7: 1, 8: 2, 9: 3},
    )(own, tapers, extra, late, arrived, far, joined, depth, flow, stored)
    turned = [(20 + i) % groups for i in range(groups)]
    shared = lax.all_to_all(parts.reshape(groups, 8, LANES), "dom", 0, 0, tiled=True, axis_index_groups=[turned])
    (rows,) = call(
        lambda *refs: combine_kernel(groups, *refs), "combine", [VMEM], [((groups * 8, LANES), f32)],
    )(shared.reshape(groups * 8, LANES))
    whole = lax.all_to_all(
        rows.reshape(groups, 8, LANES), "dom", 0, 0, tiled=True, axis_index_groups=[turned]
    )
    return tuple(
        call(spread_kernel, "spread", [VMEM], [((ROWS, COLS), f32)] * 3)(whole.reshape(groups * 8, LANES))
    )


def solution(mesh):
    return jax.shard_map(
        local,
        mesh=mesh,
        in_specs=(
            P("dom", "strip", None),
            P("dom", "strip", None),
            P("dom", "strip", None),
            P("strip", None),
            P(None, "dom", "strip", None),
            P(None, "dom", "strip", None),
            P("strip"),
            P("strip"),
            P("strip"),
            P("strip"),
        ),
        out_specs=(P("strip", None), P("strip", None), P("strip", None)),
        check_vma=False,
    )
```

```python
import jax
import jax.numpy as jnp
from jax import lax
from jax.experimental import pallas as pl
from jax.experimental.pallas import tpu as pltpu
from jax.sharding import PartitionSpec as P

advection = 0.4
gravity = 0.5
diffusion = 0.15
friction = 0.3
drainage = 0.1

MEMBERS = 24
ROWS = 32
COLS = 256
SENS = 32
LANES = 128
CHUNK = 8
PITCH = 40
SAMPLED = 6 * MEMBERS
ACROSS = SAMPLED + MEMBERS
MESSAGE = ACROSS + 8

f32 = jnp.float32
bf16 = jnp.bfloat16


def sides(left_half, right_half):
    lane = lax.broadcasted_iota(jnp.int32, left_half.shape, 1)
    first, last = lane == 0, lane == LANES - 1
    left_back, right_back = pltpu.roll(left_half, 1, 1), pltpu.roll(right_half, 1, 1)
    left_on, right_on = pltpu.roll(left_half, LANES - 1, 1), pltpu.roll(right_half, LANES - 1, 1)
    return (
        jnp.where(first, left_half, left_back) + jnp.where(last, right_on, left_on),
        jnp.where(first, left_back, right_back) + jnp.where(last, right_half, right_on),
    )


def spread(field):
    return [diffusion * (around - 2.0 * here) for around, here in zip(sides(*field), field)]


def halves(values):
    return [values[:, :LANES], values[:, LANES:]]


def each(function, *rows):
    return [function(*parts) for parts in zip(*rows)]


def put(ref, slot, row):
    for h in range(2):
        ref[(2 * slot + h) * MEMBERS : (2 * slot + h + 1) * MEMBERS] = row[h]


def get(ref, slot):
    return [ref[(2 * slot + h) * MEMBERS : (2 * slot + h + 1) * MEMBERS] for h in range(2)]


def split(values, pieces):
    stack = []
    for _ in range(pieces):
        piece = values.astype(bf16).astype(f32)
        stack.append(piece)
        values = values - piece
    return jnp.concatenate(stack, axis=0)


def pick(rows, hit):
    left = jnp.concatenate([split(jnp.concatenate(values, axis=1), pieces) for values, pieces in rows], axis=0)
    total = jnp.dot(left.astype(bf16), hit, preferred_element_type=f32)
    found, at = [], 0
    for _, pieces in rows:
        parts = [total[at + i * MEMBERS : at + (i + 1) * MEMBERS] for i in range(pieces)]
        found.append(sum(parts[1:], parts[0]))
        at += pieces * MEMBERS
    return found


def next_flow(flow, depth, noise, row):
    depth_above = jnp.where(row == ROWS - 1, 0.0, pltpu.roll(depth, ROWS - 1, 0))
    return (flow - gravity * (depth_above - depth) + noise) * (1.0 / (1.0 + friction * jnp.abs(flow)))


def forecast_kernel(
    cell_hbm, cells_hbm, radius_hbm, observed_hbm, sigma_hbm,
    surface_hbm, discharge_hbm, storage_hbm, exchange_hbm, depth_noise_hbm, flow_noise_hbm,
    own_ref, along_ref, far_ref, extra_ref, depth_ref, flow_ref, stored_ref,
    surface_ref, discharge_ref, storage_ref, exchange_ref, depth_noise_ref, flow_noise_ref,
    first_ref, last_ref, cell_ref, cells_ref, radius_ref, observed_ref, sigma_ref, sems,
):
    chunks = []
    for c in range(MEMBERS // CHUNK):
        some = pl.ds(c * CHUNK, CHUNK)
        pairs = [
            (ref.at[some], to.at[some])
            for ref, to in ((surface_hbm, surface_ref), (discharge_hbm, discharge_ref), (storage_hbm, storage_ref))
        ] + [
            (depth_noise_hbm.at[:, some], depth_noise_ref.at[:, some]),
            (flow_noise_hbm.at[0, some], flow_noise_ref.at[some]),
        ]
        if c == 0:
            pairs.append((exchange_hbm, exchange_ref))
        chunks.append(pairs)
    chunks.append([
        (cell_hbm, cell_ref), (cells_hbm, cells_ref), (radius_hbm, radius_ref), (observed_hbm, observed_ref),
        (sigma_hbm, sigma_ref),
    ])
    copies, used = [], 0
    for pairs in chunks:
        copies.append([])
        for source, target in pairs:
            copies[-1].append(pltpu.make_async_copy(source, target, sems.at[used]))
            copies[-1][-1].start()
            used += 1

    row = lax.broadcasted_iota(jnp.int32, (ROWS, LANES), 0)

    def member(p, carry):
        edge = pl.ds(pl.multiple_of(p * 8, 8), 8)

        def keep(slot, value):
            for h in range(2):
                first_ref[slot, h, edge] = value[h][:8]
                if slot != 5:
                    last_ref[slot, h, edge] = value[h][ROWS - 8 :]

        depth, flow, stored = [halves(ref[p].astype(f32)) for ref in (surface_ref, discharge_ref, storage_ref)]
        keep(0, depth)
        keep(1, flow)
        keep(2, stored)
        for step in range(2):
            depth_noise = halves(depth_noise_ref[step, p].astype(f32))
            keep(3 + 2 * step, depth_noise)
            beside = sides(*depth)
            for h in range(2):
                flow_below = jnp.where(row == 0, 0.0, pltpu.roll(flow[h], 1, 0))
                inflow = rate[h] * (depth[h] - stored[h])
                depth[h] = (
                    (1.0 - 2.0 * diffusion) * depth[h] + diffusion * beside[h]
                    - advection * (flow[h] - flow_below) - inflow + depth_noise[h]
                )
                stored[h] = (1.0 - drainage) * stored[h] + inflow
            if step == 0:
                flow_noise = halves(flow_noise_ref[p].astype(f32))
                keep(4, flow_noise)
                flow = each(lambda q, d, n: next_flow(q, d, n, row), flow, depth, flow_noise)
        at = pl.ds(pl.multiple_of(p * PITCH, 8), ROWS)
        for ref, value in ((depth_ref, depth), (flow_ref, flow), (stored_ref, stored)):
            for h in range(2):
                ref[h, at] = value[h]
        return carry

    for c in range(MEMBERS // CHUNK):
        for copy in copies[c]:
            copy.wait()
        if c == 0:
            rate = halves(exchange_ref[...].astype(f32))
        lax.fori_loop(c * CHUNK, (c + 1) * CHUNK, member, 0, unroll=4)

    def row_of(ref, slot, row):
        return [ref[slot, h, pl.ds(row, MEMBERS, stride=8)] for h in range(2)]

    def step_one(surface, flow, flow_below, stored, rate, noise):
        return each(
            lambda s, q, b, t, e, n, d: s - advection * (q - b) + d - e * (s - t) + n,
            surface, flow, flow_below, stored, rate, noise, spread(surface),
        )

    nothing = [jnp.zeros((MEMBERS, LANES), f32)] * 2
    rate_0, rate_1, rate_31 = [[r[i : i + 1] for r in rate] for i in (0, 1, ROWS - 1)]
    surface_0, surface_1 = row_of(first_ref, 0, 0), row_of(first_ref, 0, 1)
    flow_0, flow_1 = row_of(first_ref, 1, 0), row_of(first_ref, 1, 1)
    stored_0, stored_1 = row_of(first_ref, 2, 0), row_of(first_ref, 2, 1)
    depth_0 = step_one(surface_0, flow_0, nothing, stored_0, rate_0, row_of(first_ref, 3, 0))
    depth_1 = step_one(surface_1, flow_1, flow_0, stored_1, rate_1, row_of(first_ref, 3, 1))
    stored_next = each(lambda s, t, e: (1.0 - drainage) * t + e * (s - t), surface_0, stored_0, rate_0)
    inverse_0 = each(lambda q: 1.0 / (1.0 + friction * jnp.abs(q)), flow_0)
    flow_part = each(
        lambda q, d, n, i: (q - gravity * d + n) * i, flow_0, depth_1, row_of(first_ref, 4, 0), inverse_0
    )
    up_ref, down_ref = own_ref.at[0], own_ref.at[1]
    put(up_ref, 0, depth_0)
    put(up_ref, 1, each(lambda e, i: 1.0 - e - (advection * gravity) * i, rate_0, inverse_0))
    put(up_ref, 2, each(lambda e, t, n, q: e * t + n - advection * q, rate_0, stored_next, row_of(first_ref, 5, 0), flow_part))
    flow_31 = row_of(last_ref, 1, 7)
    depth_31 = step_one(
        row_of(last_ref, 0, 7), flow_31, row_of(last_ref, 1, 6), row_of(last_ref, 2, 7), rate_31, row_of(last_ref, 3, 7)
    )
    inverse_31 = each(lambda q: 1.0 / (1.0 + friction * jnp.abs(q)), flow_31)
    put(down_ref, 0, flow_31)
    put(down_ref, 1, each(lambda q, d, n, i: (q + gravity * d + n) * i, flow_31, depth_31, row_of(last_ref, 4, 7), inverse_31))
    put(down_ref, 2, each(lambda i: gravity * i, inverse_31))
    put(far_ref, 0, flow_31)
    put(extra_ref, 0, each(lambda i: gravity * i, inverse_0))
    put(extra_ref, 1, each(lambda q, i, d: q + gravity * i * d, flow_part, inverse_0, depth_0))
    put(extra_ref, 2, each(lambda e, z: e + z, rate_0, nothing))
    for copy in copies[-1]:
        copy.wait()
    cells = cells_ref[...]
    reach = radius_ref[...].astype(f32)
    facts = [
        ((cells >> 8) & (ROWS - 1)).astype(f32), (cells & (COLS - 1)).astype(f32), reach * reach,
        (cells >> 13).astype(f32), observed_ref[...], sigma_ref[...], jnp.zeros((2, SENS), f32),
    ]
    facts = jnp.concatenate([jnp.concatenate(facts, axis=0), jnp.ones((8, LANES - SENS), f32)], axis=1)
    lane = lax.broadcasted_iota(jnp.int32, (MEMBERS, LANES), 1)
    hit = (lax.broadcasted_iota(jnp.int32, (COLS, LANES), 0).astype(f32) == facts[1:2]).astype(f32).astype(bf16)
    (slope,) = pick([(each(lambda i: (advection * advection * gravity) * i, inverse_0), 3)], hit)
    sampled = pltpu.roll(jnp.where((facts[0:1] == 1.0) & (lane < SENS), slope, 0.0), SENS, 1)
    for k in range(SENS):
        cell = cell_ref[k]
        found = depth_ref[(cell >> 7) & 1, pl.ds((cell >> 8) & (ROWS - 1), MEMBERS, stride=PITCH)]
        sampled = jnp.where(lane == k, pltpu.roll(found, (k - cell) & (LANES - 1), 1), sampled)
    for i in range(2):
        own_ref[i, SAMPLED:ACROSS] = sampled
        own_ref[i, ACROSS:MESSAGE] = facts
    along_ref[...] = own_ref[(cell_ref[0] >> 13) & 1]


def line(ref, row):
    return [ref[h, pl.ds(row, MEMBERS, stride=PITCH)] for h in range(2)]


def set_line(ref, row, values):
    for h in range(2):
        ref[h, pl.ds(row, MEMBERS, stride=PITCH)] = values[h]


def is_odd(strip):
    return strip - 2.0 * jnp.floor(0.5 * strip) > 0.5


def flow_kernel(
    flow_noise_hbm, own_ref, depth_ref, flow_in, flow_ref, late_ref, across_ref, flow_noise_ref, first_ref, last_ref, sems
):
    del flow_in
    copies = []
    for c in range(MEMBERS // CHUNK):
        some = pl.ds(c * CHUNK, CHUNK)
        copies.append(pltpu.make_async_copy(flow_noise_hbm.at[1, some], flow_noise_ref.at[some], sems.at[c]))
        copies[c].start()
    across_ref[0] = jnp.where(is_odd(own_ref[0, ACROSS + 3 : ACROSS + 4, 0:1]), own_ref[0], own_ref[1])
    for slot, row in ((2, 1), (3, ROWS - 2)):
        put(late_ref, slot, each(lambda q: 1.0 / (1.0 + friction * jnp.abs(q)), line(flow_ref, row)))
    row = lax.broadcasted_iota(jnp.int32, (ROWS, LANES), 0)

    def member(p, carry):
        at, edge = pl.ds(pl.multiple_of(p * PITCH, 8), ROWS), pl.ds(pl.multiple_of(p * 8, 8), 8)
        noise = halves(flow_noise_ref[p].astype(f32))
        for h in range(2):
            first_ref[h, edge] = noise[h][:8]
            last_ref[h, edge] = noise[h][ROWS - 8 :]
            flow_ref[h, at] = next_flow(flow_ref[h, at], depth_ref[h, at], noise[h], row)
        return carry

    for c in range(MEMBERS // CHUNK):
        copies[c].wait()
        lax.fori_loop(c * CHUNK, (c + 1) * CHUNK, member, 0, unroll=4)
    put(late_ref, 0, [first_ref[h, pl.ds(0, MEMBERS, stride=8)] for h in range(2)])
    put(late_ref, 1, [last_ref[h, pl.ds(7, MEMBERS, stride=8)] for h in range(2)])


def join_kernel(across_ref, arrived_ref, far_ref, joined_ref):
    del across_ref, far_ref
    joined_ref[1] = arrived_ref[...]


def taper_terms(entry, offset, strip):
    gap = lax.broadcasted_iota(jnp.int32, (SENS, COLS), 1).astype(f32) - entry[:, 1:2]
    squared = jnp.where(entry[:, 3:4] == strip + offset, entry[:, 2:3], 0.0)
    return squared - gap * gap, jnp.broadcast_to(entry[:, 0:1] + offset * ROWS, (SENS, LANES))


def taper_pieces(near, lines, here):
    gap = here - lines
    gap = gap * gap
    value = jnp.maximum(near - jnp.concatenate([gap, gap], axis=1), 0.0)
    coarse = value.astype(bf16)
    return coarse, (value - coarse.astype(f32)).astype(bf16)


def taper_kernel(own_ref, tapers_ref, near_ref):
    facts = own_ref[0, ACROSS:MESSAGE]
    near_ref[...], lines = taper_terms(jnp.transpose(facts)[:SENS], 0.0, facts[3:4, 0:1])

    def at_row(r, carry):
        tapers_ref[r, :SENS], tapers_ref[r, SENS:] = taper_pieces(near_ref[...], lines, r.astype(f32))
        return carry

    lax.fori_loop(0, ROWS, at_row, 0, unroll=4)


def finish_kernel(
    own_ref, tapers_ref, extra_ref, late_ref, arrived_ref, far_ref, joined_ref, depth_in, flow_in, stored_in,
    out_ref, depth_ref, flow_ref, stored_ref,
    before_ref, after_ref, near_ref, weight_ref,
):
    del depth_in, flow_in, stored_in
    up_ref, down_ref = own_ref.at[0], own_ref.at[1]
    strip = own_ref[0, ACROSS + 3 : ACROSS + 4, 0:1]
    odd = is_odd(strip)
    before_ref[...] = jnp.where(odd, joined_ref[0], joined_ref[1])
    after_ref[...] = jnp.where(odd, joined_ref[1], joined_ref[0])
    has_before = before_ref[ACROSS + 3 : ACROSS + 4, 0:1] == strip - 1.0
    has_after = after_ref[ACROSS + 3 : ACROSS + 4, 0:1] == strip + 1.0
    keep = lambda condition, row: each(lambda v: jnp.where(condition, v, 0.0), row)

    back = keep(has_before, get(before_ref, 0))
    start = each(lambda d, q: d + advection * q, get(up_ref, 0), back)
    back_next = keep(has_before, each(lambda f, i, d: f - i * d, get(before_ref, 1), get(before_ref, 2), start))
    depth_0 = each(
        lambda d, c, s, k, q: d * c + s + k + advection * q,
        start, get(up_ref, 1), spread(start), get(up_ref, 2), back_next,
    )
    turn_0 = get(extra_ref, 0)
    more_1 = each(lambda i, q: (advection * advection) * i * q, turn_0, back)
    depth_1 = each(lambda d, m: d + m, line(depth_ref, 1), more_1)
    flow_0 = each(lambda f, i, q: f + advection * i * q, get(extra_ref, 1), turn_0, back)
    set_line(depth_ref, 0, depth_0)
    set_line(depth_ref, 1, depth_1)
    set_line(flow_ref, 0, each(
        lambda f, a, d, n: (f - gravity * (a - d) + n) * (1.0 / (1.0 + friction * jnp.abs(f))),
        flow_0, depth_1, depth_0, get(late_ref, 0),
    ))
    set_line(flow_ref, 1, each(lambda f, i, m: f + gravity * i * m, line(flow_ref, 1), get(late_ref, 2), more_1))
    set_line(stored_ref, 0, each(lambda t, e, q: t + advection * e * q, line(stored_ref, 0), get(extra_ref, 2), back))
    last = get(down_ref, 0)
    end = keep(has_after, each(lambda d, q: d + advection * q, get(after_ref, 0), last))
    flow_31 = each(lambda f, i, d: f - i * d, get(down_ref, 1), get(down_ref, 2), end)
    depth_32 = keep(has_after, each(
        lambda d, c, s, k, q: d * c + s + k + advection * q,
        end, get(after_ref, 1), spread(end), get(after_ref, 2), flow_31,
    ))
    more_31 = each(lambda i, d: advection * i * d, get(down_ref, 2), end)
    depth_31 = each(lambda d, m: d + m, line(depth_ref, ROWS - 1), more_31)
    set_line(depth_ref, ROWS - 1, depth_31)
    set_line(flow_ref, ROWS - 1, each(
        lambda f, a, d, n: (f - gravity * (a - d) + n) * (1.0 / (1.0 + friction * jnp.abs(f))),
        flow_31, depth_32, depth_31, get(late_ref, 1),
    ))
    set_line(flow_ref, ROWS - 2, each(
        lambda f, i, m: f - gravity * i * m, line(flow_ref, ROWS - 2), get(late_ref, 3), more_31
    ))

    lane = lax.broadcasted_iota(jnp.int32, (1, LANES), 1)
    group = lane // SENS

    def beside(first, end, shift=0):
        parts = (own_ref[0, first:end], before_ref[first:end], after_ref[first:end])
        parts = [pltpu.roll(part, (i * SENS - shift) % LANES, 1) for i, part in enumerate(parts)]
        return jnp.where(group == 0, parts[0], jnp.where(group == 1, parts[1], parts[2]))

    facts = beside(ACROSS, MESSAGE)
    place = facts[0:1]
    hit = (lax.broadcasted_iota(jnp.int32, (COLS, LANES), 0).astype(f32) == facts[1:2]).astype(f32).astype(bf16)

    far = each(lambda a, b: jnp.where(strip > 1.5, jnp.where(odd, a, b), 0.0), get(arrived_ref, 0), get(far_ref, 0))
    beyond_31 = each(lambda i, d: advection * i * d, keep(has_before, get(before_ref, 2)), start)
    wanted = [
        (beyond_31, 3, ROWS - 1.0, 1), (depth_0, 3, 0.0, 0), (more_1, 3, 1.0, 0), (more_31, 3, ROWS - 1.0, 0),
        (depth_32, 3, 0.0, 2), (far, 1, 1.0, 1), (last, 1, 1.0, 2),
    ]
    found = pick([(values, pieces) for values, pieces, _, _ in wanted], hit)
    found = [jnp.where((place == row) & (group == of), value, 0.0) for value, (_, _, row, of) in zip(found, wanted)]
    added, beyond = sum(found[1:5], found[0]), found[5] + found[6]
    known = jnp.where((place == 0.0) & (group != 1), 0.0, beside(SAMPLED, ACROSS))
    found = known + added + beside(SAMPLED, ACROSS, SENS) * beyond
    real = group < 3
    misfit = (found - facts[4:5]) / jnp.where(real, facts[5:6], 1.0)
    lik = jnp.where(real, -0.5 * misfit * misfit / jnp.where(real, facts[2:3], 1.0), 0.0)
    pieces = split(lik, 3)
    pieces = jnp.concatenate(
        [jnp.where(group == 0, pieces, pltpu.roll(pieces, SENS, 1)), pltpu.roll(pieces, LANES - SENS, 1)], axis=1
    )[:, : 6 * SENS].astype(bf16)

    entries = jnp.transpose(facts)
    lines = []
    for part, offset in enumerate((-1.0, 1.0)):
        near_ref[part], rows = taper_terms(entries[(part + 1) * SENS : (part + 2) * SENS], offset, strip)
        lines.append(rows)
    for i in range(ROWS // 8):
        for r in range(8 * i, 8 * i + 8):
            fringe = [taper_pieces(near_ref[part], lines[part], float(r)) for part in range(2)]
            tapers = jnp.concatenate([tapers_ref[r]] + [piece for pieced in zip(*fringe) for piece in pieced], axis=0)
            part = jnp.dot(pieces, tapers, preferred_element_type=f32)
            weight = part[:MEMBERS] + part[MEMBERS : 2 * MEMBERS] + part[2 * MEMBERS :]
            for half in range(2):
                weight_ref[half, r * MEMBERS : (r + 1) * MEMBERS] = weight[:, half * LANES : (half + 1) * LANES]
        for half in range(2):
            weights = [weight_ref[half, pl.ds(8 * i * MEMBERS + p, 8, stride=MEMBERS)] for p in range(MEMBERS)]
            best = weights[0]
            for p in range(1, MEMBERS):
                best = jnp.maximum(best, weights[p])
            sums = [jnp.zeros((8, LANES), f32) for _ in range(4)]
            for p in range(MEMBERS):
                factor = jnp.exp(weights[p] - best)
                at = pl.ds(p * PITCH + 8 * i, 8)
                sums[0] = sums[0] + factor
                sums[1] = sums[1] + factor * depth_ref[half, at]
                sums[2] = sums[2] + factor * flow_ref[half, at]
                sums[3] = sums[3] + factor * stored_ref[half, at]
            inverse = 1.0 / sums[0]
            results = (best + jnp.log(sums[0]), sums[1] * inverse, sums[2] * inverse, sums[3] * inverse)
            for slot, result in enumerate(results):
                out_ref[pl.ds(64 * i + 2 * slot + half, 8, stride=8)] = result


def combine_kernel(groups, in_ref, out_ref):
    def quantity(slot, half):
        return in_ref[pl.ds(2 * slot + half, groups, stride=8)]

    rows = []
    totals = []
    for half in range(2):
        level = quantity(0, half)
        share = jnp.exp(level - jnp.max(level, axis=0, keepdims=True))
        totals.append((share, 1.0 / jnp.sum(share, axis=0, keepdims=True)))
    for slot in range(1, 4):
        for half in range(2):
            share, inverse = totals[half]
            rows.append(jnp.sum(share * quantity(slot, half), axis=0, keepdims=True) * inverse)
    rows.append(jnp.zeros((2, LANES), f32))
    result = jnp.concatenate(rows, axis=0)
    for copy in range(groups):
        out_ref[copy * 8 : (copy + 1) * 8] = result


def spread_kernel(in_ref, depth_ref, flow_ref, stored_ref):
    for slot, ref in enumerate((depth_ref, flow_ref, stored_ref)):
        for half in range(2):
            ref[:, half * LANES : (half + 1) * LANES] = in_ref[pl.ds(2 * slot + half, ROWS, stride=8)]


VMEM = pl.BlockSpec(memory_space=pltpu.VMEM)
HBM = pl.BlockSpec(memory_space=pltpu.HBM)


def call(kernel, name, in_specs, outs, scratch=(), aliases=None):
    return pl.pallas_call(
        kernel,
        name=name,
        in_specs=in_specs,
        out_specs=[VMEM] * len(outs),
        out_shape=[jax.ShapeDtypeStruct(shape, dtype) for shape, dtype in outs],
        scratch_shapes=list(scratch),
        input_output_aliases=aliases or {},
        compiler_params=pltpu.CompilerParams(vmem_limit_bytes=40 * 1024 * 1024),
    )


def local(
    surface, discharge, storage, exchange, depth_perturbation, flow_perturbation,
    sensor_cell, sensor_radius, observed, sensor_sigma,
):
    strips = lax.axis_size("strip")
    groups = lax.axis_size("dom")
    order = list(range(0, strips, 2)) + list(range(strips - 1, 0, -2))
    onward = [(order[i], order[(i + 1) % strips]) for i in range(strips)]
    backward = [(b, a) for a, b in onward]
    swapped = [(i, i ^ 1) for i in range(strips)]
    stay = lambda values: pltpu.with_memory_space_constraint(values, pltpu.HBM)
    as_row = lambda values: stay(values.reshape(1, SENS))
    fields = [stay(f) for f in (surface, discharge, storage, exchange, depth_perturbation, flow_perturbation)]
    grid = ((2, MEMBERS * PITCH + ROWS, LANES), f32)
    message = (MESSAGE, LANES)
    edges = lambda count: ((2 * count * MEMBERS, LANES), f32)
    row_of = lambda dtype: pltpu.VMEM((1, SENS), dtype)
    own, along, far, extra, depth, flow, stored = call(
        forecast_kernel, "forecast", [HBM] * 11,
        [((2,) + message, f32), (message, f32), edges(1), edges(3), grid, grid, grid],
        [pltpu.VMEM(field.shape, field.dtype) for field in fields[:-1]]
        + [
            pltpu.VMEM(fields[0].shape, bf16),
            pltpu.VMEM((8, 2, MEMBERS * 8, LANES), f32), pltpu.VMEM((8, 2, MEMBERS * 8, LANES), f32),
            pltpu.SMEM((SENS,), jnp.int32), row_of(jnp.int32), row_of(jnp.int32), row_of(f32), row_of(f32),
            pltpu.SemaphoreType.DMA((21,)),
        ],
    )(stay(sensor_cell), as_row(sensor_cell), as_row(sensor_radius), as_row(observed), as_row(sensor_sigma), *fields)
    strip_edges = pltpu.VMEM((2, MEMBERS * 8, LANES), f32)
    flow, late, across = call(
        flow_kernel, "flow", [HBM] + [VMEM] * 3, [grid, edges(4), ((2,) + message, f32)],
        [
            pltpu.VMEM(fields[0].shape, bf16), strip_edges, strip_edges, pltpu.SemaphoreType.DMA((MEMBERS // CHUNK,)),
        ],
        aliases={3: 0},
    )(fields[-1], own, depth, flow)
    arrived = lax.ppermute(along, "strip", backward)
    far = lax.ppermute(far, "strip", onward)
    (joined,) = call(join_kernel, "join", [VMEM] * 3, [((2,) + message, f32)], aliases={0: 0})(across, arrived, far)
    joined = lax.ppermute(joined, "strip", swapped)
    (tapers,) = call(
        taper_kernel, "taper", [VMEM], [((ROWS, 2 * SENS, COLS), bf16)], [pltpu.VMEM((SENS, COLS), f32)],
    )(own)
    parts, depth, flow, stored = call(
        finish_kernel, "finish", [VMEM] * 10, [((groups * 8, LANES), f32), grid, grid, grid],
        [
            pltpu.VMEM(message, f32), pltpu.VMEM(message, f32), pltpu.VMEM((2, SENS, COLS), f32),
 pltpu.VMEM((2, ROWS * MEMBERS, LANES), f32),
        ],
        aliases={7: 1, 8: 2, 9: 3},
    )(own, tapers, extra, late, arrived, far, joined, depth, flow, stored)
    turned = [(20 + i) % groups for i in range(groups)]
    shared = lax.all_to_all(parts.reshape(groups, 8, LANES), "dom", 0, 0, tiled=True, axis_index_groups=[turned])
    (rows,) = call(
        lambda *refs: combine_kernel(groups, *refs), "combine", [VMEM], [((groups * 8, LANES), f32)],
    )(shared.reshape(groups * 8, LANES))
    whole = lax.all_to_all(
        rows.reshape(groups, 8, LANES), "dom", 0, 0, tiled=True, axis_index_groups=[turned]
    )
    return tuple(
        call(spread_kernel, "spread", [VMEM], [((ROWS, COLS), f32)] * 3)(whole.reshape(groups * 8, LANES))
    )


def solution(mesh):
    return jax.shard_map(
        local,
        mesh=mesh,
        in_specs=(
            P("dom", "strip", None),
            P("dom", "strip", None),
            P("dom", "strip", None),
            P("strip", None),
            P(None, "dom", "strip", None),
            P(None, "dom", "strip", None),
            P("strip"),
            P("strip"),
            P("strip"),
            P("strip"),
        ),
        out_specs=(P("strip", None), P("strip", None), P("strip", None)),
        check_vma=False,
    )
```

```python
import jax
import jax.numpy as jnp
from jax import lax
from jax.experimental import pallas as pl
from jax.experimental.pallas import tpu as pltpu
from jax.sharding import PartitionSpec as P

advection = 0.4
gravity = 0.5
diffusion = 0.15
friction = 0.3
drainage = 0.1

MEMBERS = 24
ROWS = 32
COLS = 256
SENS = 32
LANES = 128
CHUNK = 8
PITCH = 40
SAMPLED = 6 * MEMBERS
ACROSS = SAMPLED + MEMBERS
MESSAGE = ACROSS + 8

f32 = jnp.float32
bf16 = jnp.bfloat16


def sides(left_half, right_half):
    lane = lax.broadcasted_iota(jnp.int32, left_half.shape, 1)
    first, last = lane == 0, lane == LANES - 1
    left_back, right_back = pltpu.roll(left_half, 1, 1), pltpu.roll(right_half, 1, 1)
    left_on, right_on = pltpu.roll(left_half, LANES - 1, 1), pltpu.roll(right_half, LANES - 1, 1)
    return (
        jnp.where(first, left_half, left_back) + jnp.where(last, right_on, left_on),
        jnp.where(first, left_back, right_back) + jnp.where(last, right_half, right_on),
    )


def spread(field):
    return [diffusion * (around - 2.0 * here) for around, here in zip(sides(*field), field)]


def halves(values):
    return [values[:, :LANES], values[:, LANES:]]


def each(function, *rows):
    return [function(*parts) for parts in zip(*rows)]


def put(ref, slot, row):
    for h in range(2):
        ref[(2 * slot + h) * MEMBERS : (2 * slot + h + 1) * MEMBERS] = row[h]


def get(ref, slot):
    return [ref[(2 * slot + h) * MEMBERS : (2 * slot + h + 1) * MEMBERS] for h in range(2)]


def split(values, pieces):
    stack = []
    for _ in range(pieces):
        piece = values.astype(bf16).astype(f32)
        stack.append(piece)
        values = values - piece
    return jnp.concatenate(stack, axis=0)


def pick(rows, hit):
    left = jnp.concatenate([split(jnp.concatenate(values, axis=1), pieces) for values, pieces in rows], axis=0)
    total = jnp.dot(left.astype(bf16), hit, preferred_element_type=f32)
    found, at = [], 0
    for _, pieces in rows:
        parts = [total[at + i * MEMBERS : at + (i + 1) * MEMBERS] for i in range(pieces)]
        found.append(sum(parts[1:], parts[0]))
        at += pieces * MEMBERS
    return found


def next_flow(flow, depth, noise, row):
    depth_above = jnp.where(row == ROWS - 1, 0.0, pltpu.roll(depth, ROWS - 1, 0))
    return (flow - gravity * (depth_above - depth) + noise) * (1.0 / (1.0 + friction * jnp.abs(flow)))


def forecast_kernel(
    cell_hbm, cells_hbm, radius_hbm, observed_hbm, sigma_hbm,
    surface_hbm, discharge_hbm, storage_hbm, exchange_hbm, depth_noise_hbm, flow_noise_hbm,
    own_ref, along_ref, far_ref, extra_ref, depth_ref, flow_ref, stored_ref,
    surface_ref, discharge_ref, storage_ref, exchange_ref, depth_noise_ref, flow_noise_ref,
    first_ref, last_ref, cell_ref, cells_ref, radius_ref, observed_ref, sigma_ref, sems,
):
    chunks = []
    for c in range(MEMBERS // CHUNK):
        some = pl.ds(c * CHUNK, CHUNK)
        pairs = [
            (ref.at[some], to.at[some])
            for ref, to in ((surface_hbm, surface_ref), (discharge_hbm, discharge_ref), (storage_hbm, storage_ref))
        ] + [
            (depth_noise_hbm.at[:, some], depth_noise_ref.at[:, some]),
            (flow_noise_hbm.at[0, some], flow_noise_ref.at[some]),
        ]
        if c == 0:
            pairs.append((exchange_hbm, exchange_ref))
        chunks.append(pairs)
    chunks.append([
        (cell_hbm, cell_ref), (cells_hbm, cells_ref), (radius_hbm, radius_ref), (observed_hbm, observed_ref),
        (sigma_hbm, sigma_ref),
    ])
    copies, used = [], 0
    for pairs in chunks:
        copies.append([])
        for source, target in pairs:
            copies[-1].append(pltpu.make_async_copy(source, target, sems.at[used]))
            copies[-1][-1].start()
            used += 1

    row = lax.broadcasted_iota(jnp.int32, (ROWS, LANES), 0)

    def member(p, carry):
        edge = pl.ds(pl.multiple_of(p * 8, 8), 8)

        def keep(slot, value):
            for h in range(2):
                first_ref[slot, h, edge] = value[h][:8]
                if slot != 5:
                    last_ref[slot, h, edge] = value[h][ROWS - 8 :]

        depth, flow, stored = [halves(ref[p].astype(f32)) for ref in (surface_ref, discharge_ref, storage_ref)]
        keep(0, depth)
        keep(1, flow)
        keep(2, stored)
        for step in range(2):
            depth_noise = halves(depth_noise_ref[step, p].astype(f32))
            keep(3 + 2 * step, depth_noise)
            beside = sides(*depth)
            for h in range(2):
                flow_below = jnp.where(row == 0, 0.0, pltpu.roll(flow[h], 1, 0))
                inflow = rate[h] * (depth[h] - stored[h])
                depth[h] = (
                    (1.0 - 2.0 * diffusion) * depth[h] + diffusion * beside[h]
                    - advection * (flow[h] - flow_below) - inflow + depth_noise[h]
                )
                stored[h] = (1.0 - drainage) * stored[h] + inflow
            if step == 0:
                flow_noise = halves(flow_noise_ref[p].astype(f32))
                keep(4, flow_noise)
                flow = each(lambda q, d, n: next_flow(q, d, n, row), flow, depth, flow_noise)
        at = pl.ds(pl.multiple_of(p * PITCH, 8), ROWS)
        for ref, value in ((depth_ref, depth), (flow_ref, flow), (stored_ref, stored)):
            for h in range(2):
                ref[h, at] = value[h]
        return carry

    for c in range(MEMBERS // CHUNK):
        for copy in copies[c]:
            copy.wait()
        if c == 0:
            rate = halves(exchange_ref[...].astype(f32))
        lax.fori_loop(c * CHUNK, (c + 1) * CHUNK, member, 0, unroll=4)

    def row_of(ref, slot, row):
        return [ref[slot, h, pl.ds(row, MEMBERS, stride=8)] for h in range(2)]

    def step_one(surface, flow, flow_below, stored, rate, noise):
        return each(
            lambda s, q, b, t, e, n, d: s - advection * (q - b) + d - e * (s - t) + n,
            surface, flow, flow_below, stored, rate, noise, spread(surface),
        )

    nothing = [jnp.zeros((MEMBERS, LANES), f32)] * 2
    rate_0, rate_1, rate_31 = [[r[i : i + 1] for r in rate] for i in (0, 1, ROWS - 1)]
    surface_0, surface_1 = row_of(first_ref, 0, 0), row_of(first_ref, 0, 1)
    flow_0, flow_1 = row_of(first_ref, 1, 0), row_of(first_ref, 1, 1)
    stored_0, stored_1 = row_of(first_ref, 2, 0), row_of(first_ref, 2, 1)
    depth_0 = step_one(surface_0, flow_0, nothing, stored_0, rate_0, row_of(first_ref, 3, 0))
    depth_1 = step_one(surface_1, flow_1, flow_0, stored_1, rate_1, row_of(first_ref, 3, 1))
    stored_next = each(lambda s, t, e: (1.0 - drainage) * t + e * (s - t), surface_0, stored_0, rate_0)
    inverse_0 = each(lambda q: 1.0 / (1.0 + friction * jnp.abs(q)), flow_0)
    flow_part = each(
        lambda q, d, n, i: (q - gravity * d + n) * i, flow_0, depth_1, row_of(first_ref, 4, 0), inverse_0
    )
    up_ref, down_ref = own_ref.at[0], own_ref.at[1]
    put(up_ref, 0, depth_0)
    put(up_ref, 1, each(lambda e, i: 1.0 - e - (advection * gravity) * i, rate_0, inverse_0))
    put(up_ref, 2, each(lambda e, t, n, q: e * t + n - advection * q, rate_0, stored_next, row_of(first_ref, 5, 0), flow_part))
    flow_31 = row_of(last_ref, 1, 7)
    depth_31 = step_one(
        row_of(last_ref, 0, 7), flow_31, row_of(last_ref, 1, 6), row_of(last_ref, 2, 7), rate_31, row_of(last_ref, 3, 7)
    )
    inverse_31 = each(lambda q: 1.0 / (1.0 + friction * jnp.abs(q)), flow_31)
    put(down_ref, 0, flow_31)
    put(down_ref, 1, each(lambda q, d, n, i: (q + gravity * d + n) * i, flow_31, depth_31, row_of(last_ref, 4, 7), inverse_31))
    put(down_ref, 2, each(lambda i: gravity * i, inverse_31))
    put(far_ref, 0, flow_31)
    put(extra_ref, 0, each(lambda i: gravity * i, inverse_0))
    put(extra_ref, 1, each(lambda q, i, d: q + gravity * i * d, flow_part, inverse_0, depth_0))
    put(extra_ref, 2, each(lambda e, z: e + z, rate_0, nothing))
    for copy in copies[-1]:
        copy.wait()
    cells = cells_ref[...]
    reach = radius_ref[...].astype(f32)
    facts = [
        ((cells >> 8) & (ROWS - 1)).astype(f32), (cells & (COLS - 1)).astype(f32), reach * reach,
        (cells >> 13).astype(f32), observed_ref[...], sigma_ref[...], jnp.zeros((2, SENS), f32),
    ]
    facts = jnp.concatenate([jnp.concatenate(facts, axis=0), jnp.ones((8, LANES - SENS), f32)], axis=1)
    lane = lax.broadcasted_iota(jnp.int32, (MEMBERS, LANES), 1)
    hit = (lax.broadcasted_iota(jnp.int32, (COLS, LANES), 0).astype(f32) == facts[1:2]).astype(f32).astype(bf16)
    (slope,) = pick([(each(lambda i: (advection * advection * gravity) * i, inverse_0), 3)], hit)
    sampled = pltpu.roll(jnp.where((facts[0:1] == 1.0) & (lane < SENS), slope, 0.0), SENS, 1)
    for k in range(SENS):
        cell = cell_ref[k]
        found = depth_ref[(cell >> 7) & 1, pl.ds((cell >> 8) & (ROWS - 1), MEMBERS, stride=PITCH)]
        sampled = jnp.where(lane == k, pltpu.roll(found, (k - cell) & (LANES - 1), 1), sampled)
    for i in range(2):
        own_ref[i, SAMPLED:ACROSS] = sampled
        own_ref[i, ACROSS:MESSAGE] = facts
    along_ref[...] = own_ref[(cell_ref[0] >> 13) & 1]


def line(ref, row):
    return [ref[h, pl.ds(row, MEMBERS, stride=PITCH)] for h in range(2)]


def set_line(ref, row, values):
    for h in range(2):
        ref[h, pl.ds(row, MEMBERS, stride=PITCH)] = values[h]


def is_odd(strip):
    return strip - 2.0 * jnp.floor(0.5 * strip) > 0.5


def flow_kernel(
    flow_noise_hbm, own_ref, depth_ref, flow_in, flow_ref, late_ref, across_ref, flow_noise_ref, first_ref, last_ref, sems
):
    del flow_in
    copies = []
    for c in range(MEMBERS // CHUNK):
        some = pl.ds(c * CHUNK, CHUNK)
        copies.append(pltpu.make_async_copy(flow_noise_hbm.at[1, some], flow_noise_ref.at[some], sems.at[c]))
        copies[c].start()
    across_ref[0] = jnp.where(is_odd(own_ref[0, ACROSS + 3 : ACROSS + 4, 0:1]), own_ref[0], own_ref[1])
    for slot, row in ((2, 1), (3, ROWS - 2)):
        put(late_ref, slot, each(lambda q: 1.0 / (1.0 + friction * jnp.abs(q)), line(flow_ref, row)))
    row = lax.broadcasted_iota(jnp.int32, (ROWS, LANES), 0)

    def member(p, carry):
        at, edge = pl.ds(pl.multiple_of(p * PITCH, 8), ROWS), pl.ds(pl.multiple_of(p * 8, 8), 8)
        noise = halves(flow_noise_ref[p].astype(f32))
        for h in range(2):
            first_ref[h, edge] = noise[h][:8]
            last_ref[h, edge] = noise[h][ROWS - 8 :]
            flow_ref[h, at] = next_flow(flow_ref[h, at], depth_ref[h, at], noise[h], row)
        return carry

    for c in range(MEMBERS // CHUNK):
        copies[c].wait()
        lax.fori_loop(c * CHUNK, (c + 1) * CHUNK, member, 0, unroll=4)
    put(late_ref, 0, [first_ref[h, pl.ds(0, MEMBERS, stride=8)] for h in range(2)])
    put(late_ref, 1, [last_ref[h, pl.ds(7, MEMBERS, stride=8)] for h in range(2)])


def join_kernel(across_ref, arrived_ref, far_ref, joined_ref):
    del across_ref, far_ref
    joined_ref[1] = arrived_ref[...]


def taper_terms(entry, offset, strip):
    gap = lax.broadcasted_iota(jnp.int32, (SENS, COLS), 1).astype(f32) - entry[:, 1:2]
    squared = jnp.where(entry[:, 3:4] == strip + offset, entry[:, 2:3], 0.0)
    return squared - gap * gap, jnp.broadcast_to(entry[:, 0:1] + offset * ROWS, (SENS, LANES))


def taper_pieces(near, lines, here):
    gap = here - lines
    gap = gap * gap
    value = jnp.maximum(near - jnp.concatenate([gap, gap], axis=1), 0.0)
    coarse = value.astype(bf16)
    return coarse, (value - coarse.astype(f32)).astype(bf16)


def taper_kernel(own_ref, tapers_ref, near_ref):
    facts = own_ref[0, ACROSS:MESSAGE]
    near_ref[...], lines = taper_terms(jnp.transpose(facts)[:SENS], 0.0, facts[3:4, 0:1])

    def at_row(r, carry):
        tapers_ref[r, :SENS], tapers_ref[r, SENS:] = taper_pieces(near_ref[...], lines, r.astype(f32))
        return carry

    lax.fori_loop(0, ROWS, at_row, 0, unroll=4)


def finish_kernel(
    own_ref, tapers_ref, extra_ref, late_ref, arrived_ref, far_ref, joined_ref, depth_in, flow_in, stored_in,
    out_ref, depth_ref, flow_ref, stored_ref,
    near_ref, weight_ref,
):
    del depth_in, flow_in, stored_in
    up_ref, down_ref = own_ref.at[0], own_ref.at[1]
    strip = own_ref[0, ACROSS + 3 : ACROSS + 4, 0:1]
    odd = is_odd(strip)
    parity = lax.axis_index("strip") & 1
    before_ref, after_ref = joined_ref.at[1 - parity], joined_ref.at[parity]
    has_before = before_ref[ACROSS + 3 : ACROSS + 4, 0:1] == strip - 1.0
    has_after = after_ref[ACROSS + 3 : ACROSS + 4, 0:1] == strip + 1.0
    keep = lambda condition, row: each(lambda v: jnp.where(condition, v, 0.0), row)

    back = keep(has_before, get(before_ref, 0))
    start = each(lambda d, q: d + advection * q, get(up_ref, 0), back)
    back_next = keep(has_before, each(lambda f, i, d: f - i * d, get(before_ref, 1), get(before_ref, 2), start))
    depth_0 = each(
        lambda d, c, s, k, q: d * c + s + k + advection * q,
        start, get(up_ref, 1), spread(start), get(up_ref, 2), back_next,
    )
    turn_0 = get(extra_ref, 0)
    more_1 = each(lambda i, q: (advection * advection) * i * q, turn_0, back)
    depth_1 = each(lambda d, m: d + m, line(depth_ref, 1), more_1)
    flow_0 = each(lambda f, i, q: f + advection * i * q, get(extra_ref, 1), turn_0, back)
    set_line(depth_ref, 0, depth_0)
    set_line(depth_ref, 1, depth_1)
    set_line(flow_ref, 0, each(
        lambda f, a, d, n: (f - gravity * (a - d) + n) * (1.0 / (1.0 + friction * jnp.abs(f))),
        flow_0, depth_1, depth_0, get(late_ref, 0),
    ))
    set_line(flow_ref, 1, each(lambda f, i, m: f + gravity * i * m, line(flow_ref, 1), get(late_ref, 2), more_1))
    set_line(stored_ref, 0, each(lambda t, e, q: t + advection * e * q, line(stored_ref, 0), get(extra_ref, 2), back))
    last = get(down_ref, 0)
    end = keep(has_after, each(lambda d, q: d + advection * q, get(after_ref, 0), last))
    flow_31 = each(lambda f, i, d: f - i * d, get(down_ref, 1), get(down_ref, 2), end)
    depth_32 = keep(has_after, each(
        lambda d, c, s, k, q: d * c + s + k + advection * q,
        end, get(after_ref, 1), spread(end), get(after_ref, 2), flow_31,
    ))
    more_31 = each(lambda i, d: advection * i * d, get(down_ref, 2), end)
    depth_31 = each(lambda d, m: d + m, line(depth_ref, ROWS - 1), more_31)
    set_line(depth_ref, ROWS - 1, depth_31)
    set_line(flow_ref, ROWS - 1, each(
        lambda f, a, d, n: (f - gravity * (a - d) + n) * (1.0 / (1.0 + friction * jnp.abs(f))),
        flow_31, depth_32, depth_31, get(late_ref, 1),
    ))
    set_line(flow_ref, ROWS - 2, each(
        lambda f, i, m: f - gravity * i * m, line(flow_ref, ROWS - 2), get(late_ref, 3), more_31
    ))

    lane = lax.broadcasted_iota(jnp.int32, (1, LANES), 1)
    group = lane // SENS

    def beside(first, end, shift=0):
        parts = (own_ref[0, first:end], before_ref[first:end], after_ref[first:end])
        parts = [pltpu.roll(part, (i * SENS - shift) % LANES, 1) for i, part in enumerate(parts)]
        return jnp.where(group == 0, parts[0], jnp.where(group == 1, parts[1], parts[2]))

    facts = beside(ACROSS, MESSAGE)
    place = facts[0:1]
    hit = (lax.broadcasted_iota(jnp.int32, (COLS, LANES), 0).astype(f32) == facts[1:2]).astype(f32).astype(bf16)

    far = each(lambda a, b: jnp.where(strip > 1.5, jnp.where(odd, a, b), 0.0), get(arrived_ref, 0), get(far_ref, 0))
    beyond_31 = each(lambda i, d: advection * i * d, keep(has_before, get(before_ref, 2)), start)
    wanted = [
        (beyond_31, 3, ROWS - 1.0, 1), (depth_0, 3, 0.0, 0), (more_1, 3, 1.0, 0), (more_31, 3, ROWS - 1.0, 0),
        (depth_32, 3, 0.0, 2), (far, 1, 1.0, 1), (last, 1, 1.0, 2),
    ]
    found = pick([(values, pieces) for values, pieces, _, _ in wanted], hit)
    found = [jnp.where((place == row) & (group == of), value, 0.0) for value, (_, _, row, of) in zip(found, wanted)]
    added, beyond = sum(found[1:5], found[0]), found[5] + found[6]
    known = jnp.where((place == 0.0) & (group != 1), 0.0, beside(SAMPLED, ACROSS))
    found = known + added + beside(SAMPLED, ACROSS, SENS) * beyond
    real = group < 3
    misfit = (found - facts[4:5]) / jnp.where(real, facts[5:6], 1.0)
    lik = jnp.where(real, -0.5 * misfit * misfit / jnp.where(real, facts[2:3], 1.0), 0.0)
    pieces = split(lik, 3)
    pieces = jnp.concatenate(
        [jnp.where(group == 0, pieces, pltpu.roll(pieces, SENS, 1)), pltpu.roll(pieces, LANES - SENS, 1)], axis=1
    )[:, : 6 * SENS].astype(bf16)

    entries = jnp.transpose(facts)
    lines = []
    for part, offset in enumerate((-1.0, 1.0)):
        near_ref[part], rows = taper_terms(entries[(part + 1) * SENS : (part + 2) * SENS], offset, strip)
        lines.append(rows)
    for i in range(ROWS // 8):
        for r in range(8 * i, 8 * i + 8):
            fringe = [taper_pieces(near_ref[part], lines[part], float(r)) for part in range(2)]
            tapers = jnp.concatenate([tapers_ref[r]] + [piece for pieced in zip(*fringe) for piece in pieced], axis=0)
            part = jnp.dot(pieces, tapers, preferred_element_type=f32)
            weight = part[:MEMBERS] + part[MEMBERS : 2 * MEMBERS] + part[2 * MEMBERS :]
            for half in range(2):
                weight_ref[half, r * MEMBERS : (r + 1) * MEMBERS] = weight[:, half * LANES : (half + 1) * LANES]
        for half in range(2):
            weights = [weight_ref[half, pl.ds(8 * i * MEMBERS + p, 8, stride=MEMBERS)] for p in range(MEMBERS)]
            best = weights[0]
            for p in range(1, MEMBERS):
                best = jnp.maximum(best, weights[p])
            sums = [jnp.zeros((8, LANES), f32) for _ in range(4)]
            for p in range(MEMBERS):
                factor = jnp.exp(weights[p] - best)
                at = pl.ds(p * PITCH + 8 * i, 8)
                sums[0] = sums[0] + factor
                sums[1] = sums[1] + factor * depth_ref[half, at]
                sums[2] = sums[2] + factor * flow_ref[half, at]
                sums[3] = sums[3] + factor * stored_ref[half, at]
            inverse = 1.0 / sums[0]
            results = (best + jnp.log(sums[0]), sums[1] * inverse, sums[2] * inverse, sums[3] * inverse)
            for slot, result in enumerate(results):
                out_ref[pl.ds(64 * i + 2 * slot + half, 8, stride=8)] = result


def combine_kernel(groups, in_ref, out_ref):
    def quantity(slot, half):
        return in_ref[pl.ds(2 * slot + half, groups, stride=8)]

    rows = []
    totals = []
    for half in range(2):
        level = quantity(0, half)
        share = jnp.exp(level - jnp.max(level, axis=0, keepdims=True))
        totals.append((share, 1.0 / jnp.sum(share, axis=0, keepdims=True)))
    for slot in range(1, 4):
        for half in range(2):
            share, inverse = totals[half]
            rows.append(jnp.sum(share * quantity(slot, half), axis=0, keepdims=True) * inverse)
    rows.append(jnp.zeros((2, LANES), f32))
    result = jnp.concatenate(rows, axis=0)
    for copy in range(groups):
        out_ref[copy * 8 : (copy + 1) * 8] = result


def spread_kernel(in_ref, depth_ref, flow_ref, stored_ref):
    for slot, ref in enumerate((depth_ref, flow_ref, stored_ref)):
        for half in range(2):
            ref[:, half * LANES : (half + 1) * LANES] = in_ref[pl.ds(2 * slot + half, ROWS, stride=8)]


VMEM = pl.BlockSpec(memory_space=pltpu.VMEM)
HBM = pl.BlockSpec(memory_space=pltpu.HBM)


def call(kernel, name, in_specs, outs, scratch=(), aliases=None):
    return pl.pallas_call(
        kernel,
        name=name,
        in_specs=in_specs,
        out_specs=[VMEM] * len(outs),
        out_shape=[jax.ShapeDtypeStruct(shape, dtype) for shape, dtype in outs],
        scratch_shapes=list(scratch),
        input_output_aliases=aliases or {},
        compiler_params=pltpu.CompilerParams(vmem_limit_bytes=40 * 1024 * 1024),
    )


def local(
    surface, discharge, storage, exchange, depth_perturbation, flow_perturbation,
    sensor_cell, sensor_radius, observed, sensor_sigma,
):
    strips = lax.axis_size("strip")
    groups = lax.axis_size("dom")
    order = list(range(0, strips, 2)) + list(range(strips - 1, 0, -2))
    onward = [(order[i], order[(i + 1) % strips]) for i in range(strips)]
    backward = [(b, a) for a, b in onward]
    swapped = [(i, i ^ 1) for i in range(strips)]
    stay = lambda values: pltpu.with_memory_space_constraint(values, pltpu.HBM)
    as_row = lambda values: stay(values.reshape(1, SENS))
    fields = [stay(f) for f in (surface, discharge, storage, exchange, depth_perturbation, flow_perturbation)]
    grid = ((2, MEMBERS * PITCH + ROWS, LANES), f32)
    message = (MESSAGE, LANES)
    edges = lambda count: ((2 * count * MEMBERS, LANES), f32)
    row_of = lambda dtype: pltpu.VMEM((1, SENS), dtype)
    own, along, far, extra, depth, flow, stored = call(
        forecast_kernel, "forecast", [HBM] * 11,
        [((2,) + message, f32), (message, f32), edges(1), edges(3), grid, grid, grid],
        [pltpu.VMEM(field.shape, field.dtype) for field in fields[:-1]]
        + [
            pltpu.VMEM(fields[0].shape, bf16),
            pltpu.VMEM((8, 2, MEMBERS * 8, LANES), f32), pltpu.VMEM((8, 2, MEMBERS * 8, LANES), f32),
            pltpu.SMEM((SENS,), jnp.int32), row_of(jnp.int32), row_of(jnp.int32), row_of(f32), row_of(f32),
            pltpu.SemaphoreType.DMA((21,)),
        ],
    )(stay(sensor_cell), as_row(sensor_cell), as_row(sensor_radius), as_row(observed), as_row(sensor_sigma), *fields)
    strip_edges = pltpu.VMEM((2, MEMBERS * 8, LANES), f32)
    flow, late, across = call(
        flow_kernel, "flow", [HBM] + [VMEM] * 3, [grid, edges(4), ((2,) + message, f32)],
        [
            pltpu.VMEM(fields[0].shape, bf16), strip_edges, strip_edges, pltpu.SemaphoreType.DMA((MEMBERS // CHUNK,)),
        ],
        aliases={3: 0},
    )(fields[-1], own, depth, flow)
    arrived = lax.ppermute(along, "strip", backward)
    far = lax.ppermute(far, "strip", onward)
    (joined,) = call(join_kernel, "join", [VMEM] * 3, [((2,) + message, f32)], aliases={0: 0})(across, arrived, far)
    joined = lax.ppermute(joined, "strip", swapped)
    (tapers,) = call(
        taper_kernel, "taper", [VMEM], [((ROWS, 2 * SENS, COLS), bf16)], [pltpu.VMEM((SENS, COLS), f32)],
    )(own)
    parts, depth, flow, stored = call(
        finish_kernel, "finish", [VMEM] * 10, [((groups * 8, LANES), f32), grid, grid, grid],
        [
            pltpu.VMEM((2, SENS, COLS), f32),
 pltpu.VMEM((2, ROWS * MEMBERS, LANES), f32),
        ],
        aliases={7: 1, 8: 2, 9: 3},
    )(own, tapers, extra, late, arrived, far, joined, depth, flow, stored)
    winding = [8 * x + (7 - y if x % 2 else y) for x in range(groups // 8) for y in range(8)]
    start = winding.index(20)
    turned = winding[start:] + winding[:start]
    shared = lax.all_to_all(parts.reshape(groups, 8, LANES), "dom", 0, 0, tiled=True, axis_index_groups=[turned])
    (rows,) = call(
        lambda *refs: combine_kernel(groups, *refs), "combine", [VMEM], [((groups * 8, LANES), f32)],
    )(shared.reshape(groups * 8, LANES))
    whole = lax.all_to_all(
        rows.reshape(groups, 8, LANES), "dom", 0, 0, tiled=True, axis_index_groups=[turned]
    )
    return tuple(
        call(spread_kernel, "spread", [VMEM], [((ROWS, COLS), f32)] * 3)(whole.reshape(groups * 8, LANES))
    )


def solution(mesh):
    return jax.shard_map(
        local,
        mesh=mesh,
        in_specs=(
            P("dom", "strip", None),
            P("dom", "strip", None),
            P("dom", "strip", None),
            P("strip", None),
            P(None, "dom", "strip", None),
            P(None, "dom", "strip", None),
            P("strip"),
            P("strip"),
            P("strip"),
            P("strip"),
        ),
        out_specs=(P("strip", None), P("strip", None), P("strip", None)),
        check_vma=False,
    )
```
